32 devices in a mesh: dp: 4 (over x, core), fsdp: 8 (over z, y).
Axes of the slice: x: 2, y: 2, z: 4, core: 2. Of those that a mesh axis runs over, the one named last changes fastest.
Arguments:
- tokens: bfloat16 [65536, 768], P(('dp', 'fsdp')), may hold values from -12 to 12
- cotangent: bfloat16 [65536, 768], P(('dp', 'fsdp')), may hold values from -6 to 6
- seg_counts: int32 [512], P(('dp', 'fsdp')), may hold values from 1 to 128, as said below
- w_qkv: float32 [768, 2304], P(('dp', 'fsdp')), may hold values from -0.109375 to 0.109375
- w_out: float32 [768, 768], P(('dp', 'fsdp')), may hold values from -0.875 to 0.875
- w_up: float32 [768, 3072], P(('dp', 'fsdp')), may hold values from -0.21875 to 0.21875
- w_down: float32 [768, 3072], P(('dp', 'fsdp')), may hold values from -0.109375 to 0.109375
- small_params: float32 [9216], P(('dp', 'fsdp')), may hold values from -1 to 6
- first_qkv: float32 [768, 2304], P(('dp', 'fsdp')), may hold values from -0.00024414062 to 0.00024414062
- second_qkv: float32 [768, 2304], P(('dp', 'fsdp')), may hold values from 1.4128508e-10 to 5.651403e-10
- first_out: float32 [768, 768], P(('dp', 'fsdp')), may hold values from -0.00024414062 to 0.00024414062
- second_out: float32 [768, 768], P(('dp', 'fsdp')), may hold values from 1.4128508e-10 to 5.651403e-10
- first_up: float32 [768, 3072], P(('dp', 'fsdp')), may hold values from -0.00024414062 to 0.00024414062
- second_up: float32 [768, 3072], P(('dp', 'fsdp')), may hold values from 1.4128508e-10 to 5.651403e-10
- first_down: float32 [768, 3072], P(('dp', 'fsdp')), may hold values from -0.00024414062 to 0.00024414062
- second_down: float32 [768, 3072], P(('dp', 'fsdp')), may hold values from 1.4128508e-10 to 5.651403e-10
- first_small: float32 [9216], P(('dp', 'fsdp')), may hold values from -0.00048828125 to 0.00048828125
- second_small: float32 [9216], P(('dp', 'fsdp')), may hold values from 5.651403e-10 to 2.2605613e-09
Outputs:
- layer_out: bfloat16 [65536, 768], P(('dp', 'fsdp'))
- grad_tokens: bfloat16 [65536, 768], P(('dp', 'fsdp'))
- grad_norm: float32 [], replicated
- new_qkv: float32 [768, 2304], P(('dp', 'fsdp'))
- moment_qkv: float32 [768, 2304], P(('dp', 'fsdp'))
- square_qkv: float32 [768, 2304], P(('dp', 'fsdp'))
- copy_qkv: bfloat16 [768, 2304], P(('dp', 'fsdp'))
- new_out: float32 [768, 768], P(('dp', 'fsdp'))
- moment_out: float32 [768, 768], P(('dp', 'fsdp'))
- square_out: float32 [768, 768], P(('dp', 'fsdp'))
- copy_out: bfloat16 [768, 768], P(('dp', 'fsdp'))
- new_up: float32 [768, 3072], P(('dp', 'fsdp'))
- moment_up: float32 [768, 3072], P(('dp', 'fsdp'))
- square_up: float32 [768, 3072], P(('dp', 'fsdp'))
- copy_up: bfloat16 [768, 3072], P(('dp', 'fsdp'))
- new_down: float32 [768, 3072], P(('dp', 'fsdp'))
- moment_down: float32 [768, 3072], P(('dp', 'fsdp'))
- square_down: float32 [768, 3072], P(('dp', 'fsdp'))
- copy_down: bfloat16 [768, 3072], P(('dp', 'fsdp'))
- new_small: float32 [9216], P(('dp', 'fsdp'))
- moment_small: float32 [9216], P(('dp', 'fsdp'))
- square_small: float32 [9216], P(('dp', 'fsdp'))
- copy_small: bfloat16 [9216], P(('dp', 'fsdp'))
The draws below stay inside these ranges and needn't reach their ends.
Inputs may be any that keep to these rules, and one draw needn't show every extreme that they name: `seg_counts`: each device's 16 segments hold one document: every segment is full (128 tokens) except the device's last, which holds 1 to 128.
All inputs are finite; a program needn't handle non-finite values.
Results may differ from the reference program's by a relative error of at most 0.014.
The reference program's roundings to bfloat16 on the way count: a program that leaves them out, or rounds other values in their place, can miss the bound.
Values may be sent and summed in bfloat16 or wider, within the bound.
No kernel may reach another device: no remote copies, remote signals or barrier semaphores. Data moves between devices by JAX's collectives and lax.ppermute only.
A program may use at most 256 MiB of HBM per device.

```python
import math
import jax
import jax.numpy as jnp
from jax import lax

D = 768
HEADS = 12
HEAD_DIM = 64
FF = 3072
SEG_LEN = 128
STEP = 10
TOKENS = 65536
SEG_DEV = 16
SEGMENTS = 512
SMALL = 9216
OUTER_DEVS = 4
INNER_DEVS = 8


def rising_scale(top_factor):
    places = jnp.arange(D, dtype=jnp.int32)
    owner = places // max(D // (OUTER_DEVS * INNER_DEVS), 1)
    outer = (owner // INNER_DEVS).astype(jnp.float32) / max(OUTER_DEVS - 1, 1)
    inner = (owner % INNER_DEVS).astype(jnp.float32) / max(INNER_DEVS - 1, 1)
    return jnp.sqrt((1.0 + (top_factor - 1.0) * outer) * (1.0 + (top_factor - 1.0) * inner))


def draw_tokens(key, part):
    key = jax.random.fold_in(key, 11)
    base = jax.random.truncated_normal(key, -4.0, 4.0, (TOKENS, D), jnp.float32)
    scales = rising_scale(3.0)
    return (base * scales[None, :]).astype(jnp.bfloat16)


def draw_small_params(key, part):
    key = jax.random.fold_in(key, 12)
    key_bias, key_one, key_two = jax.random.split(key, 3)
    biases = 0.2 * jax.random.truncated_normal(key_bias, -4.0, 4.0, (SMALL,), jnp.float32)
    scales = rising_scale(3.0)
    gain_one = scales * jax.random.uniform(key_one, (D,), jnp.float32, 0.8, 1.2)
    gain_two = scales * jax.random.uniform(key_two, (D,), jnp.float32, 0.8, 1.2)
    front = 4 * D + FF
    return jnp.concatenate([biases[:front], gain_one, biases[front:front + D], gain_two, biases[front + D:front + 2 * D]]).astype(jnp.float32)


def draw_seg_counts(key, part):
    key = jax.random.fold_in(key, 13)
    partial_value = jax.random.randint(key, (SEGMENTS,), 1, SEG_LEN + 1, dtype=jnp.int32)
    position = jnp.arange(SEGMENTS, dtype=jnp.int32) % SEG_DEV
    return jnp.where(position == SEG_DEV - 1, partial_value, SEG_LEN).astype(jnp.int32)


def steps_of(stream_key, dims, pieces, low, top_value):
    factor_of = 1.0
    for axis_at, shards_of in pieces:
        draws = jax.random.uniform(jax.random.fold_in(jax.random.fold_in(stream_key, 6), axis_at), (shards_of,), jnp.float32, low / len(pieces), top_value / len(pieces))
        factor_of = factor_of * jnp.repeat(jnp.exp(draws), dims[axis_at] // shards_of).reshape((-1,) + (1,) * (len(dims) - 1 - axis_at))
    return factor_of


def normal_values(key, dims, deviation, most, cuts=(), kind=jnp.bfloat16):
    array = deviation * jax.random.normal(key, dims, jnp.float32)
    if cuts:
        array = array * steps_of(key, dims, cuts, -0.22, 0.18)
    return jnp.clip(array, -most, most).astype(kind)


def setup_inputs(seed: int = 0) -> dict:
    arg_keys = jax.random.split(jax.random.key(seed), 19)
    tokens = draw_tokens(jax.random.fold_in(arg_keys[18], 71), 0)
    cotangent = normal_values(arg_keys[1], (TOKENS, D), 1.0, 6.0, ((0, 32),))
    seg_counts = draw_seg_counts(jax.random.fold_in(arg_keys[18], 71), 0)
    w_qkv = normal_values(arg_keys[3], (D, 3 * D), (4 * D) ** -0.5, 0.109375, ((0, 32),), jnp.float32)
    w_out = normal_values(arg_keys[4], (D, D), (D // 16) ** -0.5, 0.875, ((0, 32),), jnp.float32)
    w_up = normal_values(arg_keys[5], (D, FF), D ** -0.5, 0.21875, ((0, 32),), jnp.float32)
    w_down = normal_values(arg_keys[6], (D, FF), FF ** -0.5, 0.109375, ((0, 32),), jnp.float32)
    small_params = draw_small_params(jax.random.fold_in(arg_keys[18], 71), 0)
    first_qkv = normal_values(arg_keys[8], (D, 3 * D), (0.11 / (4 * D * D + 2 * D * FF) ** 0.5), 0.00024414062, ((0, 32),), jnp.float32)
    second_qkv = jnp.clip(jnp.exp(math.log(5.65140323427471e-10) - 1.3862944 * jax.random.uniform(arg_keys[9], (D, 3 * D), jnp.float32) ** steps_of(arg_keys[9], (D, 3 * D), ((0, 32),), -0.2, 0.2)), 1.4128508085686775e-10, 5.65140323427471e-10)
    first_out = normal_values(arg_keys[10], (D, D), (0.11 / (4 * D * D + 2 * D * FF) ** 0.5), 0.00024414062, ((0, 32),), jnp.float32)
    second_out = jnp.clip(jnp.exp(math.log(5.65140323427471e-10) - 1.3862944 * jax.random.uniform(arg_keys[11], (D, D), jnp.float32) ** steps_of(arg_keys[11], (D, D), ((0, 32),), -0.2, 0.2)), 1.4128508085686775e-10, 5.65140323427471e-10)
    first_up = normal_values(arg_keys[12], (D, FF), (0.11 / (4 * D * D + 2 * D * FF) ** 0.5), 0.00024414062, ((0, 32),), jnp.float32)
    second_up = jnp.clip(jnp.exp(math.log(5.65140323427471e-10) - 1.3862944 * jax.random.uniform(arg_keys[13], (D, FF), jnp.float32) ** steps_of(arg_keys[13], (D, FF), ((0, 32),), -0.2, 0.2)), 1.4128508085686775e-10, 5.65140323427471e-10)
    first_down = normal_values(arg_keys[14], (D, FF), (0.11 / (4 * D * D + 2 * D * FF) ** 0.5), 0.00024414062, ((0, 32),), jnp.float32)
    second_down = jnp.clip(jnp.exp(math.log(5.65140323427471e-10) - 1.3862944 * jax.random.uniform(arg_keys[15], (D, FF), jnp.float32) ** steps_of(arg_keys[15], (D, FF), ((0, 32),), -0.2, 0.2)), 1.4128508085686775e-10, 5.65140323427471e-10)
    first_small = normal_values(arg_keys[16], (SMALL,), (0.22 / (4 * D * D + 2 * D * FF) ** 0.5), 0.00048828125, ((0, 32),), jnp.float32)
    second_small = jnp.clip(jnp.exp(math.log(2.260561293709884e-09) - 1.3862944 * jax.random.uniform(arg_keys[17], (SMALL,), jnp.float32) ** steps_of(arg_keys[17], (SMALL,), ((0, 32),), -0.2, 0.2)), 5.65140323427471e-10, 2.260561293709884e-09)
    return {"tokens": tokens, "cotangent": cotangent, "seg_counts": seg_counts, "w_qkv": w_qkv, "w_out": w_out, "w_up": w_up, "w_down": w_down, "small_params": small_params, "first_qkv": first_qkv, "second_qkv": second_qkv, "first_out": first_out, "second_out": second_out, "first_up": first_up, "second_up": second_up, "first_down": first_down, "second_down": second_down, "first_small": first_small, "second_small": second_small}


NEG_FILL = -1e+30
SCALE_QK = 0.125
LN_EPS = 1e-05
BETA_ONE = 0.9
BETA_TWO = 0.999
ADAM_EPS = 1e-08
RATE_MATRIX = 0.03
RATE_SMALL = 0.3
DECAY = 0.01
CLIP_LIMIT = 1.0
PRECISE = lax.Precision.HIGHEST

@jax.custom_vjp
def low(v):
    return lax.optimization_barrier(v.astype(jnp.bfloat16)).astype(jnp.float32)

@jax.custom_vjp
def low_back(v):
    return v

def low_keep(v):
    return (low(v), None)

def low_pass(kept, grad):
    return (grad,)

def back_keep(v):
    return (v, None)

def back_low(kept, grad):
    return (low(grad),)
low.defvjp(low_keep, low_pass)
low_back.defvjp(back_keep, back_low)

def split_small(vector):
    front = 3 * D + FF
    return (vector[0:D], vector[D:2 * D], vector[2 * D:3 * D], vector[3 * D:front], vector[front:front + D], vector[front + D:front + 2 * D], vector[front + 2 * D:front + 3 * D], vector[front + 3 * D:front + 4 * D], vector[front + 4 * D:front + 5 * D])

def normalize(values):
    row_mean = lax.optimization_barrier(jnp.mean(values, axis=-1, keepdims=True))
    centred = values - row_mean
    variance = lax.optimization_barrier(jnp.mean(centred * centred, axis=-1, keepdims=True))
    return centred * lax.rsqrt(variance + LN_EPS)

def block_layer(inputs, counts, w_qkv, w_out, w_up, w_down, small_vec):
    qkv_low = low(w_qkv)
    out_low = low(w_out)
    up_low = low(w_up)
    down_low = low(w_down)
    bias_q, bias_v, bias_o, bias_up, bias_down, gain_one, shift_one, gain_two, shift_two = split_small(low(small_vec))
    row_count = inputs.shape[0]
    seg_count = row_count // SEG_LEN
    places = jnp.arange(SEG_LEN, dtype=jnp.int32)
    visible = places[None, :] < counts[:, None]
    live_rows = visible.reshape(row_count, 1).astype(jnp.float32)
    joined = low_back(jnp.dot(inputs, qkv_low, precision=PRECISE))
    joined = low(joined + jnp.concatenate([bias_q, jnp.zeros((D,), jnp.float32), bias_v]))
    shaped = joined.reshape(seg_count, SEG_LEN, 3, HEADS, HEAD_DIM)
    query = shaped[:, :, 0]
    keyed = shaped[:, :, 1]
    valued = shaped[:, :, 2]
    raw = jnp.einsum('sqhd,skhd->shqk', query, keyed, precision=PRECISE)
    scores = jnp.where(visible[:, None, None, :], low_back(raw) * SCALE_QK, NEG_FILL)
    probs = jax.nn.softmax(scores, axis=-1)
    mixed = jnp.einsum('shqk,skhd->sqhd', low(probs), valued, precision=PRECISE).reshape(row_count, D)
    mixed = low(low_back(mixed))
    attended = low_back(jnp.dot(mixed, out_low.T, precision=PRECISE)) + bias_o
    first = inputs + attended
    hidden = normalize(first) * gain_one + shift_one
    pre_act = low_back(jnp.dot(low(hidden), up_low, precision=PRECISE)) + bias_up
    active = low(jax.nn.gelu(pre_act, approximate=False))
    branch = low_back(jnp.dot(active, down_low.T, precision=PRECISE)) + bias_down
    second = hidden + branch
    return (normalize(second) * gain_two + shift_two) * live_rows

def adam_update(weight, first_moment, second_moment, grad_clip, rate, decay):
    fresh_one = BETA_ONE * first_moment + (1.0 - BETA_ONE) * grad_clip
    fresh_two = BETA_TWO * second_moment + (1.0 - BETA_TWO) * grad_clip * grad_clip
    correct_one = 1.0 - BETA_ONE ** STEP
    correct_two = 1.0 - BETA_TWO ** STEP
    stepped = fresh_one / correct_one / (jnp.sqrt(fresh_two / correct_two) + ADAM_EPS)
    updated = weight - rate * (stepped + decay * weight)
    return (updated, fresh_one, fresh_two, updated.astype(jnp.bfloat16))

def reference(tokens, cotangent, seg_counts, w_qkv, w_out, w_up, w_down, small_params, first_qkv, second_qkv, first_out, second_out, first_up, second_up, first_down, second_down, first_small, second_small):
    block_rows = math.gcd(TOKENS, 4096)
    block_count = TOKENS // block_rows
    params = (w_qkv.astype(jnp.float32), w_out.astype(jnp.float32), w_up.astype(jnp.float32), w_down.astype(jnp.float32), small_params.astype(jnp.float32))
    inputs_all = tokens.astype(jnp.float32).reshape(block_count, block_rows, D)
    backs_all = cotangent.astype(jnp.float32).reshape(block_count, block_rows, D)
    counts_all = seg_counts.reshape(block_count, block_rows // SEG_LEN)

    def one_block(totals, items):
        inputs, back_in, counts = items

        def apply_layer(values, *weights):
            return block_layer(values, counts, *weights)
        result, pullback = jax.vjp(apply_layer, inputs, *params)
        grads = pullback(back_in)
        totals = tuple((summed + fresh for summed, fresh in zip(totals, grads[1:])))
        return (totals, (result.astype(jnp.bfloat16), grads[0].astype(jnp.bfloat16)))
    start = tuple((jnp.zeros_like(piece) for piece in params))
    totals, (outputs, grad_inputs) = lax.scan(one_block, start, (inputs_all, backs_all, counts_all))
    squares = jnp.float32(0.0)
    for piece in totals:
        squares = squares + jnp.sum(piece * piece)
    grad_norm = jnp.sqrt(squares)
    factor = CLIP_LIMIT / jnp.maximum(grad_norm, CLIP_LIMIT)
    firsts = (first_qkv, first_out, first_up, first_down, first_small)
    seconds = (second_qkv, second_out, second_up, second_down, second_small)
    results = []
    for place in range(5):
        rate = RATE_SMALL if place == 4 else RATE_MATRIX
        decay = 0.0 if place == 4 else DECAY
        results.extend(adam_update(params[place], firsts[place], seconds[place], totals[place] * factor, rate, decay))
    return (outputs.reshape(TOKENS, D), grad_inputs.reshape(TOKENS, D), grad_norm, results[0], results[1], results[2], results[3], results[4], results[5], results[6], results[7], results[8], results[9], results[10], results[11], results[12], results[13], results[14], results[15], results[16], results[17], results[18], results[19])
```

```python
import functools
import math

import jax
import jax.numpy as jnp
from jax import lax
from jax.experimental import pallas as pl
from jax.experimental.pallas import tpu as pltpu
from jax.sharding import Mesh
from jax.sharding import PartitionSpec as P

HEAD_DIM = 64
SEG_LEN = 128
STEP = 10
NEG_FILL = -1e30
SCALE_QK = 0.125
LN_EPS = 1e-05
BETA_ONE = 0.9
BETA_TWO = 0.999
ADAM_EPS = 1e-08
RATE_MATRIX = 0.03
RATE_SMALL = 0.3
DECAY = 0.01
CLIP_LIMIT = 1.0

LANES = 128
VMEM_LIMIT = 60 * 1024 * 1024
F32 = jnp.float32
BF16 = jnp.bfloat16
ALL = ("hi", "core", "fsdp")
PEERS = ("hi", "fsdp")


def dot_nn(left, right):
    return jnp.dot(left, right, preferred_element_type=F32)


def dot_nt(left, right):
    return lax.dot_general(left, right, (((1,), (1,)), ((), ())), preferred_element_type=F32)


def dot_tn(left, right):
    return lax.dot_general(left, right, (((0,), (0,)), ((), ())), preferred_element_type=F32)


def small_places(width, hidden):
    front = 3 * width + hidden
    return {
        "bq": (0, width),
        "bv": (width, 2 * width),
        "bo": (2 * width, 3 * width),
        "b1": (3 * width, front),
        "b2": (front, front + width),
        "g1": (front + width, front + 2 * width),
        "s1": (front + 2 * width, front + 3 * width),
        "g2": (front + 3 * width, front + 4 * width),
        "s2": (front + 4 * width, front + 5 * width),
    }


def normalize(values):
    row_mean = jnp.mean(values, axis=-1, keepdims=True)
    centred = values - row_mean
    variance = jnp.mean(centred * centred, axis=-1, keepdims=True)
    inverse = lax.rsqrt(variance + LN_EPS)
    return centred * inverse, inverse


def norm_back(scaled, normed, inverse):
    return inverse * (
        scaled
        - jnp.mean(scaled, axis=-1, keepdims=True)
        - normed * jnp.mean(scaled * normed, axis=-1, keepdims=True)
    )


def fold_rows(values):
    return jnp.sum(values.reshape(values.shape[0] // 8, 8, values.shape[1]), axis=0)


def head_halves(pair):
    lane = lax.broadcasted_iota(jnp.int32, pair.shape, 1)
    zero = jnp.zeros_like(pair)
    return jnp.concatenate(
        [jnp.where(lane < HEAD_DIM, pair, zero), jnp.where(lane < HEAD_DIM, zero, pair)], axis=0
    )


def stack_heads(wide):
    return jnp.concatenate([wide[:, :SEG_LEN], wide[:, SEG_LEN:]], axis=0)


def row_spec(rows, columns):
    return pl.BlockSpec((rows, columns), lambda step, *_: (step, 0))


def held_spec(rows, columns, place=0):
    return pl.BlockSpec(
        (rows, columns), lambda step, *_: (0, place), pipeline_mode=pl.Buffered(1)
    )


def params():
    return pltpu.CompilerParams(vmem_limit_bytes=VMEM_LIMIT)


def attention_forward_body(
    counts, inputs, w_qkv, w_out, small, joined_out, probs_out, mixed_out, normed_out, inverse_out
):
    rows, width = inputs.shape
    at = small_places(width, small.shape[1] - 8 * width)
    values = inputs[...]
    for part, bias in ((0, "bq"), (1, None), (2, "bv")):
        columns = slice(part * width, (part + 1) * width)
        product = dot_nn(values, w_qkv[:, columns])
        if bias is not None:
            product = product + small[:, slice(*at[bias])]
        joined_out[:, columns] = product.astype(BF16)
    for segment in range(rows // SEG_LEN):
        place = slice(segment * SEG_LEN, (segment + 1) * SEG_LEN)
        count = counts[pl.program_id(0) * (rows // SEG_LEN) + segment]
        visible = lax.broadcasted_iota(jnp.int32, (SEG_LEN, 2 * SEG_LEN), 0) < count
        for pair in range(width // LANES):
            low, high = pair * LANES, (pair + 1) * LANES
            query = joined_out[place, low:high] * jnp.asarray(SCALE_QK, BF16)
            keyed = joined_out[place, width + low : width + high]
            valued = joined_out[place, 2 * width + low : 2 * width + high]
            scores = jnp.where(visible, dot_nt(keyed, head_halves(query)), NEG_FILL)
            raised = jnp.exp(scores - jnp.max(scores, axis=0, keepdims=True))
            probs = raised * (1.0 / jnp.sum(raised, axis=0, keepdims=True))
            probs_out[place, 2 * low : 2 * high] = probs
            mixed = dot_tn(stack_heads(probs.astype(BF16)), head_halves(valued))
            mixed_out[place, low:high] = mixed.astype(BF16)
    attended = dot_nt(mixed_out[...], w_out[...]) + small[:, slice(*at["bo"])]
    normed, inverse = normalize(values.astype(F32) + attended)
    normed_out[...] = normed
    inverse_out[...] = jnp.broadcast_to(inverse, inverse_out.shape)


def attention_forward(inputs, counts, packed, small, block=256):
    rows, width = inputs.shape
    return pl.pallas_call(
        attention_forward_body,
        grid_spec=pltpu.PrefetchScalarGridSpec(
            num_scalar_prefetch=1,
            grid=(rows // block,),
            in_specs=[
                row_spec(block, width),
                held_spec(width, 3 * width),
                held_spec(width, width, 3),
                held_spec(1, small.shape[1]),
            ],
            out_specs=[
                row_spec(block, 3 * width),
                row_spec(block, 2 * width),
                row_spec(block, width),
                row_spec(block, width),
                row_spec(block, LANES),
            ],
        ),
        out_shape=[
            jax.ShapeDtypeStruct((rows, 3 * width), BF16),
            jax.ShapeDtypeStruct((rows, 2 * width), F32),
            jax.ShapeDtypeStruct((rows, width), BF16),
            jax.ShapeDtypeStruct((rows, width), F32),
            jax.ShapeDtypeStruct((rows, LANES), F32),
        ],
        compiler_params=params(),
        name="attention_forward",
    )(counts, inputs, packed, packed, small)


def mlp_forward_body(
    counts,
    normed_one,
    cotangent,
    w_up,
    w_down,
    small,
    result_out,
    active_out,
    slope_out,
    second_out,
    sums_out,
):
    rows, width = normed_one.shape
    step = pl.program_id(0)
    at = small_places(width, small.shape[1] - 8 * width)
    hidden = normed_one[...] * small[:, slice(*at["g1"])] + small[:, slice(*at["s1"])]
    pre_act = dot_nn(hidden.astype(BF16), w_up[...]) + small[:, slice(*at["b1"])]
    spread = 0.5 * (1.0 + lax.erf(pre_act * math.sqrt(0.5)))
    density = jnp.exp(-0.5 * pre_act * pre_act) * (1.0 / math.sqrt(2.0 * math.pi))
    active = (pre_act * spread).astype(BF16)
    active_out[...] = active
    slope_out[...] = spread + pre_act * density
    second = hidden + dot_nt(active, w_down[...]) + small[:, slice(*at["b2"])]
    normed, inverse = normalize(second)
    gain = small[:, slice(*at["g2"])]
    index = lax.broadcasted_iota(jnp.int32, (SEG_LEN, 1), 0)
    live = jnp.concatenate(
        [
            (index < counts[step * (rows // SEG_LEN) + segment]).astype(F32)
            for segment in range(rows // SEG_LEN)
        ],
        axis=0,
    )
    result_out[...] = ((normed * gain + small[:, slice(*at["s2"])]) * live).astype(BF16)
    incoming = cotangent[...].astype(F32) * live
    grad_second = norm_back(incoming * gain, normed, inverse)
    second_out[...] = grad_second

    @pl.when(step == 0)
    def _():
        sums_out[...] = jnp.zeros_like(sums_out)

    sums_out[0] += fold_rows(incoming * normed)
    sums_out[1] += fold_rows(incoming)
    sums_out[2] += fold_rows(grad_second)


def mlp_forward(normed_one, counts, cotangent, packed, small, block=256):
    rows, width = normed_one.shape
    hidden = packed.shape[1] // 2
    return pl.pallas_call(
        mlp_forward_body,
        grid_spec=pltpu.PrefetchScalarGridSpec(
            num_scalar_prefetch=1,
            grid=(rows // block,),
            in_specs=[
                row_spec(block, width),
                row_spec(block, width),
                held_spec(width, hidden),
                held_spec(width, hidden, 1),
                held_spec(1, small.shape[1]),
            ],
            out_specs=[
                row_spec(block, width),
                row_spec(block, hidden),
                row_spec(block, hidden),
                row_spec(block, width),
                pl.BlockSpec((3, 8, width), lambda step, *_: (0, 0, 0)),
            ],
        ),
        out_shape=[
            jax.ShapeDtypeStruct((rows, width), BF16),
            jax.ShapeDtypeStruct((rows, hidden), BF16),
            jax.ShapeDtypeStruct((rows, hidden), F32),
            jax.ShapeDtypeStruct((rows, width), F32),
            jax.ShapeDtypeStruct((3, 8, width), F32),
        ],
        compiler_params=params(),
        name="mlp_forward",
    )(counts, normed_one, cotangent, packed, packed, small)


def mlp_backward_body(
    grad_second, slope, normed_one, inverse_one, w_up, w_down, small, pre_out, first_out, sums_out, wide_out
):
    rows, width = normed_one.shape
    hidden = slope.shape[1]
    chunk = width
    at = small_places(width, hidden)

    @pl.when(pl.program_id(0) == 0)
    def _():
        sums_out[...] = jnp.zeros_like(sums_out)
        wide_out[...] = jnp.zeros_like(wide_out)

    incoming = grad_second[...]
    incoming_low = incoming.astype(BF16)
    grad_hidden = incoming
    for piece in range(hidden // chunk):
        columns = slice(piece * chunk, (piece + 1) * chunk)
        grad_pre = dot_nn(incoming_low, w_down[:, columns]) * slope[:, columns]
        wide_out[:, columns] += fold_rows(grad_pre)
        grad_low = grad_pre.astype(BF16)
        pre_out[:, columns] = grad_low
        grad_hidden = grad_hidden + dot_nt(grad_low, w_up[:, columns])
    normed = normed_one[...]
    sums_out[0] += fold_rows(grad_hidden * normed)
    sums_out[1] += fold_rows(grad_hidden)
    grad_first = norm_back(
        grad_hidden * small[:, slice(*at["g1"])], normed, inverse_one[:, :1]
    )
    first_out[...] = grad_first
    sums_out[2] += fold_rows(grad_first)


def mlp_backward(grad_second, slope, normed_one, inverse_one, packed, small, block=256):
    rows, width = normed_one.shape
    hidden = slope.shape[1]
    return pl.pallas_call(
        mlp_backward_body,
        grid=(rows // block,),
        in_specs=[
            row_spec(block, width),
            row_spec(block, hidden),
            row_spec(block, width),
            row_spec(block, LANES),
            held_spec(width, hidden),
            held_spec(width, hidden, 1),
            held_spec(1, small.shape[1]),
        ],
        out_specs=[
            row_spec(block, hidden),
            row_spec(block, width),
            pl.BlockSpec((3, 8, width), lambda step: (0, 0, 0)),
            pl.BlockSpec((8, hidden), lambda step: (0, 0)),
        ],
        out_shape=[
            jax.ShapeDtypeStruct((rows, hidden), BF16),
            jax.ShapeDtypeStruct((rows, width), F32),
            jax.ShapeDtypeStruct((3, 8, width), F32),
            jax.ShapeDtypeStruct((8, hidden), F32),
        ],
        compiler_params=params(),
        name="mlp_backward",
    )(grad_second, slope, normed_one, inverse_one, packed, packed, small)


def attention_backward_body(
    grad_first, joined, probs, w_out, joined_grad_out, sums_out, grad_mixed
):
    rows, width = grad_first.shape

    @pl.when(pl.program_id(0) == 0)
    def _():
        sums_out[...] = jnp.zeros_like(sums_out)

    grad_mixed[...] = dot_nn(grad_first[...].astype(BF16), w_out[...]).astype(BF16)
    for segment in range(rows // SEG_LEN):
        place = slice(segment * SEG_LEN, (segment + 1) * SEG_LEN)
        for pair in range(width // LANES):
            low, high = pair * LANES, (pair + 1) * LANES
            query = joined[place, low:high]
            keyed = joined[place, width + low : width + high]
            valued = joined[place, 2 * width + low : 2 * width + high]
            grad_halves = head_halves(grad_mixed[place, low:high])
            weights = probs[place, 2 * low : 2 * high]
            grad_probs = dot_nt(valued, grad_halves)
            grad_valued = dot_nn(weights.astype(BF16), grad_halves)
            inner = jnp.sum(weights * grad_probs, axis=0, keepdims=True)
            scores_low = (weights * (grad_probs - inner) * SCALE_QK).astype(BF16)
            grad_keyed = dot_nn(scores_low, head_halves(query))
            grad_query = dot_tn(stack_heads(scores_low), head_halves(keyed))
            joined_grad_out[place, low:high] = grad_query.astype(BF16)
            joined_grad_out[place, width + low : width + high] = grad_keyed.astype(BF16)
            joined_grad_out[place, 2 * width + low : 2 * width + high] = grad_valued.astype(BF16)
            sums_out[0, :, low:high] += fold_rows(grad_query)
            sums_out[1, :, low:high] += fold_rows(grad_valued)


def attention_backward(grad_first, joined, probs, packed, block=256):
    rows, width = grad_first.shape
    return pl.pallas_call(
        attention_backward_body,
        grid=(rows // block,),
        in_specs=[
            row_spec(block, width),
            row_spec(block, 3 * width),
            row_spec(block, 2 * width),
            held_spec(width, width, 3),
        ],
        out_specs=[
            row_spec(block, 3 * width),
            pl.BlockSpec((2, 8, width), lambda step: (0, 0, 0)),
        ],
        out_shape=[
            jax.ShapeDtypeStruct((rows, 3 * width), BF16),
            jax.ShapeDtypeStruct((2, 8, width), F32),
        ],
        scratch_shapes=[pltpu.VMEM((block, width), BF16)],
        compiler_params=params(),
        name="attention_backward",
    )(grad_first, joined, probs, packed)


def grad_tokens_body(joined_grad, grad_first, w_qkv, grad_out):
    grad_out[...] = (dot_nt(joined_grad[...], w_qkv[...]) + grad_first[...]).astype(BF16)


def grad_tokens(joined_grad, grad_first, packed, block=512):
    rows, width = grad_first.shape
    return pl.pallas_call(
        grad_tokens_body,
        grid=(rows // block,),
        in_specs=[
            row_spec(block, 3 * width),
            row_spec(block, width),
            held_spec(width, 3 * width),
        ],
        out_specs=row_spec(block, width),
        out_shape=jax.ShapeDtypeStruct((rows, width), BF16),
        compiler_params=params(),
        name="grad_tokens",
    )(joined_grad, grad_first, packed)


def weight_grad_body(core, left, right, keep_out, send_out, total):
    total[...] = dot_tn(left[...], right[...])
    groups, rows = keep_out.shape[0], keep_out.shape[1]
    for group in range(groups):
        mine = pl.multiple_of((2 * group + core[0]) * rows, rows)
        other = pl.multiple_of((2 * group + 1 - core[0]) * rows, rows)
        keep_out[group] = total[pl.ds(mine, rows), :]
        send_out[group] = total[pl.ds(other, rows), :].astype(BF16)


def weight_grad(core, left, right, groups, block=768):
    tokens, height = left.shape
    width = right.shape[1]
    rows = height // (2 * groups)
    out_spec = pl.BlockSpec((groups, rows, block), lambda step, *_: (0, 0, step))
    return pl.pallas_call(
        weight_grad_body,
        grid_spec=pltpu.PrefetchScalarGridSpec(
            num_scalar_prefetch=1,
            grid=(width // block,),
            in_specs=[
                pl.BlockSpec((tokens, height), lambda step, *_: (0, 0)),
                pl.BlockSpec((tokens, block), lambda step, *_: (0, step)),
            ],
            out_specs=[out_spec, out_spec],
            scratch_shapes=[pltpu.VMEM((height, block), F32)],
        ),
        out_shape=[
            jax.ShapeDtypeStruct((groups, rows, width), F32),
            jax.ShapeDtypeStruct((groups, rows, width), BF16),
        ],
        compiler_params=params(),
        name="weight_grad",
    )(core, left, right)


def scatter_sum(keep, send, swap, peers):
    groups, rows, width = keep.shape
    received = lax.ppermute(send, ALL, swap)
    both = (keep + received.astype(F32)).astype(BF16)
    pieces = lax.all_to_all(both.reshape(groups * rows, width), PEERS, 0, 0, tiled=True)
    return jnp.sum(pieces.reshape(peers, groups * rows // peers, width).astype(F32), axis=0)


def adam_update(weight, first_moment, second_moment, grad_clip, rate, decay):
    fresh_one = BETA_ONE * first_moment + (1.0 - BETA_ONE) * grad_clip
    fresh_two = BETA_TWO * second_moment + (1.0 - BETA_TWO) * grad_clip * grad_clip
    correct_one = 1.0 - BETA_ONE**STEP
    correct_two = 1.0 - BETA_TWO**STEP
    stepped = fresh_one / correct_one / (jnp.sqrt(fresh_two / correct_two) + ADAM_EPS)
    updated = weight - rate * (stepped + decay * weight)
    return (updated, fresh_one, fresh_two, updated.astype(BF16))


def body(
    high_count,
    inner_count,
    tokens,
    cotangent,
    seg_counts,
    w_qkv,
    w_out,
    w_up,
    w_down,
    small_params,
    first_qkv,
    second_qkv,
    first_out,
    second_out,
    first_up,
    second_up,
    first_down,
    second_down,
    first_small,
    second_small,
):
    device_count = 2 * high_count * inner_count
    peers = high_count * inner_count
    masters = (w_qkv, w_out, w_up, w_down, small_params)
    own_rows, width = w_out.shape
    hidden = w_up.shape[1]
    core = lax.axis_index("core").astype(jnp.int32).reshape(1)
    swap = [
        ((high * 2 + half) * inner_count + inner, (high * 2 + 1 - half) * inner_count + inner)
        for high in range(high_count)
        for half in range(2)
        for inner in range(inner_count)
    ]

    own_small = small_params.shape[0]
    small_wide = -(-own_small // LANES) * LANES
    small_block = jnp.pad(
        small_params.astype(BF16).reshape(1, own_small),
        ((0, own_rows - 1), (0, small_wide - own_small)),
    )
    front = jnp.concatenate([w_qkv.astype(BF16), w_out.astype(BF16), small_block], axis=1)
    back = jnp.concatenate([w_up.astype(BF16), w_down.astype(BF16)], axis=1)
    packed_front = lax.all_gather(front, ALL, axis=0, tiled=True)
    packed_back = lax.all_gather(back, ALL, axis=0, tiled=True)
    small = (
        packed_front.reshape(device_count, own_rows, front.shape[1])[
            :, 0, 4 * width : 4 * width + own_small
        ]
        .reshape(1, device_count * own_small)
        .astype(F32)
    )

    joined, probs, mixed, normed_one, inverse_one = attention_forward(
        tokens, seg_counts, packed_front, small
    )
    result, active, slope, grad_second, sums_two = mlp_forward(
        normed_one, seg_counts, cotangent, packed_back, small
    )
    second_low = grad_second.astype(BF16)
    sum_down = scatter_sum(*weight_grad(core, second_low, active, high_count), swap, peers)
    at = small_places(width, hidden)
    hidden_low = (normed_one * small[:, slice(*at["g1"])] + small[:, slice(*at["s1"])]).astype(BF16)
    grad_pre, grad_first, sums_one, sums_wide = mlp_backward(
        grad_second, slope, normed_one, inverse_one, packed_back, small
    )
    sum_up = scatter_sum(*weight_grad(core, hidden_low, grad_pre, high_count), swap, peers)
    first_low = grad_first.astype(BF16)
    sum_out = scatter_sum(*weight_grad(core, first_low, mixed, high_count), swap, peers)
    joined_grad, sums_qv = attention_backward(grad_first, joined, probs, packed_front)
    sum_qkv = scatter_sum(*weight_grad(core, tokens, joined_grad, high_count), swap, peers)
    grad_inputs = grad_tokens(joined_grad, grad_first, packed_front)

    grad_small = jnp.concatenate(
        [
            jnp.sum(sums_qv, axis=1).reshape(-1),
            jnp.sum(sums_one[2], axis=0),
            jnp.sum(sums_wide, axis=0),
            jnp.sum(sums_two[2], axis=0),
            jnp.sum(sums_one[:2], axis=1).reshape(-1),
            jnp.sum(sums_two[:2], axis=1).reshape(-1),
        ]
    )
    small_pieces = lax.all_to_all(
        grad_small.reshape(device_count, own_small), ALL, 0, 0, tiled=True
    )
    sum_small = jnp.sum(small_pieces, axis=0)

    summed = (sum_qkv, sum_out, sum_up, sum_down, sum_small)
    squares = jnp.float32(0.0)
    for piece in summed:
        squares = squares + jnp.sum(piece * piece)
    spread = jnp.broadcast_to(squares, (device_count, LANES))
    total = jnp.sum(lax.all_to_all(spread, ALL, 0, 0, tiled=True)[:, 0])
    grad_norm = jnp.sqrt(total)
    factor = CLIP_LIMIT / jnp.maximum(grad_norm, CLIP_LIMIT)
    firsts = (first_qkv, first_out, first_up, first_down, first_small)
    seconds = (second_qkv, second_out, second_up, second_down, second_small)
    results = []
    for place in range(5):
        rate = RATE_SMALL if place == 4 else RATE_MATRIX
        decay = 0.0 if place == 4 else DECAY
        results.extend(
            adam_update(
                masters[place], firsts[place], seconds[place], summed[place] * factor, rate, decay
            )
        )
    return (result, grad_inputs, grad_norm, *results)


def solution(mesh):
    outer, inner = mesh.devices.shape
    finer = Mesh(mesh.devices.reshape(outer // 2, 2, inner), ALL)
    rows, flat = P(ALL, None), P(ALL)
    return jax.shard_map(
        functools.partial(body, outer // 2, inner),
        mesh=finer,
        in_specs=(rows, rows, flat) + (rows,) * 4 + (flat,) + (rows,) * 8 + (flat,) * 2,
        out_specs=(rows, rows, P()) + (rows,) * 16 + (flat,) * 4,
        check_vma=False,
    )
```

```python
import functools
import math

import jax
import jax.numpy as jnp
from jax import lax
from jax.experimental import pallas as pl
from jax.experimental.pallas import tpu as pltpu
from jax.sharding import Mesh
from jax.sharding import PartitionSpec as P

HEAD_DIM = 64
SEG_LEN = 128
STEP = 10
NEG_FILL = -1e30
SCALE_QK = 0.125
LN_EPS = 1e-05
BETA_ONE = 0.9
BETA_TWO = 0.999
ADAM_EPS = 1e-08
RATE_MATRIX = 0.03
RATE_SMALL = 0.3
DECAY = 0.01
CLIP_LIMIT = 1.0

LANES = 128
VMEM_LIMIT = 60 * 1024 * 1024
SMALL_VMEM = 28 * 1024 * 1024
F32 = jnp.float32
BF16 = jnp.bfloat16
ALL = ("hi", "core", "zed", "low")
PEERS = ("hi", "zed", "low")
PLANE = ("hi", "low")


def dot_nn(left, right):
    return jnp.dot(left, right, preferred_element_type=F32)


def dot_nt(left, right):
    return lax.dot_general(left, right, (((1,), (1,)), ((), ())), preferred_element_type=F32)


def dot_tn(left, right):
    return lax.dot_general(left, right, (((0,), (0,)), ((), ())), preferred_element_type=F32)


def small_places(width, hidden):
    front = 3 * width + hidden
    return {
        "bq": (0, width),
        "bv": (width, 2 * width),
        "bo": (2 * width, 3 * width),
        "b1": (3 * width, front),
        "b2": (front, front + width),
        "g1": (front + width, front + 2 * width),
        "s1": (front + 2 * width, front + 3 * width),
        "g2": (front + 3 * width, front + 4 * width),
        "s2": (front + 4 * width, front + 5 * width),
    }


def normalize(values):
    row_mean = jnp.mean(values, axis=-1, keepdims=True)
    centred = values - row_mean
    variance = jnp.mean(centred * centred, axis=-1, keepdims=True)
    inverse = lax.rsqrt(variance + LN_EPS)
    return centred * inverse, inverse


def norm_back(scaled, normed, inverse):
    return inverse * (
        scaled
        - jnp.mean(scaled, axis=-1, keepdims=True)
        - normed * jnp.mean(scaled * normed, axis=-1, keepdims=True)
    )


def fold_rows(values):
    return jnp.sum(values.reshape(values.shape[0] // 8, 8, values.shape[1]), axis=0)


def head_halves(pair):
    lane = lax.broadcasted_iota(jnp.int32, pair.shape, 1)
    zero = jnp.zeros_like(pair)
    return jnp.concatenate(
        [jnp.where(lane < HEAD_DIM, pair, zero), jnp.where(lane < HEAD_DIM, zero, pair)], axis=0
    )


def stack_heads(wide):
    return jnp.concatenate([wide[:, :SEG_LEN], wide[:, SEG_LEN:]], axis=0)


def row_spec(rows, columns):
    return pl.BlockSpec((rows, columns), lambda step, *_: (step, 0))


def held_spec(rows, columns, place=0):
    return pl.BlockSpec(
        (rows, columns), lambda step, *_: (0, place), pipeline_mode=pl.Buffered(1)
    )


def whole_spec(shape):
    return pl.BlockSpec(shape, lambda *_: (0,) * len(shape))


def call_kernel(
    body, name, grid, inputs, in_specs, outs, out_specs, scalars=(), scratch=(), after=(), aliases=None, flops=0,
    vmem=VMEM_LIMIT,
):
    lead, kept = len(scalars), len(scalars) + len(inputs)

    def wrapped(*refs):
        body(*refs[:kept], *refs[kept + len(after) :])

    listed = outs if isinstance(outs, list) else [outs]
    moved = sum(math.prod(x.shape) * x.dtype.itemsize for x in (*inputs, *listed))
    return pl.pallas_call(
        wrapped,
        grid_spec=pltpu.PrefetchScalarGridSpec(
            num_scalar_prefetch=lead,
            grid=grid,
            in_specs=[*in_specs, *[pl.BlockSpec(memory_space=pl.ANY)] * len(after)],
            out_specs=out_specs,
            scratch_shapes=list(scratch),
        ),
        out_shape=outs,
        input_output_aliases=aliases or {},
        cost_estimate=pl.CostEstimate(
            flops=int(flops), bytes_accessed=moved, transcendentals=0
        ),
        compiler_params=pltpu.CompilerParams(vmem_limit_bytes=vmem),
        name=name,
    )(*scalars, *inputs, *after)


def shaped(shape, kind):
    return jax.ShapeDtypeStruct(shape, kind)


def attention_forward_body(
    core, counts, inputs, mine_a, theirs_a, mine_b, theirs_b, small, joined_out, probs_out, mixed_out, w_qkv, sems
):
    rows, width = inputs.shape
    at = small_places(width, small.shape[1] - 8 * width)

    @pl.when(pl.program_id(0) == 0)
    def _():
        copies = []
        groups, span, half = mine_a.shape
        for column, (mine, theirs) in enumerate(((mine_a, theirs_a), (mine_b, theirs_b))):
            for group in range(groups):
                for flip, source in enumerate((mine, theirs)):
                    owner = 2 * group + (core[0] if flip == 0 else 1 - core[0])
                    target = w_qkv.at[
                        pl.ds(pl.multiple_of(owner * span, span), span),
                        column * half : (column + 1) * half,
                    ]
                    copies.append(
                        pltpu.make_async_copy(
                            source.at[group, :, :half], target, sems.at[len(copies)]
                        )
                    )
        for copy in copies:
            copy.start()
        for copy in copies:
            copy.wait()

    values = inputs[...]
    for part, bias in ((0, "bq"), (1, None), (2, "bv")):
        columns = slice(part * width, (part + 1) * width)
        product = dot_nn(values, w_qkv[:, columns])
        if bias is not None:
            product = product + small[:, slice(*at[bias])]
        joined_out[:, columns] = product.astype(BF16)
    for segment in range(rows // SEG_LEN):
        place = slice(segment * SEG_LEN, (segment + 1) * SEG_LEN)
        count = counts[pl.program_id(0) * (rows // SEG_LEN) + segment]
        visible = lax.broadcasted_iota(jnp.int32, (SEG_LEN, 2 * SEG_LEN), 0) < count
        for pair in range(width // LANES):
            low, high = pair * LANES, (pair + 1) * LANES
            query = joined_out[place, low:high] * jnp.asarray(SCALE_QK, BF16)
            keyed = joined_out[place, width + low : width + high]
            valued = joined_out[place, 2 * width + low : 2 * width + high]
            scores = jnp.where(visible, dot_nt(keyed, head_halves(query)), NEG_FILL)
            raised = jnp.exp(scores - jnp.max(scores, axis=0, keepdims=True))
            probs = raised * (1.0 / jnp.sum(raised, axis=0, keepdims=True))
            probs_out[place, 2 * low : 2 * high] = probs
            mixed = dot_tn(stack_heads(probs.astype(BF16)), head_halves(valued))
            mixed_out[place, low:high] = mixed.astype(BF16)


def attention_forward(core, counts, inputs, quarters, small, block=256):
    rows, width = inputs.shape
    hbm = pl.BlockSpec(memory_space=pl.ANY)
    return call_kernel(
        attention_forward_body,
        "attention_forward",
        (rows // block,),
        [inputs, *quarters, small],
        [row_spec(block, width), hbm, hbm, hbm, hbm, held_spec(1, small.shape[1])],
        [
            shaped((rows, 3 * width), BF16),
            shaped((rows, 2 * width), F32),
            shaped((rows, width), BF16),
            shaped((width, 3 * width), BF16),
        ],
        [
            row_spec(block, 3 * width),
            row_spec(block, 2 * width),
            row_spec(block, width),
            pl.BlockSpec((width, 3 * width), lambda *_: (0, 0), pipeline_mode=pl.Buffered(1)),
        ],
        scalars=[core, counts],
        scratch=[pltpu.SemaphoreType.DMA((4 * quarters[0].shape[0],))],
        flops=12 * rows * width * width,
    )


def mlp_forward_body(
    counts,
    inputs,
    mixed,
    cotangent,
    w_up,
    w_down,
    w_out,
    small,
    result_out,
    normed_out,
    inverse_out,
    hidden_out,
    active_out,
    slope_out,
    second_out,
    second_low_out,
    sums_out,
):
    rows, width = inputs.shape
    step = pl.program_id(0)
    at = small_places(width, small.shape[1] - 8 * width)
    attended = dot_nt(mixed[...], w_out[...]) + small[:, slice(*at["bo"])]
    normed_one, inverse_one = normalize(inputs[...].astype(F32) + attended)
    normed_out[...] = normed_one
    inverse_out[...] = jnp.broadcast_to(inverse_one, inverse_out.shape)
    hidden = normed_one * small[:, slice(*at["g1"])] + small[:, slice(*at["s1"])]
    hidden_low = hidden.astype(BF16)
    hidden_out[...] = hidden_low
    pre_act = dot_nn(hidden_low, w_up[...]) + small[:, slice(*at["b1"])]
    spread = 0.5 * (1.0 + lax.erf(pre_act * math.sqrt(0.5)))
    density = jnp.exp(-0.5 * pre_act * pre_act) * (1.0 / math.sqrt(2.0 * math.pi))
    active = (pre_act * spread).astype(BF16)
    active_out[...] = active
    slope_out[...] = spread + pre_act * density
    second = hidden + dot_nt(active, w_down[...]) + small[:, slice(*at["b2"])]
    normed, inverse = normalize(second)
    gain = small[:, slice(*at["g2"])]
    index = lax.broadcasted_iota(jnp.int32, (SEG_LEN, 1), 0)
    live = jnp.concatenate(
        [
            (index < counts[step * (rows // SEG_LEN) + segment]).astype(F32)
            for segment in range(rows // SEG_LEN)
        ],
        axis=0,
    )
    result_out[...] = ((normed * gain + small[:, slice(*at["s2"])]) * live).astype(BF16)
    incoming = cotangent[...].astype(F32) * live
    grad_second = norm_back(incoming * gain, normed, inverse)
    second_out[...] = grad_second
    second_low_out[...] = grad_second.astype(BF16)

    @pl.when(step == 0)
    def _():
        sums_out[...] = jnp.zeros_like(sums_out)

    sums_out[0] += fold_rows(incoming * normed)
    sums_out[1] += fold_rows(incoming)
    sums_out[2] += fold_rows(grad_second)


def mlp_forward(counts, inputs, mixed, cotangent, packed, small, block=256):
    rows, width = inputs.shape
    hidden = (packed.shape[1] - width) // 2
    return call_kernel(
        mlp_forward_body,
        "mlp_forward",
        (rows // block,),
        [inputs, mixed, cotangent, packed, packed, packed, small],
        [
            row_spec(block, width),
            row_spec(block, width),
            row_spec(block, width),
            held_spec(width, hidden),
            held_spec(width, hidden, 1),
            held_spec(width, width, 2 * hidden // width),
            held_spec(1, small.shape[1]),
        ],
        [
            shaped((rows, width), BF16),
            shaped((rows, width), F32),
            shaped((rows, LANES), F32),
            shaped((rows, width), BF16),
            shaped((rows, hidden), BF16),
            shaped((rows, hidden), F32),
            shaped((rows, width), F32),
            shaped((rows, width), BF16),
            shaped((3, 8, width), F32),
        ],
        [
            row_spec(block, width),
            row_spec(block, width),
            row_spec(block, LANES),
            row_spec(block, width),
            row_spec(block, hidden),
            row_spec(block, hidden),
            row_spec(block, width),
            row_spec(block, width),
            whole_spec((3, 8, width)),
        ],
        scalars=[counts],
        flops=2 * rows * width * (width + 2 * hidden),
    )


def mlp_backward_body(fresh, *refs):
    grad_second, slope, normed_one, inverse_one, w_up, w_down, small = refs[:7]
    pre_out, first_out, first_low_out, sums_out, wide_out = refs[-5:]
    rows, width = normed_one.shape
    hidden = slope.shape[1]
    chunk = width
    at = small_places(width, hidden)

    @pl.when(pl.program_id(0) == 0)
    def _():
        if fresh:
            sums_out[...] = jnp.zeros_like(sums_out)
            wide_out[...] = jnp.zeros_like(wide_out)
        else:
            sums_out[...] = refs[7][...]
            wide_out[...] = refs[8][...]

    incoming = grad_second[...]
    incoming_low = incoming.astype(BF16)
    grad_hidden = incoming
    for piece in range(hidden // chunk):
        columns = slice(piece * chunk, (piece + 1) * chunk)
        grad_pre = dot_nn(incoming_low, w_down[:, columns]) * slope[:, columns]
        wide_out[:, columns] += fold_rows(grad_pre)
        grad_low = grad_pre.astype(BF16)
        pre_out[:, columns] = grad_low
        grad_hidden = grad_hidden + dot_nt(grad_low, w_up[:, columns])
    normed = normed_one[...]
    sums_out[0] += fold_rows(grad_hidden * normed)
    sums_out[1] += fold_rows(grad_hidden)
    grad_first = norm_back(
        grad_hidden * small[:, slice(*at["g1"])], normed, inverse_one[:, :1]
    )
    first_out[...] = grad_first
    first_low_out[...] = grad_first.astype(BF16)
    sums_out[2] += fold_rows(grad_first)


def mlp_backward(
    grad_second, slope, normed_one, inverse_one, packed, small, span, earlier=None, after=(), block=256
):
    rows, width = normed_one.shape
    hidden = slope.shape[1]

    def placed(columns):
        return pl.BlockSpec((block, columns), lambda step, *_: (span[0] + step, 0))

    hbm = pl.BlockSpec(memory_space=pl.ANY)
    sums_spec, wide_spec = whole_spec((3, 8, width)), whole_spec((8, hidden))
    inputs = [grad_second, slope, normed_one, inverse_one, packed, packed, small]
    in_specs = [
        placed(width),
        placed(hidden),
        placed(width),
        placed(LANES),
        held_spec(width, hidden),
        held_spec(width, hidden, 1),
        held_spec(1, small.shape[1]),
    ]
    aliases = None
    if earlier is not None:
        inputs += [earlier[3], earlier[4], *earlier[:3]]
        in_specs += [sums_spec, wide_spec, hbm, hbm, hbm]
        aliases = {9: 0, 10: 1, 11: 2}
    return call_kernel(
        functools.partial(mlp_backward_body, earlier is None),
        "mlp_backward",
        (span[1] - span[0],),
        inputs,
        in_specs,
        [
            shaped((rows, hidden), BF16),
            shaped((rows, width), F32),
            shaped((rows, width), BF16),
            shaped((3, 8, width), F32),
            shaped((8, hidden), F32),
        ],
        [placed(hidden), placed(width), placed(width), sums_spec, wide_spec],
        after=after,
        aliases=aliases,
        flops=4 * (span[1] - span[0]) * block * width * hidden,
    )


def attention_backward_body(fresh, *refs):
    first_low, joined, probs, w_out = refs[:4]
    joined_grad_out, sums_out, grad_mixed = refs[-3:]
    rows, width = first_low.shape

    @pl.when(pl.program_id(0) == 0)
    def _():
        sums_out[...] = jnp.zeros_like(sums_out) if fresh else refs[4][...]

    grad_mixed[...] = dot_nn(first_low[...], w_out[...]).astype(BF16)
    for segment in range(rows // SEG_LEN):
        place = slice(segment * SEG_LEN, (segment + 1) * SEG_LEN)
        for pair in range(width // LANES):
            low, high = pair * LANES, (pair + 1) * LANES
            query = joined[place, low:high]
            keyed = joined[place, width + low : width + high]
            valued = joined[place, 2 * width + low : 2 * width + high]
            grad_halves = head_halves(grad_mixed[place, low:high])
            weights = probs[place, 2 * low : 2 * high]
            grad_probs = dot_nt(valued, grad_halves)
            grad_valued = dot_nn(weights.astype(BF16), grad_halves)
            inner = jnp.sum(weights * grad_probs, axis=0, keepdims=True)
            scores_low = (weights * (grad_probs - inner) * SCALE_QK).astype(BF16)
            grad_keyed = dot_nn(scores_low, head_halves(query))
            grad_query = dot_tn(stack_heads(scores_low), head_halves(keyed))
            joined_grad_out[place, low:high] = grad_query.astype(BF16)
            joined_grad_out[place, width + low : width + high] = grad_keyed.astype(BF16)
            joined_grad_out[place, 2 * width + low : 2 * width + high] = grad_valued.astype(BF16)
            sums_out[0, :, low:high] += fold_rows(grad_query)
            sums_out[1, :, low:high] += fold_rows(grad_valued)


def attention_backward(first_low, joined, probs, packed, span, earlier=None, after=(), block=256):
    rows, width = first_low.shape

    def placed(columns):
        return pl.BlockSpec((block, columns), lambda step, *_: (span[0] + step, 0))

    inputs = [first_low, joined, probs, packed]
    in_specs = [
        placed(width),
        placed(3 * width),
        placed(2 * width),
        held_spec(width, width, (packed.shape[1] - width) // width),
    ]
    aliases = None
    if earlier is not None:
        inputs += [earlier[1], earlier[0]]
        in_specs += [whole_spec((2, 8, width)), pl.BlockSpec(memory_space=pl.ANY)]
        aliases = {5: 0}
    return call_kernel(
        functools.partial(attention_backward_body, earlier is None),
        "attention_backward",
        (span[1] - span[0],),
        inputs,
        in_specs,
        [shaped((rows, 3 * width), BF16), shaped((2, 8, width), F32)],
        [placed(3 * width), whole_spec((2, 8, width))],
        scratch=[pltpu.VMEM((block, width), BF16)],
        after=after,
        aliases=aliases,
        flops=16 * (span[1] - span[0]) * block * width * width,
    )


def grad_tokens_body(joined_grad, grad_first, w_qkv, grad_out):
    grad_out[...] = (dot_nt(joined_grad[...], w_qkv[...]) + grad_first[...]).astype(BF16)


def grad_tokens(joined_grad, grad_first, w_qkv, after=(), block=512):
    rows, width = grad_first.shape
    return call_kernel(
        grad_tokens_body,
        "grad_tokens",
        (rows // block,),
        [joined_grad, grad_first, w_qkv],
        [row_spec(block, 3 * width), row_spec(block, width), held_spec(width, 3 * width)],
        shaped((rows, width), BF16),
        row_spec(block, width),
        after=after,
        flops=6 * rows * width * width,
    )


def weight_grad_body(has_extra, core, left, right, *refs):
    keep_out, send_out, total = refs[-3:]
    block = right.shape[1]
    total[...] = dot_tn(left[...], right[...])
    groups, rows = keep_out.shape[0], keep_out.shape[1]
    step = pl.program_id(0)
    columns = pl.ds(pl.multiple_of(step * block, block), block) if has_extra else slice(None)
    for group in range(groups):
        for flip, target in enumerate((keep_out, send_out)):
            half = core[0] if flip == 0 else 1 - core[0]
            start = pl.multiple_of((2 * group + half) * rows, rows)
            target[group, :, columns] = total[pl.ds(start, rows), :].astype(BF16)
    if has_extra:
        extra = refs[0]

        @pl.when(step == 0)
        def _():
            for group in range(groups):
                for flip, target in enumerate((keep_out, send_out)):
                    half = core[0] if flip == 0 else 1 - core[0]
                    target[group, :, target.shape[2] - LANES :] = extra[group, half].astype(BF16)


def weight_grad(core, left, right, groups, extra=None, after=(), block=768):
    tokens, height = left.shape
    width = right.shape[1]
    rows = height // (2 * groups)
    inputs = [left, right]
    in_specs = [
        whole_spec((tokens, height)),
        pl.BlockSpec((tokens, block), lambda step, *_: (0, step)),
    ]
    if extra is None:
        shape = (groups, rows, width)
        out_spec = pl.BlockSpec((groups, rows, block), lambda step, *_: (0, 0, step))
    else:
        inputs.append(extra)
        in_specs.append(whole_spec(extra.shape))
        shape = (groups, rows, width + LANES)
        out_spec = whole_spec(shape)
    return call_kernel(
        functools.partial(weight_grad_body, extra is not None),
        "weight_grad",
        (width // block,),
        inputs,
        in_specs,
        [shaped(shape, BF16)] * 2,
        [out_spec, out_spec],
        scalars=[core],
        scratch=[pltpu.VMEM((height, block), F32)],
        after=after,
        flops=2 * tokens * height * width,
    )


def add_body(*refs):
    both_out, column = refs[-1], 0
    for keep, received in zip(refs[:-1:2], refs[1:-1:2]):
        width = keep.shape[-1]
        both_out[..., column : column + width] = (
            keep[...].astype(F32) + received[...].astype(F32)
        ).astype(BF16)
        column += width


def add_pairs(pairs, after=()):
    groups, rows = pairs[0][0].shape[:2]
    arrays = [array for pair in pairs for array in pair]
    shape = (groups, rows, sum(pair[0].shape[-1] for pair in pairs))
    return call_kernel(
        add_body,
        "add_pairs",
        (1,),
        arrays,
        [whole_spec(array.shape) for array in arrays],
        shaped(shape, BF16),
        whole_spec(shape),
        after=after,
        vmem=SMALL_VMEM,
    )


def fold_body(pieces, total_out):
    total_out[...] = jnp.sum(pieces[...].astype(F32), axis=0)


def fold_pieces(pieces, after=()):
    count, rows, width = pieces.shape
    return call_kernel(
        fold_body,
        "fold_pieces",
        (1,),
        [pieces],
        [whole_spec(pieces.shape)],
        shaped((rows, width), F32),
        whole_spec((rows, width)),
        after=after,
        vmem=SMALL_VMEM,
    )


def squares_body(pieces, *refs):
    total_out, spread_out = refs[-2:]
    total = jnp.sum(pieces[...].astype(F32), axis=0)
    total_out[...] = total
    squares = jnp.sum(total * total)
    for other in refs[:-2]:
        squares = squares + jnp.sum(other[...] * other[...])
    spread_out[...] = jnp.zeros(spread_out.shape, F32) + squares


def fold_with_squares(pieces, others, copies, after=()):
    count, rows, width = pieces.shape
    inputs = [pieces, *others]
    outs = [shaped((rows, width), F32), shaped((copies, LANES), F32)]
    return call_kernel(
        squares_body,
        "fold_with_squares",
        (1,),
        inputs,
        [whole_spec(array.shape) for array in inputs],
        outs,
        [whole_spec(array.shape) for array in outs],
        after=after,
        vmem=SMALL_VMEM,
    )


def update_body(places, squares, *refs):
    count = len(places)
    norm_out, results = refs[-1], refs[-1 - 4 * count : -1]
    states = refs[-1 - 7 * count : -1 - 4 * count]
    totals = refs[: -1 - 7 * count]
    grad_norm = jnp.sqrt(jnp.sum(squares[:, :1], axis=0, keepdims=True))
    factor = CLIP_LIMIT / jnp.maximum(grad_norm, CLIP_LIMIT)
    norm_out[...] = jnp.broadcast_to(grad_norm, norm_out.shape)
    for index, (source, low, high) in enumerate(places):
        weight, first, second = (ref[...] for ref in states[3 * index : 3 * index + 3])
        fresh = adam_update(
            weight, first, second, totals[source][:, low:high] * factor, RATE_MATRIX, DECAY
        )
        for target, value in zip(results[4 * index : 4 * index + 4], fresh):
            target[...] = value


def update_weights(squares, totals, places, states):
    inputs = [squares, *totals, *states]
    outs = []
    for index in range(len(places)):
        shape = states[3 * index].shape
        outs += [shaped(shape, F32)] * 3 + [shaped(shape, BF16)]
    outs.append(shaped((1, LANES), F32))
    return call_kernel(
        functools.partial(update_body, places),
        "update_weights",
        (1,),
        inputs,
        [whole_spec(array.shape) for array in inputs],
        outs,
        [whole_spec(array.shape) for array in outs],
        vmem=SMALL_VMEM,
    )


def gather_axis(value, axis, size):
    pieces = [value] + [
        lax.ppermute(value, axis, [(place, place ^ step) for place in range(size)])
        for step in range(1, size)
    ]
    stacked = jnp.stack(pieces)
    place, bit = lax.axis_index(axis), 1
    while bit < size:
        paired = stacked.reshape(size // (2 * bit), 2, bit, *value.shape)
        stacked = jnp.where((place & bit) != 0, paired[:, ::-1], paired).reshape(stacked.shape)
        bit *= 2
    return stacked


def adam_update(weight, first_moment, second_moment, grad_clip, rate, decay):
    fresh_one = BETA_ONE * first_moment + (1.0 - BETA_ONE) * grad_clip
    fresh_two = BETA_TWO * second_moment + (1.0 - BETA_TWO) * grad_clip * grad_clip
    correct_one = 1.0 - BETA_ONE**STEP
    correct_two = 1.0 - BETA_TWO**STEP
    stepped = fresh_one / correct_one / (jnp.sqrt(fresh_two / correct_two) + ADAM_EPS)
    updated = weight - rate * (stepped + decay * weight)
    return (updated, fresh_one, fresh_two, updated.astype(BF16))


def body(
    high_count,
    zed_count,
    low_count,
    tokens,
    cotangent,
    seg_counts,
    w_qkv,
    w_out,
    w_up,
    w_down,
    small_params,
    first_qkv,
    second_qkv,
    first_out,
    second_out,
    first_up,
    second_up,
    first_down,
    second_down,
    first_small,
    second_small,
):
    inner_count = zed_count * low_count
    device_count = 2 * high_count * inner_count
    own_rows, width = w_out.shape
    hidden = w_up.shape[1]
    own_small = small_params.shape[0]
    core = lax.axis_index("core").astype(jnp.int32).reshape(1)
    swap = [(0, 1), (1, 0)]

    back = jnp.concatenate([w_up.astype(BF16), w_down.astype(BF16), w_out.astype(BF16)], axis=1)
    packed = lax.all_gather(back, ALL, axis=0, tiled=True)
    low_qkv = w_qkv.astype(BF16)
    per_row = own_small // own_rows
    small_block = jnp.pad(
        small_params.astype(BF16).reshape(own_rows, per_row), ((0, 0), (0, LANES - per_row))
    )
    along = gather_axis(jnp.concatenate([low_qkv, small_block], axis=1), "zed", zed_count)
    split = low_qkv.shape[1] // 2
    quarters = []
    for piece, order in ((along[..., :split], (0, 1)), (along[..., split:], (1, 0))):
        for stage in order:
            if stage == 0:
                piece = jnp.moveaxis(gather_axis(piece, "low", low_count), 0, -3)
            else:
                piece = gather_axis(piece, "hi", high_count)
        quarters.append(piece.reshape(high_count, inner_count * own_rows, piece.shape[-1]))
    quarters = [
        half
        for quarter in quarters
        for half in (quarter, lax.ppermute(quarter, "core", swap))
    ]
    mine, theirs = (half[..., split : split + per_row] for half in quarters[2:])
    small = (
        jnp.where(core[0] == 0, jnp.stack([mine, theirs], 1), jnp.stack([theirs, mine], 1))
        .reshape(1, device_count * own_small)
        .astype(F32)
    )

    joined, probs, mixed, whole_qkv = attention_forward(core, seg_counts, tokens, quarters, small)
    (
        result,
        normed_one,
        inverse_one,
        hidden_low,
        active,
        slope,
        grad_second,
        second_low,
        sums_two,
    ) = mlp_forward(seg_counts, tokens, mixed, cotangent, packed, small)


    def swap_cores(parts):
        keep, send = parts
        return keep, lax.ppermute(send, "core", swap)

    def peer_sum(both):
        columns = both.shape[-1]
        pieces = lax.all_to_all(both.reshape(-1, columns), PEERS, 0, 0, tiled=True)
        return pieces.reshape(high_count * inner_count, own_rows, columns)

    blocks = tokens.shape[0] // 256
    early_blocks, half_blocks = max(blocks // 4, 1), max(blocks // 2, 1)
    saved = (grad_second, slope, normed_one, inverse_one, packed, small)
    down = weight_grad(core, second_low, active, high_count)
    early = mlp_backward(*saved, (0, early_blocks), after=[down[0]])
    down = add_pairs([swap_cores(down)], after=[early[3]])
    grad_pre, grad_first, first_low, sums_one, sums_wide = mlp_backward(
        *saved, (early_blocks, blocks), earlier=early, after=[down]
    )
    down = peer_sum(down)
    up = weight_grad(core, hidden_low, grad_pre, high_count)
    out = weight_grad(core, first_low, mixed, high_count, after=[up[0]])
    upout = add_pairs([swap_cores(up), swap_cores(out)])
    saved = (first_low, joined, probs, packed)
    early = attention_backward(*saved, (0, half_blocks), after=[upout])
    sum_down = fold_pieces(down, after=[early[1]])
    upout = peer_sum(upout)
    joined_grad, sums_qv = attention_backward(
        *saved, (half_blocks, blocks), earlier=early, after=[sum_down]
    )
    grad_small = jnp.concatenate(
        [
            jnp.sum(sums_qv, axis=1).reshape(-1),
            jnp.sum(sums_one[2], axis=0),
            jnp.sum(sums_wide, axis=0),
            jnp.sum(sums_two[2], axis=0),
            jnp.sum(sums_one[:2], axis=1).reshape(-1),
            jnp.sum(sums_two[:2], axis=1).reshape(-1),
        ]
    )
    by_owner = jnp.pad(
        grad_small.reshape(high_count, 2, inner_count * own_rows, per_row),
        ((0, 0),) * 3 + ((0, LANES - per_row),),
    )
    qkv = weight_grad(core, tokens, joined_grad, high_count, extra=by_owner)
    qkv = add_pairs([swap_cores(qkv)])
    grad_inputs = grad_tokens(joined_grad, grad_first, whole_qkv, after=[qkv])
    sum_upout = fold_pieces(upout, after=[grad_inputs])
    sum_front, spread = fold_with_squares(peer_sum(qkv), [sum_upout, sum_down], device_count)
    squares = lax.all_to_all(spread, ALL, 0, 0, tiled=True)
    *updated, norm_row = update_weights(
        squares,
        [sum_front, sum_upout, sum_down],
        ((0, 0, 3 * width), (1, hidden, hidden + width), (1, 0, hidden), (2, 0, hidden)),
        [
            *(w_qkv, first_qkv, second_qkv),
            *(w_out, first_out, second_out),
            *(w_up, first_up, second_up),
            *(w_down, first_down, second_down),
        ],
    )
    grad_norm = norm_row[0, 0]
    factor = CLIP_LIMIT / jnp.maximum(grad_norm, CLIP_LIMIT)
    sum_small = sum_front[:, 3 * width : 3 * width + per_row].reshape(own_small)
    updated += adam_update(
        small_params, first_small, second_small, sum_small * factor, RATE_SMALL, 0.0
    )
    return (result, grad_inputs, grad_norm, *updated)


def solution(mesh):
    outer, inner = mesh.devices.shape
    finer = Mesh(mesh.devices.reshape(outer // 2, 2, inner // 2, 2), ALL)
    rows, flat = P(ALL, None), P(ALL)
    return jax.shard_map(
        functools.partial(body, outer // 2, inner // 2, 2),
        mesh=finer,
        in_specs=(rows, rows, flat) + (rows,) * 4 + (flat,) + (rows,) * 8 + (flat,) * 2,
        out_specs=(rows, rows, P()) + (rows,) * 16 + (flat,) * 4,
        check_vma=False,
    )
```

```python
import functools
import math

import jax
import jax.numpy as jnp
from jax import lax
from jax.experimental import pallas as pl
from jax.experimental.pallas import tpu as pltpu
from jax.sharding import Mesh
from jax.sharding import PartitionSpec as P

HEAD_DIM = 64
SEG_LEN = 128
STEP = 10
NEG_FILL = -1e30
SCALE_QK = 0.125
LN_EPS = 1e-05
BETA_ONE = 0.9
BETA_TWO = 0.999
ADAM_EPS = 1e-08
RATE_MATRIX = 0.03
RATE_SMALL = 0.3
DECAY = 0.01
CLIP_LIMIT = 1.0

LANES = 128
VMEM_LIMIT = 60 * 1024 * 1024
SMALL_VMEM = 60 * 1024 * 1024
F32 = jnp.float32
BF16 = jnp.bfloat16
ALL = ("hi", "core", "zed", "low")
PEERS = ("hi", "zed", "low")
PLANE = ("hi", "low")


def dot_nn(left, right):
    return jnp.dot(left, right, preferred_element_type=F32)


def dot_nt(left, right):
    return lax.dot_general(left, right, (((1,), (1,)), ((), ())), preferred_element_type=F32)


def dot_tn(left, right):
    return lax.dot_general(left, right, (((0,), (0,)), ((), ())), preferred_element_type=F32)


def small_places(width, hidden):
    front = 3 * width + hidden
    return {
        "bq": (0, width),
        "bv": (width, 2 * width),
        "bo": (2 * width, 3 * width),
        "b1": (3 * width, front),
        "b2": (front, front + width),
        "g1": (front + width, front + 2 * width),
        "s1": (front + 2 * width, front + 3 * width),
        "g2": (front + 3 * width, front + 4 * width),
        "s2": (front + 4 * width, front + 5 * width),
    }


def normalize(values):
    row_mean = jnp.mean(values, axis=-1, keepdims=True)
    centred = values - row_mean
    variance = jnp.mean(centred * centred, axis=-1, keepdims=True)
    inverse = lax.rsqrt(variance + LN_EPS)
    return centred * inverse, inverse


def norm_back(scaled, normed, inverse):
    return inverse * (
        scaled
        - jnp.mean(scaled, axis=-1, keepdims=True)
        - normed * jnp.mean(scaled * normed, axis=-1, keepdims=True)
    )


def fold_rows(values):
    return jnp.sum(values.reshape(values.shape[0] // 8, 8, values.shape[1]), axis=0)


def head_halves(pair):
    lane = lax.broadcasted_iota(jnp.int32, pair.shape, 1)
    zero = jnp.zeros_like(pair)
    return jnp.concatenate(
        [jnp.where(lane < HEAD_DIM, pair, zero), jnp.where(lane < HEAD_DIM, zero, pair)], axis=0
    )


def stack_heads(wide):
    return jnp.concatenate([wide[:, :SEG_LEN], wide[:, SEG_LEN:]], axis=0)


def row_spec(rows, columns):
    return pl.BlockSpec((rows, columns), lambda step, *_: (step, 0))


def held_spec(rows, columns, place=0):
    return pl.BlockSpec(
        (rows, columns), lambda step, *_: (0, place), pipeline_mode=pl.Buffered(1)
    )


def whole_spec(shape):
    return pl.BlockSpec(shape, lambda *_: (0,) * len(shape))


def call_kernel(
    body, name, grid, inputs, in_specs, outs, out_specs, scalars=(), scratch=(), after=(), aliases=None, flops=0,
    vmem=VMEM_LIMIT,
):
    lead, kept = len(scalars), len(scalars) + len(inputs)

    def wrapped(*refs):
        body(*refs[:kept], *refs[kept + len(after) :])

    listed = outs if isinstance(outs, list) else [outs]
    moved = sum(math.prod(x.shape) * x.dtype.itemsize for x in (*inputs, *listed))
    return pl.pallas_call(
        wrapped,
        grid_spec=pltpu.PrefetchScalarGridSpec(
            num_scalar_prefetch=lead,
            grid=grid,
            in_specs=[*in_specs, *[pl.BlockSpec(memory_space=pl.ANY)] * len(after)],
            out_specs=out_specs,
            scratch_shapes=list(scratch),
        ),
        out_shape=outs,
        input_output_aliases=aliases or {},
        cost_estimate=pl.CostEstimate(
            flops=int(flops), bytes_accessed=moved, transcendentals=0
        ),
        compiler_params=pltpu.CompilerParams(vmem_limit_bytes=vmem),
        name=name,
    )(*scalars, *inputs, *after)


def shaped(shape, kind):
    return jax.ShapeDtypeStruct(shape, kind)


def attention_forward_body(
    core, counts, inputs, mine_a, theirs_a, mine_b, theirs_b, small, joined_out, probs_out, mixed_out, normed_out, inverse_out, hidden_out, w_qkv, w_out, sems
):
    rows, width = inputs.shape
    at = small_places(width, small.shape[1] - 8 * width)

    @pl.when(pl.program_id(0) == 0)
    def _():
        copies = []
        groups, span, cut = mine_a.shape
        rest = 3 * width - cut
        moves = (
            (mine_a, theirs_a, w_qkv, 0, 0, cut),
            (mine_b, theirs_b, w_qkv, 0, cut, rest),
            (mine_b, theirs_b, w_out, rest + LANES, 0, width),
        )
        for mine, theirs, target, source, place, wide in moves:
            for group in range(groups):
                for flip, half in enumerate((mine, theirs)):
                    owner = 2 * group + (core[0] if flip == 0 else 1 - core[0])
                    block = target.at[
                        pl.ds(pl.multiple_of(owner * span, span), span), place : place + wide
                    ]
                    copies.append(
                        pltpu.make_async_copy(
                            half.at[group, :, source : source + wide], block, sems.at[len(copies)]
                        )
                    )
        for copy in copies:
            copy.start()
        for copy in copies:
            copy.wait()

    values = inputs[...]
    for part, bias in ((0, "bq"), (1, None), (2, "bv")):
        columns = slice(part * width, (part + 1) * width)
        product = dot_nn(values, w_qkv[:, columns])
        if bias is not None:
            product = product + small[:, slice(*at[bias])]
        joined_out[:, columns] = product.astype(BF16)
    for segment in range(rows // SEG_LEN):
        place = slice(segment * SEG_LEN, (segment + 1) * SEG_LEN)
        count = counts[pl.program_id(0) * (rows // SEG_LEN) + segment]
        visible = lax.broadcasted_iota(jnp.int32, (SEG_LEN, 2 * SEG_LEN), 0) < count
        for pair in range(width // LANES):
            low, high = pair * LANES, (pair + 1) * LANES
            query = joined_out[place, low:high] * jnp.asarray(SCALE_QK, BF16)
            keyed = joined_out[place, width + low : width + high]
            valued = joined_out[place, 2 * width + low : 2 * width + high]
            scores = jnp.where(visible, dot_nt(keyed, head_halves(query)), NEG_FILL)
            raised = jnp.exp(scores - jnp.max(scores, axis=0, keepdims=True))
            probs = raised * (1.0 / jnp.sum(raised, axis=0, keepdims=True))
            probs_out[place, 2 * low : 2 * high] = probs
            mixed = dot_tn(stack_heads(probs.astype(BF16)), head_halves(valued))
            mixed_out[place, low:high] = mixed.astype(BF16)
    attended = dot_nt(mixed_out[...], w_out[...]) + small[:, slice(*at["bo"])]
    normed, inverse = normalize(values.astype(F32) + attended)
    normed_out[...] = normed
    inverse_out[...] = jnp.broadcast_to(inverse, inverse_out.shape)
    hidden = normed * small[:, slice(*at["g1"])] + small[:, slice(*at["s1"])]
    hidden_out[...] = hidden.astype(BF16)


def attention_forward(core, counts, inputs, quarters, small, block=256):
    rows, width = inputs.shape
    hbm = pl.BlockSpec(memory_space=pl.ANY)
    return call_kernel(
        attention_forward_body,
        "attention_forward",
        (rows // block,),
        [inputs, *quarters, small],
        [row_spec(block, width), hbm, hbm, hbm, hbm, held_spec(1, small.shape[1])],
        [
            shaped((rows, 3 * width), BF16),
            shaped((rows, 2 * width), F32),
            shaped((rows, width), BF16),
            shaped((rows, width), F32),
            shaped((rows, LANES), F32),
            shaped((rows, width), BF16),
            shaped((width, 3 * width), BF16),
            shaped((width, width), BF16),
        ],
        [
            row_spec(block, 3 * width),
            row_spec(block, 2 * width),
            row_spec(block, width),
            row_spec(block, width),
            row_spec(block, LANES),
            row_spec(block, width),
            held_spec(width, 3 * width),
            held_spec(width, width),
        ],
        scalars=[core, counts],
        scratch=[pltpu.SemaphoreType.DMA((6 * quarters[0].shape[0],))],
        flops=12 * rows * width * width,
    )


def mlp_forward_body(
    counts,
    normed_one,
    cotangent,
    w_up,
    w_down,
    small,
    result_out,
    active_out,
    slope_out,
    second_out,
    second_low_out,
    sums_out,
):
    rows, width = normed_one.shape
    step = pl.program_id(0)
    at = small_places(width, small.shape[1] - 8 * width)
    hidden = normed_one[...] * small[:, slice(*at["g1"])] + small[:, slice(*at["s1"])]
    hidden_low = hidden.astype(BF16)
    pre_act = dot_nn(hidden_low, w_up[...]) + small[:, slice(*at["b1"])]
    spread = 0.5 * (1.0 + lax.erf(pre_act * math.sqrt(0.5)))
    density = jnp.exp(-0.5 * pre_act * pre_act) * (1.0 / math.sqrt(2.0 * math.pi))
    active = (pre_act * spread).astype(BF16)
    active_out[...] = active
    slope_out[...] = spread + pre_act * density
    second = hidden + dot_nt(active, w_down[...]) + small[:, slice(*at["b2"])]
    normed, inverse = normalize(second)
    gain = small[:, slice(*at["g2"])]
    index = lax.broadcasted_iota(jnp.int32, (SEG_LEN, 1), 0)
    live = jnp.concatenate(
        [
            (index < counts[step * (rows // SEG_LEN) + segment]).astype(F32)
            for segment in range(rows // SEG_LEN)
        ],
        axis=0,
    )
    result_out[...] = ((normed * gain + small[:, slice(*at["s2"])]) * live).astype(BF16)
    incoming = cotangent[...].astype(F32) * live
    grad_second = norm_back(incoming * gain, normed, inverse)
    second_out[...] = grad_second
    second_low_out[...] = grad_second.astype(BF16)

    @pl.when(step == 0)
    def _():
        sums_out[...] = jnp.zeros_like(sums_out)

    sums_out[0] += fold_rows(incoming * normed)
    sums_out[1] += fold_rows(incoming)
    sums_out[2] += fold_rows(grad_second)


def mlp_forward(counts, normed_one, cotangent, packed, small, block=256):
    rows, width = normed_one.shape
    hidden = packed.shape[1] // 2
    return call_kernel(
        mlp_forward_body,
        "mlp_forward",
        (rows // block,),
        [normed_one, cotangent, packed, packed, small],
        [
            row_spec(block, width),
            row_spec(block, width),
            held_spec(width, hidden),
            held_spec(width, hidden, 1),
            held_spec(1, small.shape[1]),
        ],
        [
            shaped((rows, width), BF16),
            shaped((rows, hidden), BF16),
            shaped((rows, hidden), F32),
            shaped((rows, width), F32),
            shaped((rows, width), BF16),
            shaped((3, 8, width), F32),
        ],
        [
            row_spec(block, width),
            row_spec(block, hidden),
            row_spec(block, hidden),
            row_spec(block, width),
            row_spec(block, width),
            whole_spec((3, 8, width)),
        ],
        scalars=[counts],
        flops=4 * rows * width * hidden,
    )


def mlp_backward_body(fresh, *refs):
    grad_second, slope, normed_one, inverse_one, w_up, w_down, small = refs[:7]
    pre_out, first_out, first_low_out, sums_out, wide_out = refs[-5:]
    rows, width = normed_one.shape
    hidden = slope.shape[1]
    chunk = width
    at = small_places(width, hidden)

    @pl.when(pl.program_id(0) == 0)
    def _():
        if fresh:
            sums_out[...] = jnp.zeros_like(sums_out)
            wide_out[...] = jnp.zeros_like(wide_out)
        else:
            sums_out[...] = refs[7][...]
            wide_out[...] = refs[8][...]

    incoming = grad_second[...]
    incoming_low = incoming.astype(BF16)
    grad_hidden = incoming
    for piece in range(hidden // chunk):
        columns = slice(piece * chunk, (piece + 1) * chunk)
        grad_pre = dot_nn(incoming_low, w_down[:, columns]) * slope[:, columns]
        wide_out[:, columns] += fold_rows(grad_pre)
        grad_low = grad_pre.astype(BF16)
        pre_out[:, columns] = grad_low
        grad_hidden = grad_hidden + dot_nt(grad_low, w_up[:, columns])
    normed = normed_one[...]
    sums_out[0] += fold_rows(grad_hidden * normed)
    sums_out[1] += fold_rows(grad_hidden)
    grad_first = norm_back(
        grad_hidden * small[:, slice(*at["g1"])], normed, inverse_one[:, :1]
    )
    first_out[...] = grad_first
    first_low_out[...] = grad_first.astype(BF16)
    sums_out[2] += fold_rows(grad_first)


def mlp_backward(
    grad_second, slope, normed_one, inverse_one, packed, small, span, earlier=None, after=(), block=256
):
    rows, width = normed_one.shape
    hidden = slope.shape[1]

    def placed(columns):
        return pl.BlockSpec((block, columns), lambda step, *_: (span[0] + step, 0))

    hbm = pl.BlockSpec(memory_space=pl.ANY)
    sums_spec, wide_spec = whole_spec((3, 8, width)), whole_spec((8, hidden))
    inputs = [grad_second, slope, normed_one, inverse_one, packed, packed, small]
    in_specs = [
        placed(width),
        placed(hidden),
        placed(width),
        placed(LANES),
        held_spec(width, hidden),
        held_spec(width, hidden, 1),
        held_spec(1, small.shape[1]),
    ]
    aliases = None
    if earlier is not None:
        inputs += [earlier[3], earlier[4], *earlier[:3]]
        in_specs += [sums_spec, wide_spec, hbm, hbm, hbm]
        aliases = {9: 0, 10: 1, 11: 2}
    return call_kernel(
        functools.partial(mlp_backward_body, earlier is None),
        "mlp_backward",
        (span[1] - span[0],),
        inputs,
        in_specs,
        [
            shaped((rows, hidden), BF16),
            shaped((rows, width), F32),
            shaped((rows, width), BF16),
            shaped((3, 8, width), F32),
            shaped((8, hidden), F32),
        ],
        [placed(hidden), placed(width), placed(width), sums_spec, wide_spec],
        after=after,
        aliases=aliases,
        flops=4 * (span[1] - span[0]) * block * width * hidden,
    )


def attention_backward_body(fresh, *refs):
    first_low, joined, probs, w_out = refs[:4]
    joined_grad_out, sums_out, grad_mixed = refs[-3:]
    rows, width = first_low.shape

    @pl.when(pl.program_id(0) == 0)
    def _():
        sums_out[...] = jnp.zeros_like(sums_out) if fresh else refs[4][...]

    grad_mixed[...] = dot_nn(first_low[...], w_out[...]).astype(BF16)
    for segment in range(rows // SEG_LEN):
        place = slice(segment * SEG_LEN, (segment + 1) * SEG_LEN)
        for pair in range(width // LANES):
            low, high = pair * LANES, (pair + 1) * LANES
            query = joined[place, low:high]
            keyed = joined[place, width + low : width + high]
            valued = joined[place, 2 * width + low : 2 * width + high]
            grad_halves = head_halves(grad_mixed[place, low:high])
            weights = probs[place, 2 * low : 2 * high]
            grad_probs = dot_nt(valued, grad_halves)
            grad_valued = dot_nn(weights.astype(BF16), grad_halves)
            inner = jnp.sum(weights * grad_probs, axis=0, keepdims=True)
            scores_low = (weights * (grad_probs - inner) * SCALE_QK).astype(BF16)
            grad_keyed = dot_nn(scores_low, head_halves(query))
            grad_query = dot_tn(stack_heads(scores_low), head_halves(keyed))
            joined_grad_out[place, low:high] = grad_query.astype(BF16)
            joined_grad_out[place, width + low : width + high] = grad_keyed.astype(BF16)
            joined_grad_out[place, 2 * width + low : 2 * width + high] = grad_valued.astype(BF16)
            sums_out[0, :, low:high] += fold_rows(grad_query)
            sums_out[1, :, low:high] += fold_rows(grad_valued)


def attention_backward(first_low, joined, probs, w_out, span, earlier=None, after=(), block=256):
    rows, width = first_low.shape

    def placed(columns):
        return pl.BlockSpec((block, columns), lambda step, *_: (span[0] + step, 0))

    inputs = [first_low, joined, probs, w_out]
    in_specs = [
        placed(width),
        placed(3 * width),
        placed(2 * width),
        held_spec(width, width),
    ]
    aliases = None
    if earlier is not None:
        inputs += [earlier[1], earlier[0]]
        in_specs += [whole_spec((2, 8, width)), pl.BlockSpec(memory_space=pl.ANY)]
        aliases = {5: 0}
    return call_kernel(
        functools.partial(attention_backward_body, earlier is None),
        "attention_backward",
        (span[1] - span[0],),
        inputs,
        in_specs,
        [shaped((rows, 3 * width), BF16), shaped((2, 8, width), F32)],
        [placed(3 * width), whole_spec((2, 8, width))],
        scratch=[pltpu.VMEM((block, width), BF16)],
        after=after,
        aliases=aliases,
        flops=16 * (span[1] - span[0]) * block * width * width,
    )


def grad_tokens_body(joined_grad, grad_first, w_qkv, grad_out):
    grad_out[...] = (dot_nt(joined_grad[...], w_qkv[...]) + grad_first[...]).astype(BF16)


def grad_tokens(joined_grad, grad_first, w_qkv, after=(), block=512):
    rows, width = grad_first.shape
    return call_kernel(
        grad_tokens_body,
        "grad_tokens",
        (rows // block,),
        [joined_grad, grad_first, w_qkv],
        [row_spec(block, 3 * width), row_spec(block, width), held_spec(width, 3 * width)],
        shaped((rows, width), BF16),
        row_spec(block, width),
        after=after,
        flops=6 * rows * width * width,
    )


def pack_body(*refs):
    packed_out, column = refs[-1], 0
    for ref in refs[:-1]:
        packed_out[:, column : column + ref.shape[1]] = ref[...].astype(BF16)
        column += ref.shape[1]


def pack_rows(arrays):
    shape = (arrays[0].shape[0], sum(array.shape[1] for array in arrays))
    return call_kernel(
        pack_body,
        "pack_rows",
        (1,),
        arrays,
        [whole_spec(array.shape) for array in arrays],
        shaped(shape, BF16),
        whole_spec(shape),
    )


def weight_grad_body(has_extra, core, left, right, *refs):
    keep_out, send_out, total = refs[-3:]
    block = right.shape[1]
    total[...] = dot_tn(left[...], right[...])
    groups, rows = keep_out.shape[0], keep_out.shape[1]
    step = pl.program_id(0)
    columns = pl.ds(pl.multiple_of(step * block, block), block) if has_extra else slice(None)
    for group in range(groups):
        for flip, target in enumerate((keep_out, send_out)):
            half = core[0] if flip == 0 else 1 - core[0]
            start = pl.multiple_of((2 * group + half) * rows, rows)
            target[group, :, columns] = total[pl.ds(start, rows), :].astype(BF16)
    if has_extra:
        extra = refs[0]

        @pl.when(step == 0)
        def _():
            for group in range(groups):
                for flip, target in enumerate((keep_out, send_out)):
                    half = core[0] if flip == 0 else 1 - core[0]
                    target[group, :, target.shape[2] - LANES :] = extra[group, half].astype(BF16)


def weight_grad(core, left, right, groups, extra=None, after=(), block=768):
    tokens, height = left.shape
    width = right.shape[1]
    rows = height // (2 * groups)
    inputs = [left, right]
    in_specs = [
        whole_spec((tokens, height)),
        pl.BlockSpec((tokens, block), lambda step, *_: (0, step)),
    ]
    if extra is None:
        shape = (groups, rows, width)
        out_spec = pl.BlockSpec((groups, rows, block), lambda step, *_: (0, 0, step))
    else:
        inputs.append(extra)
        in_specs.append(whole_spec(extra.shape))
        shape = (groups, rows, width + LANES)
        out_spec = whole_spec(shape)
    return call_kernel(
        functools.partial(weight_grad_body, extra is not None),
        "weight_grad",
        (width // block,),
        inputs,
        in_specs,
        [shaped(shape, BF16)] * 2,
        [out_spec, out_spec],
        scalars=[core],
        scratch=[pltpu.VMEM((height, block), F32)],
        after=after,
        flops=2 * tokens * height * width,
    )


def add_body(*refs):
    both_out, column = refs[-1], 0
    for keep, received in zip(refs[:-1:2], refs[1:-1:2]):
        width = keep.shape[-1]
        both_out[..., column : column + width] = (
            keep[...].astype(F32) + received[...].astype(F32)
        ).astype(BF16)
        column += width


def add_pairs(pairs, after=()):
    groups, rows = pairs[0][0].shape[:2]
    arrays = [array for pair in pairs for array in pair]
    shape = (groups, rows, sum(pair[0].shape[-1] for pair in pairs))
    return call_kernel(
        add_body,
        "add_pairs",
        (1,),
        arrays,
        [whole_spec(array.shape) for array in arrays],
        shaped(shape, BF16),
        whole_spec(shape),
        after=after,
        vmem=SMALL_VMEM,
    )


def fold_body(pieces, total_out):
    total_out[...] = jnp.sum(pieces[...].astype(F32), axis=0)


def fold_pieces(pieces, after=()):
    count, rows, width = pieces.shape
    return call_kernel(
        fold_body,
        "fold_pieces",
        (1,),
        [pieces],
        [whole_spec(pieces.shape)],
        shaped((rows, width), F32),
        whole_spec((rows, width)),
        after=after,
        vmem=SMALL_VMEM,
    )


def squares_body(pieces, *refs):
    total_out, spread_out = refs[-2:]
    total = jnp.sum(pieces[...].astype(F32), axis=0)
    total_out[...] = total
    squares = jnp.sum(total * total)
    for other in refs[:-2]:
        squares = squares + jnp.sum(other[...] * other[...])
    spread_out[...] = jnp.zeros(spread_out.shape, F32) + squares


def fold_with_squares(pieces, others, copies, after=()):
    count, rows, width = pieces.shape
    inputs = [pieces, *others]
    outs = [shaped((rows, width), F32), shaped((copies, LANES), F32)]
    return call_kernel(
        squares_body,
        "fold_with_squares",
        (1,),
        inputs,
        [whole_spec(array.shape) for array in inputs],
        outs,
        [whole_spec(array.shape) for array in outs],
        after=after,
        vmem=SMALL_VMEM,
    )


def update_body(places, squares, *refs):
    count = len(places)
    norm_out, results = refs[-1], refs[-1 - 4 * count : -1]
    states = refs[-1 - 7 * count : -1 - 4 * count]
    totals = refs[: -1 - 7 * count]
    grad_norm = jnp.sqrt(jnp.sum(squares[:, :1], axis=0, keepdims=True))
    factor = CLIP_LIMIT / jnp.maximum(grad_norm, CLIP_LIMIT)
    norm_out[...] = jnp.broadcast_to(grad_norm, norm_out.shape)
    for index, (source, low, high) in enumerate(places):
        weight, first, second = (ref[...] for ref in states[3 * index : 3 * index + 3])
        fresh = adam_update(
            weight, first, second, totals[source][:, low:high] * factor, RATE_MATRIX, DECAY
        )
        for target, value in zip(results[4 * index : 4 * index + 4], fresh):
            target[...] = value


def update_weights(squares, totals, places, states):
    inputs = [squares, *totals, *states]
    outs = []
    for index in range(len(places)):
        shape = states[3 * index].shape
        outs += [shaped(shape, F32)] * 3 + [shaped(shape, BF16)]
    outs.append(shaped((1, LANES), F32))
    return call_kernel(
        functools.partial(update_body, places),
        "update_weights",
        (1,),
        inputs,
        [whole_spec(array.shape) for array in inputs],
        outs,
        [whole_spec(array.shape) for array in outs],
        vmem=SMALL_VMEM,
    )


def gather_axis(value, axis, size):
    pieces = [value] + [
        lax.ppermute(value, axis, [(place, place ^ step) for place in range(size)])
        for step in range(1, size)
    ]
    stacked = jnp.stack(pieces)
    place, bit = lax.axis_index(axis), 1
    while bit < size:
        paired = stacked.reshape(size // (2 * bit), 2, bit, *value.shape)
        stacked = jnp.where((place & bit) != 0, paired[:, ::-1], paired).reshape(stacked.shape)
        bit *= 2
    return stacked


def adam_update(weight, first_moment, second_moment, grad_clip, rate, decay):
    fresh_one = BETA_ONE * first_moment + (1.0 - BETA_ONE) * grad_clip
    fresh_two = BETA_TWO * second_moment + (1.0 - BETA_TWO) * grad_clip * grad_clip
    correct_one = 1.0 - BETA_ONE**STEP
    correct_two = 1.0 - BETA_TWO**STEP
    stepped = fresh_one / correct_one / (jnp.sqrt(fresh_two / correct_two) + ADAM_EPS)
    updated = weight - rate * (stepped + decay * weight)
    return (updated, fresh_one, fresh_two, updated.astype(BF16))


def body(
    high_count,
    zed_count,
    low_count,
    tokens,
    cotangent,
    seg_counts,
    w_qkv,
    w_out,
    w_up,
    w_down,
    small_params,
    first_qkv,
    second_qkv,
    first_out,
    second_out,
    first_up,
    second_up,
    first_down,
    second_down,
    first_small,
    second_small,
):
    inner_count = zed_count * low_count
    device_count = 2 * high_count * inner_count
    own_rows, width = w_out.shape
    hidden = w_up.shape[1]
    own_small = small_params.shape[0]
    core = lax.axis_index("core").astype(jnp.int32).reshape(1)
    swap = [(0, 1), (1, 0)]

    back = pack_rows([w_up, w_down])
    packed = lax.all_gather(back, ALL, axis=0, tiled=True)
    low_qkv = w_qkv.astype(BF16)
    per_row = own_small // own_rows
    small_block = jnp.pad(
        small_params.astype(BF16).reshape(own_rows, per_row), ((0, 0), (0, LANES - per_row))
    )
    front = jnp.concatenate([low_qkv, small_block, w_out.astype(BF16)], axis=1)
    along = gather_axis(front, "zed", zed_count)
    split = 2 * width
    at_small = low_qkv.shape[1] - split
    quarters = []
    for piece, order in ((along[..., :split], (0, 1)), (along[..., split:], (1, 0))):
        for stage in order:
            if stage == 0:
                piece = jnp.moveaxis(gather_axis(piece, "low", low_count), 0, -3)
            else:
                piece = gather_axis(piece, "hi", high_count)
        quarters.append(piece.reshape(high_count, inner_count * own_rows, piece.shape[-1]))
    quarters = [
        half
        for quarter in quarters
        for half in (quarter, lax.ppermute(quarter, "core", swap))
    ]
    mine, theirs = (half[..., at_small : at_small + per_row] for half in quarters[2:])
    small = (
        jnp.where(core[0] == 0, jnp.stack([mine, theirs], 1), jnp.stack([theirs, mine], 1))
        .reshape(1, device_count * own_small)
        .astype(F32)
    )

    (
        joined,
        probs,
        mixed,
        normed_one,
        inverse_one,
        hidden_low,
        whole_qkv,
        whole_out,
    ) = attention_forward(core, seg_counts, tokens, quarters, small)
    result, active, slope, grad_second, second_low, sums_two = mlp_forward(
        seg_counts, normed_one, cotangent, packed, small
    )

    def swap_cores(parts):
        keep, send = parts
        return keep, lax.ppermute(send, "core", swap)

    def peer_sum(both):
        columns = both.shape[-1]
        pieces = lax.all_to_all(both.reshape(-1, columns), PEERS, 0, 0, tiled=True)
        return pieces.reshape(high_count * inner_count, own_rows, columns)

    blocks = tokens.shape[0] // 256
    saved = (grad_second, slope, normed_one, inverse_one, packed, small)
    down = weight_grad(core, second_low, active, high_count, block=512)
    down = add_pairs([swap_cores(down)])
    grad_pre, grad_first, first_low, sums_one, sums_wide = mlp_backward(
        *saved, (0, blocks), after=[down]
    )
    down = peer_sum(down)
    up = weight_grad(core, hidden_low, grad_pre, high_count, block=512)
    out = weight_grad(core, first_low, mixed, high_count, after=[up[0]], block=256)
    up = add_pairs([swap_cores(up)], after=[out[0]])
    sum_down = fold_pieces(down, after=[up])
    out = swap_cores(out)
    joined_grad, sums_qv = attention_backward(
        first_low, joined, probs, whole_out, (0, blocks), after=[sum_down]
    )
    up = peer_sum(up)

    grad_small = jnp.concatenate(
        [
            jnp.sum(sums_qv, axis=1).reshape(-1),
            jnp.sum(sums_one[2], axis=0),
            jnp.sum(sums_wide, axis=0),
            jnp.sum(sums_two[2], axis=0),
            jnp.sum(sums_one[:2], axis=1).reshape(-1),
            jnp.sum(sums_two[:2], axis=1).reshape(-1),
        ]
    )
    by_owner = jnp.pad(
        grad_small.reshape(high_count, 2, inner_count * own_rows, per_row),
        ((0, 0),) * 3 + ((0, LANES - per_row),),
    )
    qkv = weight_grad(core, tokens, joined_grad, high_count, extra=by_owner)
    front = jnp.concatenate(
        [
            (keep.astype(F32) + received.astype(F32)).astype(BF16)
            for keep, received in (swap_cores(qkv), out)
        ],
        axis=-1,
    )
    grad_inputs = grad_tokens(joined_grad, grad_first, whole_qkv, after=[front])
    sum_up = fold_pieces(up, after=[grad_inputs])
    sum_front, spread = fold_with_squares(peer_sum(front), [sum_up, sum_down], device_count)
    squares = lax.all_to_all(spread, ALL, 0, 0, tiled=True)
    *updated, norm_row = update_weights(
        squares,
        [sum_front, sum_up, sum_down],
        (
            (0, 0, 3 * width),
            (0, 3 * width + LANES, 4 * width + LANES),
            (1, 0, hidden),
            (2, 0, hidden),
        ),
        [
            *(w_qkv, first_qkv, second_qkv),
            *(w_out, first_out, second_out),
            *(w_up, first_up, second_up),
            *(w_down, first_down, second_down),
        ],
    )
    grad_norm = norm_row[0, 0]
    factor = CLIP_LIMIT / jnp.maximum(grad_norm, CLIP_LIMIT)
    sum_small = sum_front[:, 3 * width : 3 * width + per_row].reshape(own_small)
    updated += adam_update(
        small_params, first_small, second_small, sum_small * factor, RATE_SMALL, 0.0
    )
    return (result, grad_inputs, grad_norm, *updated)


def solution(mesh):
    outer, inner = mesh.devices.shape
    finer = Mesh(mesh.devices.reshape(outer // 2, 2, inner // 2, 2), ALL)
    rows, flat = P(ALL, None), P(ALL)
    return jax.shard_map(
        functools.partial(body, outer // 2, inner // 2, 2),
        mesh=finer,
        in_specs=(rows, rows, flat) + (rows,) * 4 + (flat,) + (rows,) * 8 + (flat,) * 2,
        out_specs=(rows, rows, P()) + (rows,) * 16 + (flat,) * 4,
        check_vma=False,
    )
```

```python
import functools
import math

import jax
import jax.numpy as jnp
from jax import lax
from jax.experimental import pallas as pl
from jax.experimental.pallas import tpu as pltpu
from jax.sharding import Mesh
from jax.sharding import PartitionSpec as P

HEAD_DIM = 64
SEG_LEN = 128
STEP = 10
NEG_FILL = -1e30
SCALE_QK = 0.125
LN_EPS = 1e-05
BETA_ONE = 0.9
BETA_TWO = 0.999
ADAM_EPS = 1e-08
RATE_MATRIX = 0.03
RATE_SMALL = 0.3
DECAY = 0.01
CLIP_LIMIT = 1.0

LANES = 128
VMEM_LIMIT = 60 * 1024 * 1024
SMALL_VMEM = 60 * 1024 * 1024
F32 = jnp.float32
BF16 = jnp.bfloat16
ALL = ("hi", "core", "zed", "low")
PEERS = ("hi", "zed", "low")
PLANE = ("hi", "low")


def dot_nn(left, right):
    return jnp.dot(left, right, preferred_element_type=F32)


def dot_nt(left, right):
    return lax.dot_general(left, right, (((1,), (1,)), ((), ())), preferred_element_type=F32)


def dot_tn(left, right):
    return lax.dot_general(left, right, (((0,), (0,)), ((), ())), preferred_element_type=F32)


def small_places(width, hidden):
    front = 3 * width + hidden
    return {
        "bq": (0, width),
        "bv": (width, 2 * width),
        "bo": (2 * width, 3 * width),
        "b1": (3 * width, front),
        "b2": (front, front + width),
        "g1": (front + width, front + 2 * width),
        "s1": (front + 2 * width, front + 3 * width),
        "g2": (front + 3 * width, front + 4 * width),
        "s2": (front + 4 * width, front + 5 * width),
    }


def normalize(values):
    row_mean = jnp.mean(values, axis=-1, keepdims=True)
    centred = values - row_mean
    variance = jnp.mean(centred * centred, axis=-1, keepdims=True)
    inverse = lax.rsqrt(variance + LN_EPS)
    return centred * inverse, inverse


def norm_back(scaled, normed, inverse):
    return inverse * (
        scaled
        - jnp.mean(scaled, axis=-1, keepdims=True)
        - normed * jnp.mean(scaled * normed, axis=-1, keepdims=True)
    )


def fold_rows(values):
    return jnp.sum(values.reshape(values.shape[0] // 8, 8, values.shape[1]), axis=0)


def head_halves(pair):
    lane = lax.broadcasted_iota(jnp.int32, pair.shape, 1)
    zero = jnp.zeros_like(pair)
    return jnp.concatenate(
        [jnp.where(lane < HEAD_DIM, pair, zero), jnp.where(lane < HEAD_DIM, zero, pair)], axis=0
    )


def stack_heads(wide):
    return jnp.concatenate([wide[:, :SEG_LEN], wide[:, SEG_LEN:]], axis=0)


def row_spec(rows, columns):
    return pl.BlockSpec((rows, columns), lambda step, *_: (step, 0))


def held_spec(rows, columns, place=0):
    return pl.BlockSpec(
        (rows, columns), lambda step, *_: (0, place), pipeline_mode=pl.Buffered(1)
    )


def whole_spec(shape):
    return pl.BlockSpec(shape, lambda *_: (0,) * len(shape))


def call_kernel(
    body, name, grid, inputs, in_specs, outs, out_specs, scalars=(), scratch=(), after=(), aliases=None, flops=0,
    vmem=VMEM_LIMIT,
):
    lead, kept = len(scalars), len(scalars) + len(inputs)

    def wrapped(*refs):
        body(*refs[:kept], *refs[kept + len(after) :])

    listed = outs if isinstance(outs, list) else [outs]
    moved = sum(math.prod(x.shape) * x.dtype.itemsize for x in (*inputs, *listed))
    return pl.pallas_call(
        wrapped,
        grid_spec=pltpu.PrefetchScalarGridSpec(
            num_scalar_prefetch=lead,
            grid=grid,
            in_specs=[*in_specs, *[pl.BlockSpec(memory_space=pl.ANY)] * len(after)],
            out_specs=out_specs,
            scratch_shapes=list(scratch),
        ),
        out_shape=outs,
        input_output_aliases=aliases or {},
        cost_estimate=pl.CostEstimate(
            flops=int(flops), bytes_accessed=moved, transcendentals=0
        ),
        compiler_params=pltpu.CompilerParams(vmem_limit_bytes=vmem),
        name=name,
    )(*scalars, *inputs, *after)


def shaped(shape, kind):
    return jax.ShapeDtypeStruct(shape, kind)


def attention_forward_body(
    core, counts, inputs, mine_a, theirs_a, mine_b, theirs_b, small, joined_out, probs_out, mixed_out, normed_out, inverse_out, hidden_out, w_qkv, w_out, sems
):
    rows, width = inputs.shape
    at = small_places(width, small.shape[1] - 8 * width)

    @pl.when(pl.program_id(0) == 0)
    def _():
        copies = []
        groups, span, cut = mine_a.shape
        rest = 3 * width - cut
        moves = (
            (mine_a, theirs_a, w_qkv, 0, 0, cut),
            (mine_b, theirs_b, w_qkv, 0, cut, rest),
            (mine_b, theirs_b, w_out, rest + LANES, 0, width),
        )
        for mine, theirs, target, source, place, wide in moves:
            for group in range(groups):
                for flip, half in enumerate((mine, theirs)):
                    owner = 2 * group + (core[0] if flip == 0 else 1 - core[0])
                    block = target.at[
                        pl.ds(pl.multiple_of(owner * span, span), span), place : place + wide
                    ]
                    copies.append(
                        pltpu.make_async_copy(
                            half.at[group, :, source : source + wide], block, sems.at[len(copies)]
                        )
                    )
        for copy in copies:
            copy.start()
        for copy in copies:
            copy.wait()

    values = inputs[...]
    for part, bias in ((0, "bq"), (1, None), (2, "bv")):
        columns = slice(part * width, (part + 1) * width)
        product = dot_nn(values, w_qkv[:, columns])
        if bias is not None:
            product = product + small[:, slice(*at[bias])]
        joined_out[:, columns] = product.astype(BF16)
    for segment in range(rows // SEG_LEN):
        place = slice(segment * SEG_LEN, (segment + 1) * SEG_LEN)
        count = counts[pl.program_id(0) * (rows // SEG_LEN) + segment]
        visible = lax.broadcasted_iota(jnp.int32, (SEG_LEN, 2 * SEG_LEN), 0) < count
        for pair in range(width // LANES):
            low, high = pair * LANES, (pair + 1) * LANES
            query = joined_out[place, low:high] * jnp.asarray(SCALE_QK, BF16)
            keyed = joined_out[place, width + low : width + high]
            valued = joined_out[place, 2 * width + low : 2 * width + high]
            scores = jnp.where(visible, dot_nt(keyed, head_halves(query)), NEG_FILL)
            raised = jnp.exp(scores - jnp.max(scores, axis=0, keepdims=True))
            probs = raised * (1.0 / jnp.sum(raised, axis=0, keepdims=True))
            probs_out[place, 2 * low : 2 * high] = probs
            mixed = dot_tn(stack_heads(probs.astype(BF16)), head_halves(valued))
            mixed_out[place, low:high] = mixed.astype(BF16)
    attended = dot_nt(mixed_out[...], w_out[...]) + small[:, slice(*at["bo"])]
    normed, inverse = normalize(values.astype(F32) + attended)
    normed_out[...] = normed
    inverse_out[...] = jnp.broadcast_to(inverse, inverse_out.shape)
    hidden = normed * small[:, slice(*at["g1"])] + small[:, slice(*at["s1"])]
    hidden_out[...] = hidden.astype(BF16)


def attention_forward(core, counts, inputs, quarters, small, block=256):
    rows, width = inputs.shape
    hbm = pl.BlockSpec(memory_space=pl.ANY)
    return call_kernel(
        attention_forward_body,
        "attention_forward",
        (rows // block,),
        [inputs, *quarters, small],
        [row_spec(block, width), hbm, hbm, hbm, hbm, held_spec(1, small.shape[1])],
        [
            shaped((rows, 3 * width), BF16),
            shaped((rows, 2 * width), F32),
            shaped((rows, width), BF16),
            shaped((rows, width), F32),
            shaped((rows, LANES), F32),
            shaped((rows, width), BF16),
            shaped((width, 3 * width), BF16),
            shaped((width, width), BF16),
        ],
        [
            row_spec(block, 3 * width),
            row_spec(block, 2 * width),
            row_spec(block, width),
            row_spec(block, width),
            row_spec(block, LANES),
            row_spec(block, width),
            held_spec(width, 3 * width),
            held_spec(width, width),
        ],
        scalars=[core, counts],
        scratch=[pltpu.SemaphoreType.DMA((6 * quarters[0].shape[0],))],
        flops=12 * rows * width * width,
    )


def tile_spec(rows, columns, tiles):
    return pl.BlockSpec((rows, columns), lambda step, *_: (jnp.minimum(step, tiles - 1), 0))


def late_spec(shape, tiles):
    return pl.BlockSpec(shape, lambda step, *_: (0, 0, jnp.maximum(step - tiles, 0)))


def late_grad(tiles, core, left, right, keep_out, send_out, total):
    step, block = pl.program_id(0), total.shape[1]

    @pl.when(step >= tiles)
    def _():
        columns = pl.ds(pl.multiple_of((step - tiles) * block, block), block)
        total[...] = dot_tn(left[...], right[:, columns])
        split_rows(total, core, keep_out, send_out)


def mlp_forward_body(
    tiles,
    core,
    counts,
    normed_one,
    cotangent,
    w_up,
    w_down,
    small,
    result_out,
    slope_out,
    second_out,
    sums_out,
    keep_out,
    send_out,
    active_all,
    second_all,
    total,
    sums,
):
    step = pl.program_id(0)

    @pl.when(step == 0)
    def _():
        sums[...] = jnp.zeros_like(sums)

    @pl.when(step < tiles)
    def _():
        rows, width = normed_one.shape
        at = small_places(width, small.shape[1] - 8 * width)
        hidden = normed_one[...] * small[:, slice(*at["g1"])] + small[:, slice(*at["s1"])]
        pre_act = dot_nn(hidden.astype(BF16), w_up[...]) + small[:, slice(*at["b1"])]
        spread = 0.5 * (1.0 + lax.erf(pre_act * math.sqrt(0.5)))
        density = jnp.exp(-0.5 * pre_act * pre_act) * (1.0 / math.sqrt(2.0 * math.pi))
        active = (pre_act * spread).astype(BF16)
        place = pl.ds(pl.multiple_of(step * rows, rows), rows)
        active_all[place, :] = active
        slope_out[...] = spread + pre_act * density
        second = hidden + dot_nt(active, w_down[...]) + small[:, slice(*at["b2"])]
        normed, inverse = normalize(second)
        gain = small[:, slice(*at["g2"])]
        index = lax.broadcasted_iota(jnp.int32, (SEG_LEN, 1), 0)
        live = jnp.concatenate(
            [
                (index < counts[step * (rows // SEG_LEN) + segment]).astype(F32)
                for segment in range(rows // SEG_LEN)
            ],
            axis=0,
        )
        result_out[...] = ((normed * gain + small[:, slice(*at["s2"])]) * live).astype(BF16)
        incoming = cotangent[...].astype(F32) * live
        grad_second = norm_back(incoming * gain, normed, inverse)
        second_out[...] = grad_second
        second_all[place, :] = grad_second.astype(BF16)
        sums[0] += fold_rows(incoming * normed)
        sums[1] += fold_rows(incoming)
        sums[2] += fold_rows(grad_second)

    @pl.when(step == tiles)
    def _():
        sums_out[...] = jnp.sum(sums[...], axis=1)

    late_grad(tiles, core, second_all, active_all, keep_out, send_out, total)


def mlp_forward(core, counts, normed_one, cotangent, packed, small, groups, block=256, wide=512):
    rows, width = normed_one.shape
    hidden = packed.shape[1] // 2
    tiles = rows // block
    shape = (groups, width // (2 * groups), hidden)
    grad_spec = late_spec((*shape[:2], wide), tiles)
    return call_kernel(
        functools.partial(mlp_forward_body, tiles),
        "mlp_forward",
        (tiles + hidden // wide,),
        [normed_one, cotangent, packed, packed, small],
        [
            tile_spec(block, width, tiles),
            tile_spec(block, width, tiles),
            held_spec(width, hidden),
            held_spec(width, hidden, 1),
            held_spec(1, small.shape[1]),
        ],
        [
            shaped((rows, width), BF16),
            shaped((rows, hidden), F32),
            shaped((rows, width), F32),
            shaped((3, width), F32),
            shaped(shape, BF16),
            shaped(shape, BF16),
        ],
        [
            tile_spec(block, width, tiles),
            tile_spec(block, hidden, tiles),
            tile_spec(block, width, tiles),
            whole_spec((3, width)),
            grad_spec,
            grad_spec,
        ],
        scalars=[core, counts],
        scratch=[
            pltpu.VMEM((rows, hidden), BF16),
            pltpu.VMEM((rows, width), BF16),
            pltpu.VMEM((width, wide), F32),
            pltpu.VMEM((3, 8, width), F32),
        ],
        flops=6 * rows * width * hidden,
    )


def mlp_backward_body(
    tiles,
    core,
    grad_second,
    slope,
    normed_one,
    inverse_one,
    hidden_low,
    w_up,
    w_down,
    small,
    first_out,
    first_low_out,
    sums_out,
    wide_out,
    keep_out,
    send_out,
    pre_all,
    hidden_all,
    total,
    sums,
    wide_sums,
):
    step = pl.program_id(0)

    @pl.when(step == 0)
    def _():
        sums[...] = jnp.zeros_like(sums)
        wide_sums[...] = jnp.zeros_like(wide_sums)

    @pl.when(step < tiles)
    def _():
        rows, width = normed_one.shape
        hidden = slope.shape[1]
        chunk = width
        at = small_places(width, hidden)
        place = pl.ds(pl.multiple_of(step * rows, rows), rows)
        hidden_all[place, :] = hidden_low[...]
        incoming = grad_second[...]
        incoming_low = incoming.astype(BF16)
        grad_hidden = incoming
        for piece in range(hidden // chunk):
            columns = slice(piece * chunk, (piece + 1) * chunk)
            grad_pre = dot_nn(incoming_low, w_down[:, columns]) * slope[:, columns]
            wide_sums[:, columns] += fold_rows(grad_pre)
            grad_low = grad_pre.astype(BF16)
            pre_all[place, columns] = grad_low
            grad_hidden = grad_hidden + dot_nt(grad_low, w_up[:, columns])
        normed = normed_one[...]
        sums[0] += fold_rows(grad_hidden * normed)
        sums[1] += fold_rows(grad_hidden)
        grad_first = norm_back(
            grad_hidden * small[:, slice(*at["g1"])], normed, inverse_one[:, :1]
        )
        first_out[...] = grad_first
        first_low_out[...] = grad_first.astype(BF16)
        sums[2] += fold_rows(grad_first)

    @pl.when(step == tiles)
    def _():
        sums_out[...] = jnp.sum(sums[...], axis=1)
        wide_out[...] = jnp.sum(wide_sums[...], axis=0, keepdims=True)

    late_grad(tiles, core, hidden_all, pre_all, keep_out, send_out, total)


def mlp_backward(
    core, grad_second, slope, normed_one, inverse_one, hidden_low, packed, small, groups, after=(), block=256, wide=512
):
    rows, width = normed_one.shape
    hidden = slope.shape[1]
    tiles = rows // block
    shape = (groups, width // (2 * groups), hidden)
    grad_spec = late_spec((*shape[:2], wide), tiles)
    return call_kernel(
        functools.partial(mlp_backward_body, tiles),
        "mlp_backward",
        (tiles + hidden // wide,),
        [grad_second, slope, normed_one, inverse_one, hidden_low, packed, packed, small],
        [
            tile_spec(block, width, tiles),
            tile_spec(block, hidden, tiles),
            tile_spec(block, width, tiles),
            tile_spec(block, LANES, tiles),
            tile_spec(block, width, tiles),
            held_spec(width, hidden),
            held_spec(width, hidden, 1),
            held_spec(1, small.shape[1]),
        ],
        [
            shaped((rows, width), F32),
            shaped((rows, width), BF16),
            shaped((3, width), F32),
            shaped((1, hidden), F32),
            shaped(shape, BF16),
            shaped(shape, BF16),
        ],
        [
            tile_spec(block, width, tiles),
            tile_spec(block, width, tiles),
            whole_spec((3, width)),
            whole_spec((1, hidden)),
            grad_spec,
            grad_spec,
        ],
        scalars=[core],
        scratch=[
            pltpu.VMEM((rows, hidden), BF16),
            pltpu.VMEM((rows, width), BF16),
            pltpu.VMEM((width, wide), F32),
            pltpu.VMEM((3, 8, width), F32),
            pltpu.VMEM((8, hidden), F32),
        ],
        after=after,
        flops=6 * rows * width * hidden,
    )


def attention_backward_body(
    first_low, joined, probs, w_out, pieces, joined_grad_out, sums_out, folded_out, grad_mixed, sums
):
    rows, width = first_low.shape
    step = pl.program_id(0)

    @pl.when(step == 0)
    def _():
        sums[...] = jnp.zeros_like(sums)

    folded_out[...] = jnp.sum(pieces[...].astype(F32), axis=0)
    grad_mixed[...] = dot_nn(first_low[...], w_out[...]).astype(BF16)
    for segment in range(rows // SEG_LEN):
        place = slice(segment * SEG_LEN, (segment + 1) * SEG_LEN)
        for pair in range(width // LANES):
            low, high = pair * LANES, (pair + 1) * LANES
            query = joined[place, low:high]
            keyed = joined[place, width + low : width + high]
            valued = joined[place, 2 * width + low : 2 * width + high]
            grad_halves = head_halves(grad_mixed[place, low:high])
            weights = probs[place, 2 * low : 2 * high]
            grad_probs = dot_nt(valued, grad_halves)
            grad_valued = dot_nn(weights.astype(BF16), grad_halves)
            inner = jnp.sum(weights * grad_probs, axis=0, keepdims=True)
            scores_low = (weights * (grad_probs - inner) * SCALE_QK).astype(BF16)
            grad_keyed = dot_nn(scores_low, head_halves(query))
            grad_query = dot_tn(stack_heads(scores_low), head_halves(keyed))
            joined_grad_out[place, low:high] = grad_query.astype(BF16)
            joined_grad_out[place, width + low : width + high] = grad_keyed.astype(BF16)
            joined_grad_out[place, 2 * width + low : 2 * width + high] = grad_valued.astype(BF16)
            sums[0, :, low:high] += fold_rows(grad_query)
            sums[1, :, low:high] += fold_rows(grad_valued)

    @pl.when(step == pl.num_programs(0) - 1)
    def _():
        sums_out[...] = jnp.sum(sums[...], axis=1)


def attention_backward(first_low, joined, probs, w_out, pieces, after=(), block=256):
    rows, width = first_low.shape
    steps = rows // block
    count, own_rows, columns = pieces.shape
    part = columns // steps
    return call_kernel(
        attention_backward_body,
        "attention_backward",
        (steps,),
        [first_low, joined, probs, w_out, pieces],
        [
            row_spec(block, width),
            row_spec(block, 3 * width),
            row_spec(block, 2 * width),
            held_spec(width, width),
            pl.BlockSpec((count, own_rows, part), lambda step, *_: (0, 0, step)),
        ],
        [
            shaped((rows, 3 * width), BF16),
            shaped((2, width), F32),
            shaped((own_rows, columns), F32),
        ],
        [
            row_spec(block, 3 * width),
            whole_spec((2, width)),
            pl.BlockSpec((own_rows, part), lambda step, *_: (0, step)),
        ],
        scratch=[pltpu.VMEM((block, width), BF16), pltpu.VMEM((2, 8, width), F32)],
        after=after,
        flops=16 * rows * width * width,
    )


def grad_tokens_body(joined_grad, grad_first, w_qkv, grad_out):
    grad_out[...] = (dot_nt(joined_grad[...], w_qkv[...]) + grad_first[...]).astype(BF16)


def grad_tokens(joined_grad, grad_first, w_qkv, after=(), block=512):
    rows, width = grad_first.shape
    return call_kernel(
        grad_tokens_body,
        "grad_tokens",
        (rows // block,),
        [joined_grad, grad_first, w_qkv],
        [row_spec(block, 3 * width), row_spec(block, width), held_spec(width, 3 * width)],
        shaped((rows, width), BF16),
        row_spec(block, width),
        after=after,
        flops=6 * rows * width * width,
    )


def pack_body(*refs):
    packed_out, column = refs[-1], 0
    for ref in refs[:-1]:
        packed_out[:, column : column + ref.shape[1]] = ref[...].astype(BF16)
        column += ref.shape[1]


def pack_rows(arrays):
    shape = (arrays[0].shape[0], sum(array.shape[1] for array in arrays))
    return call_kernel(
        pack_body,
        "pack_rows",
        (1,),
        arrays,
        [whole_spec(array.shape) for array in arrays],
        shaped(shape, BF16),
        whole_spec(shape),
    )


def split_rows(total, core, keep_out, send_out, columns=slice(None), order=None):
    groups, rows = keep_out.shape[0], keep_out.shape[1]
    for group in range(groups):
        for flip, target in enumerate((keep_out, send_out)):
            half = core[0] if flip == 0 else 1 - core[0]
            start = pl.multiple_of((2 * group + half) * rows, rows)
            if order is None:
                part = total[pl.ds(start, rows), :]
            else:
                size = rows // len(order)
                places = [pl.multiple_of(start + place * size, 8) for place in order]
                part = jnp.concatenate([total[pl.ds(place, size), :] for place in places], axis=0)
            target[group, :, columns] = part.astype(BF16)


def weight_grad_body(order, core, left, right, keep_out, send_out, total):
    total[...] = dot_tn(left[...], right[...])
    split_rows(total, core, keep_out, send_out, order=order)


def weight_grad(core, left, right, groups, order=None, after=(), block=256):
    tokens, height = left.shape
    width = right.shape[1]
    shape = (groups, height // (2 * groups), width)
    out_spec = pl.BlockSpec((*shape[:2], block), lambda step, *_: (0, 0, step))
    return call_kernel(
        functools.partial(weight_grad_body, order),
        "weight_grad",
        (width // block,),
        [left, right],
        [
            whole_spec((tokens, height)),
            pl.BlockSpec((tokens, block), lambda step, *_: (0, step)),
        ],
        [shaped(shape, BF16)] * 2,
        [out_spec, out_spec],
        scalars=[core],
        scratch=[pltpu.VMEM((height, block), F32)],
        after=after,
        flops=2 * tokens * height * width,
    )


def qkv_grad_body(order, core, left, right, extra, keep_out, send_out, keep_last, send_last, total):
    step, block = pl.program_id(0), right.shape[1]
    total[...] = dot_tn(left[...], right[...])

    @pl.when(step < 2)
    def _():
        columns = pl.ds(pl.multiple_of(step * block, block), block)
        split_rows(total, core, keep_out, send_out, columns)

    @pl.when(step == 2)
    def _():
        split_rows(total, core, keep_last, send_last, order=order)

    @pl.when(step == 0)
    def _():
        for group in range(keep_out.shape[0]):
            for flip, target in enumerate((keep_out, send_out)):
                half = core[0] if flip == 0 else 1 - core[0]
                target[group, :, target.shape[2] - LANES :] = extra[group, half].astype(BF16)


def qkv_grad(core, left, right, groups, extra, order):
    tokens, width = left.shape
    lead = (groups, width // (2 * groups))
    shapes = [(*lead, 2 * width + LANES)] * 2 + [(*lead, width)] * 2
    return call_kernel(
        functools.partial(qkv_grad_body, order),
        "qkv_grad",
        (3,),
        [left, right, extra],
        [
            whole_spec((tokens, width)),
            pl.BlockSpec((tokens, width), lambda step, *_: (0, step)),
            whole_spec(extra.shape),
        ],
        [shaped(shape, BF16) for shape in shapes],
        [whole_spec(shape) for shape in shapes],
        scalars=[core],
        scratch=[pltpu.VMEM((width, width), F32)],
        flops=6 * tokens * width * width,
    )


def plane_split_body(count, place, keep_front, other_front, *refs):
    arrays, front_out, outs = refs[: -count - 1], refs[-count - 1], refs[-count:]
    column = 0
    for keep, received in zip(arrays[::2], arrays[1::2]):
        width = keep.shape[-1]
        for step, out in enumerate(outs):
            chunk = place[0] ^ step
            both = keep[chunk].astype(F32) + received[chunk].astype(F32)
            out[:, column : column + width] = both.astype(out.dtype)
        column += width
    front_out[...] = (keep_front[...].astype(F32) + other_front[...].astype(F32)).astype(BF16)


def plane_split(front, pairs, place, count, after=()):
    arrays = [part.reshape(count, -1, part.shape[-1]) for pair in pairs for part in pair]
    shape = (arrays[0].shape[1], sum(array.shape[2] for array in arrays[::2]))
    outs = [shaped(front[0].shape, BF16), shaped(shape, F32)] + [shaped(shape, BF16)] * (count - 1)
    return call_kernel(
        functools.partial(plane_split_body, count),
        "plane_split",
        (1,),
        [*front, *arrays],
        [whole_spec(array.shape) for array in (*front, *arrays)],
        outs,
        [whole_spec(out.shape) for out in outs],
        scalars=[place],
        after=after,
    )


def line_split_body(pieces, count, place, *refs):
    outs, total = refs[-1 - count : -1], refs[-1]
    total[...] = sum(ref[...].astype(F32) for ref in refs[:pieces])
    rows = outs[0].shape[0]
    for step, out in enumerate(outs):
        start = pl.multiple_of((place[0] ^ step) * rows, rows)
        out[...] = total[pl.ds(start, rows), :].astype(out.dtype)


def line_split(pieces, place, count, after=()):
    rows, width = pieces[0].shape
    shape = (rows // count, width)
    outs = [shaped(shape, F32)] + [shaped(shape, BF16)] * (count - 1)
    return call_kernel(
        functools.partial(line_split_body, len(pieces), count),
        "line_split",
        (1,),
        pieces,
        [whole_spec(piece.shape) for piece in pieces],
        outs,
        [whole_spec(shape)] * count,
        scalars=[place],
        scratch=[pltpu.VMEM((rows, width), F32)],
        after=after,
    )


def trade(parts, axis):
    count = len(parts)
    return [parts[0]] + [
        lax.ppermute(parts[step], axis, [(place, place ^ step) for place in range(count)])
        for step in range(1, count)
    ]


def add_pairs(pairs):
    sums = [(keep.astype(F32) + received.astype(F32)).astype(BF16) for keep, received in pairs]
    return sums[0] if len(sums) == 1 else jnp.concatenate(sums, axis=-1)


def fold_body(pieces, total_out):
    total_out[...] = jnp.sum(pieces[...].astype(F32), axis=0)


def fold_pieces(pieces, after=()):
    count, rows, width = pieces.shape
    return call_kernel(
        fold_body,
        "fold_pieces",
        (1,),
        [pieces],
        [whole_spec(pieces.shape)],
        shaped((rows, width), F32),
        whole_spec((rows, width)),
        after=after,
        vmem=SMALL_VMEM,
    )


def squares_body(parts, pieces, *refs):
    total_out, *totals, spread_out = refs[-3 if parts else -2 :]
    others = refs[parts : len(refs) - (3 if parts else 2)]
    total = jnp.sum(pieces[...].astype(F32), axis=0)
    total_out[...] = total
    squares = jnp.sum(total * total)
    if parts:
        total = sum(ref[...].astype(F32) for ref in refs[:parts])
        totals[0][...] = total
        squares = squares + jnp.sum(total * total)
    for other in others:
        squares = squares + jnp.sum(other[...] * other[...])
    spread_out[...] = jnp.zeros(spread_out.shape, F32) + squares


def fold_with_squares(pieces, parts, others, copies, after=()):
    count, rows, width = pieces.shape
    inputs = [pieces, *parts, *others]
    outs = [shaped((rows, width), F32)]
    if parts:
        outs.append(shaped(parts[0].shape, F32))
    outs.append(shaped((copies, LANES), F32))
    return call_kernel(
        functools.partial(squares_body, len(parts)),
        "fold_with_squares",
        (1,),
        inputs,
        [whole_spec(array.shape) for array in inputs],
        outs,
        [whole_spec(array.shape) for array in outs],
        after=after,
        vmem=SMALL_VMEM,
    )


def update_body(places, squares, *refs):
    count = len(places)
    norm_out, results = refs[-1], refs[-1 - 4 * count : -1]
    states = refs[-1 - 7 * count : -1 - 4 * count]
    totals = refs[: -1 - 7 * count]
    grad_norm = jnp.sqrt(jnp.sum(squares[:, :1], axis=0, keepdims=True))
    factor = CLIP_LIMIT / jnp.maximum(grad_norm, CLIP_LIMIT)
    norm_out[...] = jnp.broadcast_to(grad_norm, norm_out.shape)
    for index, (source, low, high) in enumerate(places):
        weight, first, second = (ref[...] for ref in states[3 * index : 3 * index + 3])
        fresh = adam_update(
            weight, first, second, totals[source][:, low:high] * factor, RATE_MATRIX, DECAY
        )
        for target, value in zip(results[4 * index : 4 * index + 4], fresh):
            target[...] = value


def update_weights(squares, totals, places, states):
    inputs = [squares, *totals, *states]
    outs = []
    for index in range(len(places)):
        shape = states[3 * index].shape
        outs += [shaped(shape, F32)] * 3 + [shaped(shape, BF16)]
    outs.append(shaped((1, LANES), F32))
    return call_kernel(
        functools.partial(update_body, places),
        "update_weights",
        (1,),
        inputs,
        [whole_spec(array.shape) for array in inputs],
        outs,
        [whole_spec(array.shape) for array in outs],
        vmem=SMALL_VMEM,
    )


def gather_axis(value, axis, size):
    pieces = [value] + [
        lax.ppermute(value, axis, [(place, place ^ step) for place in range(size)])
        for step in range(1, size)
    ]
    stacked = jnp.stack(pieces)
    place, bit = lax.axis_index(axis), 1
    while bit < size:
        paired = stacked.reshape(size // (2 * bit), 2, bit, *value.shape)
        stacked = jnp.where((place & bit) != 0, paired[:, ::-1], paired).reshape(stacked.shape)
        bit *= 2
    return stacked


def adam_update(weight, first_moment, second_moment, grad_clip, rate, decay):
    fresh_one = BETA_ONE * first_moment + (1.0 - BETA_ONE) * grad_clip
    fresh_two = BETA_TWO * second_moment + (1.0 - BETA_TWO) * grad_clip * grad_clip
    correct_one = 1.0 - BETA_ONE**STEP
    correct_two = 1.0 - BETA_TWO**STEP
    stepped = fresh_one / correct_one / (jnp.sqrt(fresh_two / correct_two) + ADAM_EPS)
    updated = weight - rate * (stepped + decay * weight)
    return (updated, fresh_one, fresh_two, updated.astype(BF16))


def body(
    high_count,
    zed_count,
    low_count,
    tokens,
    cotangent,
    seg_counts,
    w_qkv,
    w_out,
    w_up,
    w_down,
    small_params,
    first_qkv,
    second_qkv,
    first_out,
    second_out,
    first_up,
    second_up,
    first_down,
    second_down,
    first_small,
    second_small,
):
    inner_count = zed_count * low_count
    device_count = 2 * high_count * inner_count
    own_rows, width = w_out.shape
    hidden = w_up.shape[1]
    own_small = small_params.shape[0]
    core = lax.axis_index("core").astype(jnp.int32).reshape(1)
    swap = [(0, 1), (1, 0)]

    back = pack_rows([w_up, w_down])
    packed = lax.all_gather(back, ALL, axis=0, tiled=True)
    low_qkv = w_qkv.astype(BF16)
    per_row = own_small // own_rows
    small_block = jnp.pad(
        small_params.astype(BF16).reshape(own_rows, per_row), ((0, 0), (0, LANES - per_row))
    )
    front = jnp.concatenate([low_qkv, small_block, w_out.astype(BF16)], axis=1)
    along = gather_axis(front, "zed", zed_count)
    split = 2 * width
    at_small = low_qkv.shape[1] - split
    quarters = []
    for piece, order in ((along[..., :split], (0, 1)), (along[..., split:], (1, 0))):
        for stage in order:
            if stage == 0:
                piece = jnp.moveaxis(gather_axis(piece, "low", low_count), 0, -3)
            else:
                piece = gather_axis(piece, "hi", high_count)
        quarters.append(piece.reshape(high_count, inner_count * own_rows, piece.shape[-1]))
    quarters = [
        half
        for quarter in quarters
        for half in (quarter, lax.ppermute(quarter, "core", swap))
    ]
    mine, theirs = (half[..., at_small : at_small + per_row] for half in quarters[2:])
    small = (
        jnp.where(core[0] == 0, jnp.stack([mine, theirs], 1), jnp.stack([theirs, mine], 1))
        .reshape(1, device_count * own_small)
        .astype(F32)
    )

    (
        joined,
        probs,
        mixed,
        normed_one,
        inverse_one,
        hidden_low,
        whole_qkv,
        whole_out,
    ) = attention_forward(core, seg_counts, tokens, quarters, small)
    result, slope, grad_second, sums_two, *down = mlp_forward(
        core, seg_counts, normed_one, cotangent, packed, small, high_count
    )

    def swap_cores(parts):
        keep, send = parts
        return keep, lax.ppermute(send, "core", swap)

    def peer_sum(both):
        columns = both.shape[-1]
        pieces = lax.all_to_all(both.reshape(-1, columns), PEERS, 0, 0, tiled=True)
        return pieces.reshape(high_count * inner_count, own_rows, columns)

    down = add_pairs([swap_cores(down)])
    grad_first, first_low, sums_one, sums_wide, *up = mlp_backward(
        core,
        grad_second,
        slope,
        normed_one,
        inverse_one,
        hidden_low,
        packed,
        small,
        high_count,
        after=[down],
    )
    down = peer_sum(down)
    by_low = [zed * low_count + low for low in range(low_count) for zed in range(zed_count)]
    order = by_low if own_rows % 8 == 0 else None
    out = weight_grad(core, first_low, mixed, high_count, order, after=[up[0]])
    keep, received = swap_cores(up)
    keep, out_done = lax.optimization_barrier((keep, out[0]))
    up = add_pairs([(keep, received)])
    out = swap_cores(out)
    joined_grad, sums_qv, sum_down = attention_backward(
        first_low, joined, probs, whole_out, down, after=[out_done, up]
    )
    up = peer_sum(up)
    grad_small = jnp.concatenate(
        [
            sums_qv.reshape(-1),
            sums_one[2],
            sums_wide[0],
            sums_two[2],
            sums_one[:2].reshape(-1),
            sums_two[:2].reshape(-1),
        ]
    )
    by_owner = jnp.pad(
        grad_small.reshape(high_count, 2, inner_count * own_rows, per_row),
        ((0, 0),) * 3 + ((0, LANES - per_row),),
    )
    *query, keep, send = qkv_grad(core, tokens, joined_grad, high_count, by_owner, order)
    value = swap_cores((keep, send))
    query = swap_cores(query)
    if order is not None:
        plane = high_count * low_count
        high, low = lax.axis_index("hi"), lax.axis_index("low")
        place = (high * low_count + low).astype(jnp.int32).reshape(1)
        front, *last = plane_split(query, [value, out], place, plane)
        last = trade(last, PLANE)
        grad_inputs = grad_tokens(joined_grad, grad_first, whole_qkv, after=[front, last[0]])
        place = lax.axis_index("zed").astype(jnp.int32).reshape(1)
        last = trade(line_split(last, place, zed_count, after=[grad_inputs]), "zed")
    else:
        front = add_pairs([query, value, out])
        grad_inputs = grad_tokens(joined_grad, grad_first, whole_qkv, after=[front])
        last = []
    sum_up = fold_pieces(up, after=[grad_inputs, *last[:1]])
    sum_front, *sum_last, spread = fold_with_squares(
        peer_sum(front), last, [sum_up, sum_down], device_count
    )
    cut = 2 * width + LANES
    if order is None:
        sum_last = [sum_front[:, cut:]]
    sum_qkv = jnp.concatenate([sum_front[:, : 2 * width], sum_last[0][:, :width]], axis=1)
    squares = lax.all_to_all(spread, ALL, 0, 0, tiled=True)
    *updated, norm_row = update_weights(
        squares,
        [sum_qkv, sum_last[0], sum_up, sum_down],
        ((0, 0, 3 * width), (1, width, 2 * width), (2, 0, hidden), (3, 0, hidden)),
        [
            *(w_qkv, first_qkv, second_qkv),
            *(w_out, first_out, second_out),
            *(w_up, first_up, second_up),
            *(w_down, first_down, second_down),
        ],
    )
    grad_norm = norm_row[0, 0]
    factor = CLIP_LIMIT / jnp.maximum(grad_norm, CLIP_LIMIT)
    sum_small = sum_front[:, 2 * width : 2 * width + per_row].reshape(own_small)
    updated += adam_update(
        small_params, first_small, second_small, sum_small * factor, RATE_SMALL, 0.0
    )
    return (result, grad_inputs, grad_norm, *updated)


def solution(mesh):
    outer, inner = mesh.devices.shape
    finer = Mesh(mesh.devices.reshape(outer // 2, 2, inner // 2, 2), ALL)
    rows, flat = P(ALL, None), P(ALL)
    return jax.shard_map(
        functools.partial(body, outer // 2, inner // 2, 2),
        mesh=finer,
        in_specs=(rows, rows, flat) + (rows,) * 4 + (flat,) + (rows,) * 8 + (flat,) * 2,
        out_specs=(rows, rows, P()) + (rows,) * 16 + (flat,) * 4,
        check_vma=False,
    )
```

```python
import functools
import math

import jax
import jax.numpy as jnp
from jax import lax
from jax.experimental import pallas as pl
from jax.experimental.pallas import tpu as pltpu
from jax.sharding import Mesh
from jax.sharding import PartitionSpec as P

HEAD_DIM = 64
SEG_LEN = 128
STEP = 10
NEG_FILL = -1e30
SCALE_QK = 0.125
LN_EPS = 1e-05
BETA_ONE = 0.9
BETA_TWO = 0.999
ADAM_EPS = 1e-08
RATE_MATRIX = 0.03
RATE_SMALL = 0.3
DECAY = 0.01
CLIP_LIMIT = 1.0

LANES = 128
VMEM_LIMIT = 60 * 1024 * 1024
SMALL_VMEM = 60 * 1024 * 1024
F32 = jnp.float32
BF16 = jnp.bfloat16
ALL = ("hi", "core", "zed", "low")
PEERS = ("hi", "zed", "low")
PLANE = ("hi", "low")


def dot_nn(left, right):
    return jnp.dot(left, right, preferred_element_type=F32)


def dot_nt(left, right):
    return lax.dot_general(left, right, (((1,), (1,)), ((), ())), preferred_element_type=F32)


def dot_tn(left, right):
    return lax.dot_general(left, right, (((0,), (0,)), ((), ())), preferred_element_type=F32)


def small_places(width, hidden):
    front = 3 * width + hidden
    return {
        "bq": (0, width),
        "bv": (width, 2 * width),
        "bo": (2 * width, 3 * width),
        "b1": (3 * width, front),
        "b2": (front, front + width),
        "g1": (front + width, front + 2 * width),
        "s1": (front + 2 * width, front + 3 * width),
        "g2": (front + 3 * width, front + 4 * width),
        "s2": (front + 4 * width, front + 5 * width),
    }


def normalize(values):
    row_mean = jnp.mean(values, axis=-1, keepdims=True)
    centred = values - row_mean
    variance = jnp.mean(centred * centred, axis=-1, keepdims=True)
    inverse = lax.rsqrt(variance + LN_EPS)
    return centred * inverse, inverse


def norm_back(scaled, normed, inverse):
    return inverse * (
        scaled
        - jnp.mean(scaled, axis=-1, keepdims=True)
        - normed * jnp.mean(scaled * normed, axis=-1, keepdims=True)
    )


def fold_rows(values):
    return jnp.sum(values.reshape(values.shape[0] // 8, 8, values.shape[1]), axis=0)


def head_halves(pair):
    lane = lax.broadcasted_iota(jnp.int32, pair.shape, 1)
    zero = jnp.zeros_like(pair)
    return jnp.concatenate(
        [jnp.where(lane < HEAD_DIM, pair, zero), jnp.where(lane < HEAD_DIM, zero, pair)], axis=0
    )


def stack_heads(wide):
    return jnp.concatenate([wide[:, :SEG_LEN], wide[:, SEG_LEN:]], axis=0)


def row_spec(rows, columns):
    return pl.BlockSpec((rows, columns), lambda step, *_: (step, 0))


def held_spec(rows, columns, place=0):
    return pl.BlockSpec(
        (rows, columns), lambda step, *_: (0, place), pipeline_mode=pl.Buffered(1)
    )


def whole_spec(shape):
    return pl.BlockSpec(shape, lambda *_: (0,) * len(shape))


def call_kernel(
    body, name, grid, inputs, in_specs, outs, out_specs, scalars=(), scratch=(), after=(), aliases=None, flops=0,
    vmem=VMEM_LIMIT,
):
    lead, kept = len(scalars), len(scalars) + len(inputs)

    def wrapped(*refs):
        body(*refs[:kept], *refs[kept + len(after) :])

    listed = outs if isinstance(outs, list) else [outs]
    moved = sum(math.prod(x.shape) * x.dtype.itemsize for x in (*inputs, *listed))
    return pl.pallas_call(
        wrapped,
        grid_spec=pltpu.PrefetchScalarGridSpec(
            num_scalar_prefetch=lead,
            grid=grid,
            in_specs=[*in_specs, *[pl.BlockSpec(memory_space=pl.ANY)] * len(after)],
            out_specs=out_specs,
            scratch_shapes=list(scratch),
        ),
        out_shape=outs,
        input_output_aliases=aliases or {},
        cost_estimate=pl.CostEstimate(
            flops=int(flops), bytes_accessed=moved, transcendentals=0
        ),
        compiler_params=pltpu.CompilerParams(vmem_limit_bytes=vmem),
        name=name,
    )(*scalars, *inputs, *after)


def shaped(shape, kind):
    return jax.ShapeDtypeStruct(shape, kind)


def attention_forward_body(
    core, counts, inputs, mine_a, theirs_a, mine_b, theirs_b, small, joined_out, probs_out, mixed_out, normed_out, inverse_out, hidden_out, w_qkv, w_out, sems
):
    rows, width = inputs.shape
    at = small_places(width, small.shape[1] - 8 * width)

    @pl.when(pl.program_id(0) == 0)
    def _():
        copies = []
        groups, span, cut = mine_a.shape
        rest = 3 * width - cut
        moves = (
            (mine_a, theirs_a, w_qkv, 0, 0, cut),
            (mine_b, theirs_b, w_qkv, 0, cut, rest),
            (mine_b, theirs_b, w_out, rest + LANES, 0, width),
        )
        for mine, theirs, target, source, place, wide in moves:
            for group in range(groups):
                for flip, half in enumerate((mine, theirs)):
                    owner = 2 * group + (core[0] if flip == 0 else 1 - core[0])
                    block = target.at[
                        pl.ds(pl.multiple_of(owner * span, span), span), place : place + wide
                    ]
                    copies.append(
                        pltpu.make_async_copy(
                            half.at[group, :, source : source + wide], block, sems.at[len(copies)]
                        )
                    )
        for copy in copies:
            copy.start()
        for copy in copies:
            copy.wait()

    values = inputs[...]
    for part, bias in ((0, "bq"), (1, None), (2, "bv")):
        columns = slice(part * width, (part + 1) * width)
        product = dot_nn(values, w_qkv[:, columns])
        if bias is not None:
            product = product + small[:, slice(*at[bias])]
        joined_out[:, columns] = product.astype(BF16)
    for segment in range(rows // SEG_LEN):
        place = slice(segment * SEG_LEN, (segment + 1) * SEG_LEN)
        count = counts[pl.program_id(0) * (rows // SEG_LEN) + segment]
        visible = lax.broadcasted_iota(jnp.int32, (SEG_LEN, 2 * SEG_LEN), 0) < count
        for pair in range(width // LANES):
            low, high = pair * LANES, (pair + 1) * LANES
            query = joined_out[place, low:high] * jnp.asarray(SCALE_QK, BF16)
            keyed = joined_out[place, width + low : width + high]
            valued = joined_out[place, 2 * width + low : 2 * width + high]
            scores = jnp.where(visible, dot_nt(keyed, head_halves(query)), NEG_FILL)
            raised = jnp.exp(scores - jnp.max(scores, axis=0, keepdims=True))
            probs = raised * (1.0 / jnp.sum(raised, axis=0, keepdims=True))
            probs_out[place, 2 * low : 2 * high] = probs
            mixed = dot_tn(stack_heads(probs.astype(BF16)), head_halves(valued))
            mixed_out[place, low:high] = mixed.astype(BF16)
    attended = dot_nt(mixed_out[...], w_out[...]) + small[:, slice(*at["bo"])]
    normed, inverse = normalize(values.astype(F32) + attended)
    normed_out[...] = normed
    inverse_out[...] = jnp.broadcast_to(inverse, inverse_out.shape)
    hidden = normed * small[:, slice(*at["g1"])] + small[:, slice(*at["s1"])]
    hidden_out[...] = hidden.astype(BF16)


def attention_forward(core, counts, inputs, quarters, small, block=256):
    rows, width = inputs.shape
    hbm = pl.BlockSpec(memory_space=pl.ANY)
    return call_kernel(
        attention_forward_body,
        "attention_forward",
        (rows // block,),
        [inputs, *quarters, small],
        [row_spec(block, width), hbm, hbm, hbm, hbm, held_spec(1, small.shape[1])],
        [
            shaped((rows, 3 * width), BF16),
            shaped((rows, 2 * width), F32),
            shaped((rows, width), BF16),
            shaped((rows, width), F32),
            shaped((rows, LANES), F32),
            shaped((rows, width), BF16),
            shaped((width, 3 * width), BF16),
            shaped((width, width), BF16),
        ],
        [
            row_spec(block, 3 * width),
            row_spec(block, 2 * width),
            row_spec(block, width),
            row_spec(block, width),
            row_spec(block, LANES),
            row_spec(block, width),
            held_spec(width, 3 * width),
            held_spec(width, width),
        ],
        scalars=[core, counts],
        scratch=[pltpu.SemaphoreType.DMA((6 * quarters[0].shape[0],))],
        flops=12 * rows * width * width,
    )


def tile_spec(rows, columns, tiles):
    return pl.BlockSpec((rows, columns), lambda step, *_: (jnp.minimum(step, tiles - 1), 0))


def late_spec(shape, tiles):
    return pl.BlockSpec(shape, lambda step, *_: (0, 0, jnp.maximum(step - tiles, 0)))


def late_grad(tiles, core, left, right, keep_out, send_out, total):
    step, block = pl.program_id(0), total.shape[1]

    @pl.when(step >= tiles)
    def _():
        columns = pl.ds(pl.multiple_of((step - tiles) * block, block), block)
        total[...] = dot_tn(left[...], right[:, columns])
        split_rows(total, core, keep_out, send_out)


def mlp_forward_body(
    tiles,
    core,
    counts,
    normed_one,
    cotangent,
    w_up,
    w_down,
    small,
    result_out,
    slope_out,
    second_out,
    sums_out,
    keep_out,
    send_out,
    active_all,
    second_all,
    total,
    sums,
):
    step = pl.program_id(0)

    @pl.when(step == 0)
    def _():
        sums[...] = jnp.zeros_like(sums)

    @pl.when(step < tiles)
    def _():
        rows, width = normed_one.shape
        at = small_places(width, small.shape[1] - 8 * width)
        hidden = normed_one[...] * small[:, slice(*at["g1"])] + small[:, slice(*at["s1"])]
        pre_act = dot_nn(hidden.astype(BF16), w_up[...]) + small[:, slice(*at["b1"])]
        spread = 0.5 * (1.0 + lax.erf(pre_act * math.sqrt(0.5)))
        density = jnp.exp(-0.5 * pre_act * pre_act) * (1.0 / math.sqrt(2.0 * math.pi))
        active = (pre_act * spread).astype(BF16)
        place = pl.ds(pl.multiple_of(step * rows, rows), rows)
        active_all[place, :] = active
        slope_out[...] = spread + pre_act * density
        second = hidden + dot_nt(active, w_down[...]) + small[:, slice(*at["b2"])]
        normed, inverse = normalize(second)
        gain = small[:, slice(*at["g2"])]
        index = lax.broadcasted_iota(jnp.int32, (SEG_LEN, 1), 0)
        live = jnp.concatenate(
            [
                (index < counts[step * (rows // SEG_LEN) + segment]).astype(F32)
                for segment in range(rows // SEG_LEN)
            ],
            axis=0,
        )
        result_out[...] = ((normed * gain + small[:, slice(*at["s2"])]) * live).astype(BF16)
        incoming = cotangent[...].astype(F32) * live
        grad_second = norm_back(incoming * gain, normed, inverse)
        second_out[...] = grad_second
        second_all[place, :] = grad_second.astype(BF16)
        sums[0] += fold_rows(incoming * normed)
        sums[1] += fold_rows(incoming)
        sums[2] += fold_rows(grad_second)

    @pl.when(step == tiles)
    def _():
        sums_out[...] = jnp.sum(sums[...], axis=1)

    late_grad(tiles, core, second_all, active_all, keep_out, send_out, total)


def mlp_forward(core, counts, normed_one, cotangent, packed, small, groups, block=256, wide=512):
    rows, width = normed_one.shape
    hidden = packed.shape[1] // 2
    tiles = rows // block
    shape = (groups, width // (2 * groups), hidden)
    grad_spec = late_spec((*shape[:2], wide), tiles)
    return call_kernel(
        functools.partial(mlp_forward_body, tiles),
        "mlp_forward",
        (tiles + hidden // wide,),
        [normed_one, cotangent, packed, packed, small],
        [
            tile_spec(block, width, tiles),
            tile_spec(block, width, tiles),
            held_spec(width, hidden),
            held_spec(width, hidden, 1),
            held_spec(1, small.shape[1]),
        ],
        [
            shaped((rows, width), BF16),
            shaped((rows, hidden), F32),
            shaped((rows, width), F32),
            shaped((3, width), F32),
            shaped(shape, BF16),
            shaped(shape, BF16),
        ],
        [
            tile_spec(block, width, tiles),
            tile_spec(block, hidden, tiles),
            tile_spec(block, width, tiles),
            whole_spec((3, width)),
            grad_spec,
            grad_spec,
        ],
        scalars=[core, counts],
        scratch=[
            pltpu.VMEM((rows, hidden), BF16),
            pltpu.VMEM((rows, width), BF16),
            pltpu.VMEM((width, wide), F32),
            pltpu.VMEM((3, 8, width), F32),
        ],
        flops=6 * rows * width * hidden,
    )


def mlp_backward_body(
    tiles,
    core,
    grad_second,
    slope,
    normed_one,
    inverse_one,
    hidden_low,
    w_up,
    w_down,
    small,
    first_out,
    first_low_out,
    sums_out,
    wide_out,
    keep_out,
    send_out,
    pre_all,
    hidden_all,
    total,
    sums,
    wide_sums,
):
    step = pl.program_id(0)

    @pl.when(step == 0)
    def _():
        sums[...] = jnp.zeros_like(sums)
        wide_sums[...] = jnp.zeros_like(wide_sums)

    @pl.when(step < tiles)
    def _():
        rows, width = normed_one.shape
        hidden = slope.shape[1]
        chunk = width
        at = small_places(width, hidden)
        place = pl.ds(pl.multiple_of(step * rows, rows), rows)
        hidden_all[place, :] = hidden_low[...]
        incoming = grad_second[...]
        incoming_low = incoming.astype(BF16)
        grad_hidden = incoming
        for piece in range(hidden // chunk):
            columns = slice(piece * chunk, (piece + 1) * chunk)
            grad_pre = dot_nn(incoming_low, w_down[:, columns]) * slope[:, columns]
            wide_sums[:, columns] += fold_rows(grad_pre)
            grad_low = grad_pre.astype(BF16)
            pre_all[place, columns] = grad_low
            grad_hidden = grad_hidden + dot_nt(grad_low, w_up[:, columns])
        normed = normed_one[...]
        sums[0] += fold_rows(grad_hidden * normed)
        sums[1] += fold_rows(grad_hidden)
        grad_first = norm_back(
            grad_hidden * small[:, slice(*at["g1"])], normed, inverse_one[:, :1]
        )
        first_out[...] = grad_first
        first_low_out[...] = grad_first.astype(BF16)
        sums[2] += fold_rows(grad_first)

    @pl.when(step == tiles)
    def _():
        sums_out[...] = jnp.sum(sums[...], axis=1)
        wide_out[...] = jnp.sum(wide_sums[...], axis=0, keepdims=True)

    late_grad(tiles, core, hidden_all, pre_all, keep_out, send_out, total)


def mlp_backward(
    core, grad_second, slope, normed_one, inverse_one, hidden_low, packed, small, groups, after=(), block=256, wide=512
):
    rows, width = normed_one.shape
    hidden = slope.shape[1]
    tiles = rows // block
    shape = (groups, width // (2 * groups), hidden)
    grad_spec = late_spec((*shape[:2], wide), tiles)
    return call_kernel(
        functools.partial(mlp_backward_body, tiles),
        "mlp_backward",
        (tiles + hidden // wide,),
        [grad_second, slope, normed_one, inverse_one, hidden_low, packed, packed, small],
        [
            tile_spec(block, width, tiles),
            tile_spec(block, hidden, tiles),
            tile_spec(block, width, tiles),
            tile_spec(block, LANES, tiles),
            tile_spec(block, width, tiles),
            held_spec(width, hidden),
            held_spec(width, hidden, 1),
            held_spec(1, small.shape[1]),
        ],
        [
            shaped((rows, width), F32),
            shaped((rows, width), BF16),
            shaped((3, width), F32),
            shaped((1, hidden), F32),
            shaped(shape, BF16),
            shaped(shape, BF16),
        ],
        [
            tile_spec(block, width, tiles),
            tile_spec(block, width, tiles),
            whole_spec((3, width)),
            whole_spec((1, hidden)),
            grad_spec,
            grad_spec,
        ],
        scalars=[core],
        scratch=[
            pltpu.VMEM((rows, hidden), BF16),
            pltpu.VMEM((rows, width), BF16),
            pltpu.VMEM((width, wide), F32),
            pltpu.VMEM((3, 8, width), F32),
            pltpu.VMEM((8, hidden), F32),
        ],
        after=after,
        flops=6 * rows * width * hidden,
    )


def attention_backward_body(
    first_low, joined, probs, w_out, pieces, joined_grad_out, sums_out, folded_out, grad_mixed, sums
):
    rows, width = first_low.shape
    step = pl.program_id(0)

    @pl.when(step == 0)
    def _():
        sums[...] = jnp.zeros_like(sums)

    folded_out[...] = jnp.sum(pieces[...].astype(F32), axis=0)
    grad_mixed[...] = dot_nn(first_low[...], w_out[...]).astype(BF16)
    for segment in range(rows // SEG_LEN):
        place = slice(segment * SEG_LEN, (segment + 1) * SEG_LEN)
        for pair in range(width // LANES):
            low, high = pair * LANES, (pair + 1) * LANES
            query = joined[place, low:high]
            keyed = joined[place, width + low : width + high]
            valued = joined[place, 2 * width + low : 2 * width + high]
            grad_halves = head_halves(grad_mixed[place, low:high])
            weights = probs[place, 2 * low : 2 * high]
            grad_probs = dot_nt(valued, grad_halves)
            grad_valued = dot_nn(weights.astype(BF16), grad_halves)
            inner = jnp.sum(weights * grad_probs, axis=0, keepdims=True)
            scores_low = (weights * (grad_probs - inner) * SCALE_QK).astype(BF16)
            grad_keyed = dot_nn(scores_low, head_halves(query))
            grad_query = dot_tn(stack_heads(scores_low), head_halves(keyed))
            joined_grad_out[place, low:high] = grad_query.astype(BF16)
            joined_grad_out[place, width + low : width + high] = grad_keyed.astype(BF16)
            joined_grad_out[place, 2 * width + low : 2 * width + high] = grad_valued.astype(BF16)
            sums[0, :, low:high] += fold_rows(grad_query)
            sums[1, :, low:high] += fold_rows(grad_valued)

    @pl.when(step == pl.num_programs(0) - 1)
    def _():
        sums_out[...] = jnp.sum(sums[...], axis=1)


def attention_backward(first_low, joined, probs, w_out, pieces, after=(), block=512):
    rows, width = first_low.shape
    steps = rows // block
    count, own_rows, columns = pieces.shape
    part = columns // steps
    return call_kernel(
        attention_backward_body,
        "attention_backward",
        (steps,),
        [first_low, joined, probs, w_out, pieces],
        [
            row_spec(block, width),
            row_spec(block, 3 * width),
            row_spec(block, 2 * width),
            held_spec(width, width),
            pl.BlockSpec((count, own_rows, part), lambda step, *_: (0, 0, step)),
        ],
        [
            shaped((rows, 3 * width), BF16),
            shaped((2, width), F32),
            shaped((own_rows, columns), F32),
        ],
        [
            row_spec(block, 3 * width),
            whole_spec((2, width)),
            pl.BlockSpec((own_rows, part), lambda step, *_: (0, step)),
        ],
        scratch=[pltpu.VMEM((block, width), BF16), pltpu.VMEM((2, 8, width), F32)],
        after=after,
        flops=16 * rows * width * width,
    )


def grad_tokens_body(joined_grad, grad_first, w_qkv, grad_out):
    grad_out[...] = (dot_nt(joined_grad[...], w_qkv[...]) + grad_first[...]).astype(BF16)


def grad_tokens(joined_grad, grad_first, w_qkv, after=(), block=512):
    rows, width = grad_first.shape
    return call_kernel(
        grad_tokens_body,
        "grad_tokens",
        (rows // block,),
        [joined_grad, grad_first, w_qkv],
        [row_spec(block, 3 * width), row_spec(block, width), held_spec(width, 3 * width)],
        shaped((rows, width), BF16),
        row_spec(block, width),
        after=after,
        flops=6 * rows * width * width,
    )


def pack_body(*refs):
    packed_out, column = refs[-1], 0
    for ref in refs[:-1]:
        packed_out[:, column : column + ref.shape[1]] = ref[...].astype(BF16)
        column += ref.shape[1]


def pack_rows(arrays):
    shape = (arrays[0].shape[0], sum(array.shape[1] for array in arrays))
    return call_kernel(
        pack_body,
        "pack_rows",
        (1,),
        arrays,
        [whole_spec(array.shape) for array in arrays],
        shaped(shape, BF16),
        whole_spec(shape),
    )


def split_rows(total, core, keep_out, send_out, columns=slice(None), order=None):
    groups, rows = keep_out.shape[0], keep_out.shape[1]
    for group in range(groups):
        for flip, target in enumerate((keep_out, send_out)):
            half = core[0] if flip == 0 else 1 - core[0]
            start = pl.multiple_of((2 * group + half) * rows, rows)
            if order is None:
                part = total[pl.ds(start, rows), :]
            else:
                size = rows // len(order)
                places = [pl.multiple_of(start + place * size, 8) for place in order]
                part = jnp.concatenate([total[pl.ds(place, size), :] for place in places], axis=0)
            target[group, :, columns] = part.astype(BF16)


def weight_grad_body(order, core, left, right, keep_out, send_out, total):
    total[...] = dot_tn(left[...], right[...])
    split_rows(total, core, keep_out, send_out, order=order)


def weight_grad(core, left, right, groups, order=None, after=(), block=256):
    tokens, height = left.shape
    width = right.shape[1]
    shape = (groups, height // (2 * groups), width)
    out_spec = pl.BlockSpec((*shape[:2], block), lambda step, *_: (0, 0, step))
    return call_kernel(
        functools.partial(weight_grad_body, order),
        "weight_grad",
        (width // block,),
        [left, right],
        [
            whole_spec((tokens, height)),
            pl.BlockSpec((tokens, block), lambda step, *_: (0, step)),
        ],
        [shaped(shape, BF16)] * 2,
        [out_spec, out_spec],
        scalars=[core],
        scratch=[pltpu.VMEM((height, block), F32)],
        after=after,
        flops=2 * tokens * height * width,
    )


def qkv_grad_body(order, core, left, right, extra, keep_out, send_out, keep_last, send_last, total):
    step, block = pl.program_id(0), right.shape[1]
    total[...] = dot_tn(left[...], right[...])

    @pl.when(step < 2)
    def _():
        columns = pl.ds(pl.multiple_of(step * block, block), block)
        split_rows(total, core, keep_out, send_out, columns)

    @pl.when(step == 2)
    def _():
        split_rows(total, core, keep_last, send_last, order=order)

    @pl.when(step == 0)
    def _():
        for group in range(keep_out.shape[0]):
            for flip, target in enumerate((keep_out, send_out)):
                half = core[0] if flip == 0 else 1 - core[0]
                target[group, :, target.shape[2] - LANES :] = extra[group, half].astype(BF16)


def qkv_grad(core, left, right, groups, extra, order):
    tokens, width = left.shape
    lead = (groups, width // (2 * groups))
    shapes = [(*lead, 2 * width + LANES)] * 2 + [(*lead, width)] * 2
    return call_kernel(
        functools.partial(qkv_grad_body, order),
        "qkv_grad",
        (3,),
        [left, right, extra],
        [
            whole_spec((tokens, width)),
            pl.BlockSpec((tokens, width), lambda step, *_: (0, step)),
            whole_spec(extra.shape),
        ],
        [shaped(shape, BF16) for shape in shapes],
        [whole_spec(shape) for shape in shapes],
        scalars=[core],
        scratch=[pltpu.VMEM((width, width), F32)],
        flops=6 * tokens * width * width,
    )


def plane_split_body(count, place, keep_front, other_front, *refs):
    arrays, front_out, outs = refs[: -count - 1], refs[-count - 1], refs[-count:]
    column = 0
    for keep, received in zip(arrays[::2], arrays[1::2]):
        width = keep.shape[-1]
        for step, out in enumerate(outs):
            chunk = place[0] ^ step
            both = keep[chunk].astype(F32) + received[chunk].astype(F32)
            out[:, column : column + width] = both.astype(out.dtype)
        column += width
    front_out[...] = (keep_front[...].astype(F32) + other_front[...].astype(F32)).astype(BF16)


def plane_split(front, pairs, place, count, after=()):
    arrays = [part.reshape(count, -1, part.shape[-1]) for pair in pairs for part in pair]
    shape = (arrays[0].shape[1], sum(array.shape[2] for array in arrays[::2]))
    outs = [shaped(front[0].shape, BF16), shaped(shape, F32)] + [shaped(shape, BF16)] * (count - 1)
    return call_kernel(
        functools.partial(plane_split_body, count),
        "plane_split",
        (1,),
        [*front, *arrays],
        [whole_spec(array.shape) for array in (*front, *arrays)],
        outs,
        [whole_spec(out.shape) for out in outs],
        scalars=[place],
        after=after,
    )


def line_split_body(pieces, count, place, *refs):
    outs, total = refs[-1 - count : -1], refs[-1]
    total[...] = sum(ref[...].astype(F32) for ref in refs[:pieces])
    rows = outs[0].shape[0]
    for step, out in enumerate(outs):
        start = pl.multiple_of((place[0] ^ step) * rows, rows)
        out[...] = total[pl.ds(start, rows), :].astype(out.dtype)


def line_split(pieces, place, count, after=()):
    rows, width = pieces[0].shape
    shape = (rows // count, width)
    outs = [shaped(shape, F32)] + [shaped(shape, BF16)] * (count - 1)
    return call_kernel(
        functools.partial(line_split_body, len(pieces), count),
        "line_split",
        (1,),
        pieces,
        [whole_spec(piece.shape) for piece in pieces],
        outs,
        [whole_spec(shape)] * count,
        scalars=[place],
        scratch=[pltpu.VMEM((rows, width), F32)],
        after=after,
    )


def trade(parts, axis):
    count = len(parts)
    return [parts[0]] + [
        lax.ppermute(parts[step], axis, [(place, place ^ step) for place in range(count)])
        for step in range(1, count)
    ]


def add_pairs(pairs):
    sums = [(keep.astype(F32) + received.astype(F32)).astype(BF16) for keep, received in pairs]
    return sums[0] if len(sums) == 1 else jnp.concatenate(sums, axis=-1)


def fold_body(pieces, total_out):
    total_out[...] = jnp.sum(pieces[...].astype(F32), axis=0)


def fold_pieces(pieces, after=()):
    count, rows, width = pieces.shape
    return call_kernel(
        fold_body,
        "fold_pieces",
        (1,),
        [pieces],
        [whole_spec(pieces.shape)],
        shaped((rows, width), F32),
        whole_spec((rows, width)),
        after=after,
        vmem=SMALL_VMEM,
    )


def squares_body(parts, pieces, *refs):
    total_out, *totals, spread_out = refs[-3 if parts else -2 :]
    others = refs[parts : len(refs) - (3 if parts else 2)]
    total = jnp.sum(pieces[...].astype(F32), axis=0)
    total_out[...] = total
    squares = jnp.sum(total * total)
    if parts:
        total = sum(ref[...].astype(F32) for ref in refs[:parts])
        totals[0][...] = total
        squares = squares + jnp.sum(total * total)
    for other in others:
        squares = squares + jnp.sum(other[...] * other[...])
    spread_out[...] = jnp.zeros(spread_out.shape, F32) + squares


def fold_with_squares(pieces, parts, others, copies, after=()):
    count, rows, width = pieces.shape
    inputs = [pieces, *parts, *others]
    outs = [shaped((rows, width), F32)]
    if parts:
        outs.append(shaped(parts[0].shape, F32))
    outs.append(shaped((copies, LANES), F32))
    return call_kernel(
        functools.partial(squares_body, len(parts)),
        "fold_with_squares",
        (1,),
        inputs,
        [whole_spec(array.shape) for array in inputs],
        outs,
        [whole_spec(array.shape) for array in outs],
        after=after,
        vmem=SMALL_VMEM,
    )


def update_body(places, squares, *refs):
    count = len(places)
    norm_out, results = refs[-1], refs[-1 - 4 * count : -1]
    states = refs[-1 - 7 * count : -1 - 4 * count]
    totals = refs[: -1 - 7 * count]
    grad_norm = jnp.sqrt(jnp.sum(squares[:, :1], axis=0, keepdims=True))
    factor = CLIP_LIMIT / jnp.maximum(grad_norm, CLIP_LIMIT)
    norm_out[...] = jnp.broadcast_to(grad_norm, norm_out.shape)
    for index, parts in enumerate(places):
        weight, first, second = (ref[...] for ref in states[3 * index : 3 * index + 3])
        grad = jnp.concatenate([totals[source][:, low:high] for source, low, high in parts], axis=1)
        fresh = adam_update(weight, first, second, grad * factor, RATE_MATRIX, DECAY)
        for target, value in zip(results[4 * index : 4 * index + 4], fresh):
            target[...] = value


def update_weights(squares, totals, places, states):
    inputs = [squares, *totals, *states]
    outs = []
    for index in range(len(places)):
        shape = states[3 * index].shape
        outs += [shaped(shape, F32)] * 3 + [shaped(shape, BF16)]
    outs.append(shaped((1, LANES), F32))
    return call_kernel(
        functools.partial(update_body, places),
        "update_weights",
        (1,),
        inputs,
        [whole_spec(array.shape) for array in inputs],
        outs,
        [whole_spec(array.shape) for array in outs],
        vmem=SMALL_VMEM,
    )


def gather_axis(value, axis, size):
    pieces = [value] + [
        lax.ppermute(value, axis, [(place, place ^ step) for place in range(size)])
        for step in range(1, size)
    ]
    stacked = jnp.stack(pieces)
    place, bit = lax.axis_index(axis), 1
    while bit < size:
        paired = stacked.reshape(size // (2 * bit), 2, bit, *value.shape)
        stacked = jnp.where((place & bit) != 0, paired[:, ::-1], paired).reshape(stacked.shape)
        bit *= 2
    return stacked


def adam_update(weight, first_moment, second_moment, grad_clip, rate, decay):
    fresh_one = BETA_ONE * first_moment + (1.0 - BETA_ONE) * grad_clip
    fresh_two = BETA_TWO * second_moment + (1.0 - BETA_TWO) * grad_clip * grad_clip
    correct_one = 1.0 - BETA_ONE**STEP
    correct_two = 1.0 - BETA_TWO**STEP
    stepped = fresh_one / correct_one / (jnp.sqrt(fresh_two / correct_two) + ADAM_EPS)
    updated = weight - rate * (stepped + decay * weight)
    return (updated, fresh_one, fresh_two, updated.astype(BF16))


def body(
    high_count,
    zed_count,
    low_count,
    tokens,
    cotangent,
    seg_counts,
    w_qkv,
    w_out,
    w_up,
    w_down,
    small_params,
    first_qkv,
    second_qkv,
    first_out,
    second_out,
    first_up,
    second_up,
    first_down,
    second_down,
    first_small,
    second_small,
):
    inner_count = zed_count * low_count
    device_count = 2 * high_count * inner_count
    own_rows, width = w_out.shape
    hidden = w_up.shape[1]
    own_small = small_params.shape[0]
    core = lax.axis_index("core").astype(jnp.int32).reshape(1)
    swap = [(0, 1), (1, 0)]

    back = pack_rows([w_up, w_down])
    packed = lax.all_gather(back, ALL, axis=0, tiled=True)
    low_qkv = w_qkv.astype(BF16)
    per_row = own_small // own_rows
    small_block = jnp.pad(
        small_params.astype(BF16).reshape(own_rows, per_row), ((0, 0), (0, LANES - per_row))
    )
    front = jnp.concatenate([low_qkv, small_block, w_out.astype(BF16)], axis=1)
    along = gather_axis(front, "zed", zed_count)
    split = 2 * width
    at_small = low_qkv.shape[1] - split
    quarters = []
    for piece, order in ((along[..., :split], (0, 1)), (along[..., split:], (1, 0))):
        for stage in order:
            if stage == 0:
                piece = jnp.moveaxis(gather_axis(piece, "low", low_count), 0, -3)
            else:
                piece = gather_axis(piece, "hi", high_count)
        quarters.append(piece.reshape(high_count, inner_count * own_rows, piece.shape[-1]))
    quarters = [
        half
        for quarter in quarters
        for half in (quarter, lax.ppermute(quarter, "core", swap))
    ]
    mine, theirs = (half[..., at_small : at_small + per_row] for half in quarters[2:])
    small = (
        jnp.where(core[0] == 0, jnp.stack([mine, theirs], 1), jnp.stack([theirs, mine], 1))
        .reshape(1, device_count * own_small)
        .astype(F32)
    )

    (
        joined,
        probs,
        mixed,
        normed_one,
        inverse_one,
        hidden_low,
        whole_qkv,
        whole_out,
    ) = attention_forward(core, seg_counts, tokens, quarters, small)
    result, slope, grad_second, sums_two, *down = mlp_forward(
        core, seg_counts, normed_one, cotangent, packed, small, high_count
    )

    def swap_cores(parts):
        keep, send = parts
        return keep, lax.ppermute(send, "core", swap)

    def peer_sum(both):
        columns = both.shape[-1]
        pieces = lax.all_to_all(both.reshape(-1, columns), PEERS, 0, 0, tiled=True)
        return pieces.reshape(high_count * inner_count, own_rows, columns)

    down = add_pairs([swap_cores(down)])
    grad_first, first_low, sums_one, sums_wide, *up = mlp_backward(
        core,
        grad_second,
        slope,
        normed_one,
        inverse_one,
        hidden_low,
        packed,
        small,
        high_count,
        after=[down],
    )
    down = peer_sum(down)
    by_low = [zed * low_count + low for low in range(low_count) for zed in range(zed_count)]
    order = by_low if own_rows % 8 == 0 else None
    out = weight_grad(core, first_low, mixed, high_count, order, after=[up[0]])
    keep, received = swap_cores(up)
    keep, out_done = lax.optimization_barrier((keep, out[0]))
    up = add_pairs([(keep, received)])
    out = swap_cores(out)
    joined_grad, sums_qv, sum_down = attention_backward(
        first_low, joined, probs, whole_out, down, after=[out_done, up]
    )
    up = peer_sum(up)
    grad_small = jnp.concatenate(
        [
            sums_qv.reshape(-1),
            sums_one[2],
            sums_wide[0],
            sums_two[2],
            sums_one[:2].reshape(-1),
            sums_two[:2].reshape(-1),
        ]
    )
    by_owner = jnp.pad(
        grad_small.reshape(high_count, 2, inner_count * own_rows, per_row),
        ((0, 0),) * 3 + ((0, LANES - per_row),),
    )
    *query, keep, send = qkv_grad(core, tokens, joined_grad, high_count, by_owner, order)
    value = swap_cores((keep, send))
    query = swap_cores(query)
    if order is not None:
        plane = high_count * low_count
        high, low = lax.axis_index("hi"), lax.axis_index("low")
        place = (high * low_count + low).astype(jnp.int32).reshape(1)
        front, *last = plane_split(query, [value, out], place, plane)
        last = trade(last, PLANE)
        grad_inputs = grad_tokens(joined_grad, grad_first, whole_qkv, after=[front, last[0]])
        place = lax.axis_index("zed").astype(jnp.int32).reshape(1)
        last = trade(line_split(last, place, zed_count, after=[grad_inputs]), "zed")
    else:
        front = add_pairs([query, value, out])
        grad_inputs = grad_tokens(joined_grad, grad_first, whole_qkv, after=[front])
        last = []
    sum_up = fold_pieces(up, after=[grad_inputs, *last[:1]])
    sum_front, *sum_last, spread = fold_with_squares(
        peer_sum(front), last, [sum_up, sum_down], device_count
    )
    if order is None:
        sum_last = [sum_front[:, 2 * width + LANES :]]
    squares = lax.all_to_all(spread, ALL, 0, 0, tiled=True)
    *updated, norm_row = update_weights(
        squares,
        [sum_front, sum_last[0], sum_up, sum_down],
        (
            ((0, 0, 2 * width), (1, 0, width)),
            ((1, width, 2 * width),),
            ((2, 0, hidden),),
            ((3, 0, hidden),),
        ),
        [
            *(w_qkv, first_qkv, second_qkv),
            *(w_out, first_out, second_out),
            *(w_up, first_up, second_up),
            *(w_down, first_down, second_down),
        ],
    )
    grad_norm = norm_row[0, 0]
    factor = CLIP_LIMIT / jnp.maximum(grad_norm, CLIP_LIMIT)
    sum_small = sum_front[:, 2 * width : 2 * width + per_row].reshape(own_small)
    updated += adam_update(
        small_params, first_small, second_small, sum_small * factor, RATE_SMALL, 0.0
    )
    return (result, grad_inputs, grad_norm, *updated)


def solution(mesh):
    outer, inner = mesh.devices.shape
    finer = Mesh(mesh.devices.reshape(outer // 2, 2, inner // 2, 2), ALL)
    rows, flat = P(ALL, None), P(ALL)
    return jax.shard_map(
        functools.partial(body, outer // 2, inner // 2, 2),
        mesh=finer,
        in_specs=(rows, rows, flat) + (rows,) * 4 + (flat,) + (rows,) * 8 + (flat,) * 2,
        out_specs=(rows, rows, P()) + (rows,) * 16 + (flat,) * 4,
        check_vma=False,
    )
```

```python
import functools
import math

import jax
import jax.numpy as jnp
from jax import lax
from jax.experimental import pallas as pl
from jax.experimental.pallas import tpu as pltpu
from jax.sharding import Mesh
from jax.sharding import PartitionSpec as P

HEAD_DIM = 64
SEG_LEN = 128
STEP = 10
NEG_FILL = -1e30
SCALE_QK = 0.125
LN_EPS = 1e-05
BETA_ONE = 0.9
BETA_TWO = 0.999
ADAM_EPS = 1e-08
RATE_MATRIX = 0.03
RATE_SMALL = 0.3
DECAY = 0.01
CLIP_LIMIT = 1.0

LANES = 128
VMEM_LIMIT = 60 * 1024 * 1024
SMALL_VMEM = 60 * 1024 * 1024
F32 = jnp.float32
BF16 = jnp.bfloat16
ALL = ("hi", "core", "zed", "low")
PEERS = ("hi", "zed", "low")
PLANE = ("hi", "low")


def dot_nn(left, right):
    return jnp.dot(left, right, preferred_element_type=F32)


def dot_nt(left, right):
    return lax.dot_general(left, right, (((1,), (1,)), ((), ())), preferred_element_type=F32)


def dot_tn(left, right):
    return lax.dot_general(left, right, (((0,), (0,)), ((), ())), preferred_element_type=F32)


def small_places(width, hidden):
    front = 3 * width + hidden
    return {
        "bq": (0, width),
        "bv": (width, 2 * width),
        "bo": (2 * width, 3 * width),
        "b1": (3 * width, front),
        "b2": (front, front + width),
        "g1": (front + width, front + 2 * width),
        "s1": (front + 2 * width, front + 3 * width),
        "g2": (front + 3 * width, front + 4 * width),
        "s2": (front + 4 * width, front + 5 * width),
    }


def normalize(values):
    row_mean = jnp.mean(values, axis=-1, keepdims=True)
    centred = values - row_mean
    variance = jnp.mean(centred * centred, axis=-1, keepdims=True)
    inverse = lax.rsqrt(variance + LN_EPS)
    return centred * inverse, inverse


def norm_back(scaled, normed, inverse):
    return inverse * (
        scaled
        - jnp.mean(scaled, axis=-1, keepdims=True)
        - normed * jnp.mean(scaled * normed, axis=-1, keepdims=True)
    )


def fold_rows(values):
    return jnp.sum(values.reshape(values.shape[0] // 8, 8, values.shape[1]), axis=0)


def head_halves(pair):
    lane = lax.broadcasted_iota(jnp.int32, pair.shape, 1)
    zero = jnp.zeros_like(pair)
    return jnp.concatenate(
        [jnp.where(lane < HEAD_DIM, pair, zero), jnp.where(lane < HEAD_DIM, zero, pair)], axis=0
    )


def stack_heads(wide):
    return jnp.concatenate([wide[:, :SEG_LEN], wide[:, SEG_LEN:]], axis=0)


def row_spec(rows, columns):
    return pl.BlockSpec((rows, columns), lambda step, *_: (step, 0))


def held_spec(rows, columns, place=0):
    return pl.BlockSpec(
        (rows, columns), lambda step, *_: (0, place), pipeline_mode=pl.Buffered(1)
    )


def whole_spec(shape):
    return pl.BlockSpec(shape, lambda *_: (0,) * len(shape))


def call_kernel(
    body, name, grid, inputs, in_specs, outs, out_specs, scalars=(), scratch=(), after=(), aliases=None, flops=0,
    vmem=VMEM_LIMIT,
):
    lead, kept = len(scalars), len(scalars) + len(inputs)

    def wrapped(*refs):
        body(*refs[:kept], *refs[kept + len(after) :])

    listed = outs if isinstance(outs, list) else [outs]
    moved = sum(math.prod(x.shape) * x.dtype.itemsize for x in (*inputs, *listed))
    return pl.pallas_call(
        wrapped,
        grid_spec=pltpu.PrefetchScalarGridSpec(
            num_scalar_prefetch=lead,
            grid=grid,
            in_specs=[*in_specs, *[pl.BlockSpec(memory_space=pl.ANY)] * len(after)],
            out_specs=out_specs,
            scratch_shapes=list(scratch),
        ),
        out_shape=outs,
        input_output_aliases=aliases or {},
        cost_estimate=pl.CostEstimate(
            flops=int(flops), bytes_accessed=moved, transcendentals=0
        ),
        compiler_params=pltpu.CompilerParams(vmem_limit_bytes=vmem),
        name=name,
    )(*scalars, *inputs, *after)


def shaped(shape, kind):
    return jax.ShapeDtypeStruct(shape, kind)


def attention_forward_body(
    core, counts, inputs, mine_a, theirs_a, mine_b, theirs_b, small, joined_out, probs_out, mixed_out, normed_out, inverse_out, hidden_out, w_qkv, w_out, sems
):
    rows, width = inputs.shape
    at = small_places(width, small.shape[1] - 8 * width)

    @pl.when(pl.program_id(0) == 0)
    def _():
        copies = []
        groups, span, cut = mine_a.shape
        rest = 3 * width - cut
        moves = (
            (mine_a, theirs_a, w_qkv, 0, 0, cut),
            (mine_b, theirs_b, w_qkv, 0, cut, rest),
            (mine_b, theirs_b, w_out, rest + LANES, 0, width),
        )
        for mine, theirs, target, source, place, wide in moves:
            for group in range(groups):
                for flip, half in enumerate((mine, theirs)):
                    owner = 2 * group + (core[0] if flip == 0 else 1 - core[0])
                    block = target.at[
                        pl.ds(pl.multiple_of(owner * span, span), span), place : place + wide
                    ]
                    copies.append(
                        pltpu.make_async_copy(
                            half.at[group, :, source : source + wide], block, sems.at[len(copies)]
                        )
                    )
        for copy in copies:
            copy.start()
        for copy in copies:
            copy.wait()

    values = inputs[...]
    for part, bias in ((0, "bq"), (1, None), (2, "bv")):
        columns = slice(part * width, (part + 1) * width)
        product = dot_nn(values, w_qkv[:, columns])
        if bias is not None:
            product = product + small[:, slice(*at[bias])]
        joined_out[:, columns] = product.astype(BF16)
    for segment in range(rows // SEG_LEN):
        place = slice(segment * SEG_LEN, (segment + 1) * SEG_LEN)
        count = counts[pl.program_id(0) * (rows // SEG_LEN) + segment]
        visible = lax.broadcasted_iota(jnp.int32, (SEG_LEN, 2 * SEG_LEN), 0) < count
        for pair in range(width // LANES):
            low, high = pair * LANES, (pair + 1) * LANES
            query = joined_out[place, low:high] * jnp.asarray(SCALE_QK, BF16)
            keyed = joined_out[place, width + low : width + high]
            valued = joined_out[place, 2 * width + low : 2 * width + high]
            scores = jnp.where(visible, dot_nt(keyed, head_halves(query)), NEG_FILL)
            raised = jnp.exp(scores - jnp.max(scores, axis=0, keepdims=True))
            probs = raised * (1.0 / jnp.sum(raised, axis=0, keepdims=True))
            probs_out[place, 2 * low : 2 * high] = probs
            mixed = dot_tn(stack_heads(probs.astype(BF16)), head_halves(valued))
            mixed_out[place, low:high] = mixed.astype(BF16)
    attended = dot_nt(mixed_out[...], w_out[...]) + small[:, slice(*at["bo"])]
    normed, inverse = normalize(values.astype(F32) + attended)
    normed_out[...] = normed
    inverse_out[...] = jnp.broadcast_to(inverse, inverse_out.shape)
    hidden = normed * small[:, slice(*at["g1"])] + small[:, slice(*at["s1"])]
    hidden_out[...] = hidden.astype(BF16)


def attention_forward(core, counts, inputs, quarters, small, block=256):
    rows, width = inputs.shape
    hbm = pl.BlockSpec(memory_space=pl.ANY)
    return call_kernel(
        attention_forward_body,
        "attention_forward",
        (rows // block,),
        [inputs, *quarters, small],
        [row_spec(block, width), hbm, hbm, hbm, hbm, held_spec(1, small.shape[1])],
        [
            shaped((rows, 3 * width), BF16),
            shaped((rows, 2 * width), F32),
            shaped((rows, width), BF16),
            shaped((rows, width), F32),
            shaped((rows, LANES), F32),
            shaped((rows, width), BF16),
            shaped((width, 3 * width), BF16),
            shaped((width, width), BF16),
        ],
        [
            row_spec(block, 3 * width),
            row_spec(block, 2 * width),
            row_spec(block, width),
            row_spec(block, width),
            row_spec(block, LANES),
            row_spec(block, width),
            held_spec(width, 3 * width),
            held_spec(width, width),
        ],
        scalars=[core, counts],
        scratch=[pltpu.SemaphoreType.DMA((6 * quarters[0].shape[0],))],
        flops=12 * rows * width * width,
    )


def tile_spec(rows, columns, tiles):
    return pl.BlockSpec((rows, columns), lambda step, *_: (jnp.minimum(step, tiles - 1), 0))


def late_spec(shape, tiles):
    return pl.BlockSpec(shape, lambda step, *_: (0, 0, jnp.maximum(step - tiles, 0)))


def late_grad(tiles, core, left, right, keep_out, send_out, total):
    step, block = pl.program_id(0), total.shape[1]

    @pl.when(step >= tiles)
    def _():
        columns = pl.ds(pl.multiple_of((step - tiles) * block, block), block)
        total[...] = dot_tn(left[...], right[:, columns])
        split_rows(total, core, keep_out, send_out)


def mlp_forward_body(
    tiles,
    core,
    counts,
    normed_one,
    cotangent,
    w_up,
    w_down,
    small,
    result_out,
    slope_out,
    second_out,
    sums_out,
    keep_out,
    send_out,
    active_all,
    second_all,
    total,
    sums,
):
    step = pl.program_id(0)

    @pl.when(step == 0)
    def _():
        sums[...] = jnp.zeros_like(sums)

    @pl.when(step < tiles)
    def _():
        rows, width = normed_one.shape
        at = small_places(width, small.shape[1] - 8 * width)
        hidden = normed_one[...] * small[:, slice(*at["g1"])] + small[:, slice(*at["s1"])]
        pre_act = dot_nn(hidden.astype(BF16), w_up[...]) + small[:, slice(*at["b1"])]
        spread = 0.5 * (1.0 + lax.erf(pre_act * math.sqrt(0.5)))
        density = jnp.exp(-0.5 * pre_act * pre_act) * (1.0 / math.sqrt(2.0 * math.pi))
        active = (pre_act * spread).astype(BF16)
        place = pl.ds(pl.multiple_of(step * rows, rows), rows)
        active_all[place, :] = active
        slope_out[...] = spread + pre_act * density
        second = hidden + dot_nt(active, w_down[...]) + small[:, slice(*at["b2"])]
        normed, inverse = normalize(second)
        gain = small[:, slice(*at["g2"])]
        index = lax.broadcasted_iota(jnp.int32, (SEG_LEN, 1), 0)
        live = jnp.concatenate(
            [
                (index < counts[step * (rows // SEG_LEN) + segment]).astype(F32)
                for segment in range(rows // SEG_LEN)
            ],
            axis=0,
        )
        result_out[...] = ((normed * gain + small[:, slice(*at["s2"])]) * live).astype(BF16)
        incoming = cotangent[...].astype(F32) * live
        grad_second = norm_back(incoming * gain, normed, inverse)
        second_out[...] = grad_second
        second_all[place, :] = grad_second.astype(BF16)
        sums[0] += fold_rows(incoming * normed)
        sums[1] += fold_rows(incoming)
        sums[2] += fold_rows(grad_second)

    @pl.when(step == tiles)
    def _():
        sums_out[...] = jnp.sum(sums[...], axis=1)

    late_grad(tiles, core, second_all, active_all, keep_out, send_out, total)


def mlp_forward(core, counts, normed_one, cotangent, packed, small, groups, block=256, wide=512):
    rows, width = normed_one.shape
    hidden = packed.shape[1] // 2
    tiles = rows // block
    shape = (groups, width // (2 * groups), hidden)
    grad_spec = late_spec((*shape[:2], wide), tiles)
    return call_kernel(
        functools.partial(mlp_forward_body, tiles),
        "mlp_forward",
        (tiles + hidden // wide,),
        [normed_one, cotangent, packed, packed, small],
        [
            tile_spec(block, width, tiles),
            tile_spec(block, width, tiles),
            held_spec(width, hidden),
            held_spec(width, hidden, 1),
            held_spec(1, small.shape[1]),
        ],
        [
            shaped((rows, width), BF16),
            shaped((rows, hidden), F32),
            shaped((rows, width), F32),
            shaped((3, width), F32),
            shaped(shape, BF16),
            shaped(shape, BF16),
        ],
        [
            tile_spec(block, width, tiles),
            tile_spec(block, hidden, tiles),
            tile_spec(block, width, tiles),
            whole_spec((3, width)),
            grad_spec,
            grad_spec,
        ],
        scalars=[core, counts],
        scratch=[
            pltpu.VMEM((rows, hidden), BF16),
            pltpu.VMEM((rows, width), BF16),
            pltpu.VMEM((width, wide), F32),
            pltpu.VMEM((3, 8, width), F32),
        ],
        flops=6 * rows * width * hidden,
    )


def weight_copies(packed, targets, chunk, sems):
    copies, column = [], 0
    for target in targets:
        for place in range(0, target.shape[1], chunk):
            copies.append(
                pltpu.make_async_copy(
                    packed.at[:, column : column + chunk],
                    target.at[:, place : place + chunk],
                    sems.at[len(copies)],
                )
            )
            column += chunk
    return copies


def mlp_backward_body(
    tiles,
    core,
    grad_second,
    slope,
    normed_one,
    inverse_one,
    hidden_low,
    packed,
    small,
    first_out,
    first_low_out,
    sums_out,
    wide_out,
    keep_out,
    send_out,
    pre_all,
    hidden_all,
    total,
    sums,
    wide_sums,
    w_up,
    w_down,
    sems,
):
    step = pl.program_id(0)
    chunk = normed_one.shape[1]
    copies = weight_copies(packed, (w_up, w_down), chunk, sems)
    half = len(copies) // 2

    def tile(arriving):
        rows, width = normed_one.shape
        hidden = slope.shape[1]
        at = small_places(width, hidden)
        place = pl.ds(pl.multiple_of(step * rows, rows), rows)
        hidden_all[place, :] = hidden_low[...]
        incoming = grad_second[...]
        incoming_low = incoming.astype(BF16)
        grad_hidden = incoming
        for piece in range(hidden // chunk):
            columns = slice(piece * chunk, (piece + 1) * chunk)
            if arriving:
                copies[half + piece].wait()
                copies[piece].wait()
            grad_pre = dot_nn(incoming_low, w_down[:, columns]) * slope[:, columns]
            wide_sums[:, columns] += fold_rows(grad_pre)
            grad_low = grad_pre.astype(BF16)
            pre_all[place, columns] = grad_low
            grad_hidden = grad_hidden + dot_nt(grad_low, w_up[:, columns])
        normed = normed_one[...]
        sums[0] += fold_rows(grad_hidden * normed)
        sums[1] += fold_rows(grad_hidden)
        grad_first = norm_back(
            grad_hidden * small[:, slice(*at["g1"])], normed, inverse_one[:, :1]
        )
        first_out[...] = grad_first
        first_low_out[...] = grad_first.astype(BF16)
        sums[2] += fold_rows(grad_first)

    @pl.when(step == 0)
    def _():
        for piece in range(half):
            copies[half + piece].start()
            copies[piece].start()
        sums[...] = jnp.zeros_like(sums)
        wide_sums[...] = jnp.zeros_like(wide_sums)
        tile(True)

    @pl.when((step > 0) & (step < tiles))
    def _():
        tile(False)

    @pl.when(step == tiles)
    def _():
        sums_out[...] = jnp.sum(sums[...], axis=1)
        wide_out[...] = jnp.sum(wide_sums[...], axis=0, keepdims=True)

    late_grad(tiles, core, hidden_all, pre_all, keep_out, send_out, total)


def mlp_backward(
    core, grad_second, slope, normed_one, inverse_one, hidden_low, packed, small, groups, after=(), block=256, wide=512
):
    rows, width = normed_one.shape
    hidden = slope.shape[1]
    tiles = rows // block
    shape = (groups, width // (2 * groups), hidden)
    grad_spec = late_spec((*shape[:2], wide), tiles)
    return call_kernel(
        functools.partial(mlp_backward_body, tiles),
        "mlp_backward",
        (tiles + hidden // wide,),
        [grad_second, slope, normed_one, inverse_one, hidden_low, packed, small],
        [
            tile_spec(block, width, tiles),
            tile_spec(block, hidden, tiles),
            tile_spec(block, width, tiles),
            tile_spec(block, LANES, tiles),
            tile_spec(block, width, tiles),
            pl.BlockSpec(memory_space=pl.ANY),
            held_spec(1, small.shape[1]),
        ],
        [
            shaped((rows, width), F32),
            shaped((rows, width), BF16),
            shaped((3, width), F32),
            shaped((1, hidden), F32),
            shaped(shape, BF16),
            shaped(shape, BF16),
        ],
        [
            tile_spec(block, width, tiles),
            tile_spec(block, width, tiles),
            whole_spec((3, width)),
            whole_spec((1, hidden)),
            grad_spec,
            grad_spec,
        ],
        scalars=[core],
        scratch=[
            pltpu.VMEM((rows, hidden), BF16),
            pltpu.VMEM((rows, width), BF16),
            pltpu.VMEM((width, wide), F32),
            pltpu.VMEM((3, 8, width), F32),
            pltpu.VMEM((8, hidden), F32),
            pltpu.VMEM((width, hidden), BF16),
            pltpu.VMEM((width, hidden), BF16),
            pltpu.SemaphoreType.DMA((2 * hidden // width,)),
        ],
        after=after,
        flops=6 * rows * width * hidden,
    )


def attention_backward_body(
    first_low, joined, probs, w_out, pieces, joined_grad_out, sums_out, folded_out, grad_mixed, sums
):
    rows, width = first_low.shape
    step = pl.program_id(0)

    @pl.when(step == 0)
    def _():
        sums[...] = jnp.zeros_like(sums)

    folded_out[...] = jnp.sum(pieces[...].astype(F32), axis=0)
    grad_mixed[...] = dot_nn(first_low[...], w_out[...]).astype(BF16)
    for segment in range(rows // SEG_LEN):
        place = slice(segment * SEG_LEN, (segment + 1) * SEG_LEN)
        for pair in range(width // LANES):
            low, high = pair * LANES, (pair + 1) * LANES
            query = joined[place, low:high]
            keyed = joined[place, width + low : width + high]
            valued = joined[place, 2 * width + low : 2 * width + high]
            grad_halves = head_halves(grad_mixed[place, low:high])
            weights = probs[place, 2 * low : 2 * high]
            grad_probs = dot_nt(valued, grad_halves)
            grad_valued = dot_nn(weights.astype(BF16), grad_halves)
            inner = jnp.sum(weights * grad_probs, axis=0, keepdims=True)
            scores_low = (weights * (grad_probs - inner) * SCALE_QK).astype(BF16)
            grad_keyed = dot_nn(scores_low, head_halves(query))
            grad_query = dot_tn(stack_heads(scores_low), head_halves(keyed))
            joined_grad_out[place, low:high] = grad_query.astype(BF16)
            joined_grad_out[place, width + low : width + high] = grad_keyed.astype(BF16)
            joined_grad_out[place, 2 * width + low : 2 * width + high] = grad_valued.astype(BF16)
            sums[0, :, low:high] += fold_rows(grad_query)
            sums[1, :, low:high] += fold_rows(grad_valued)

    @pl.when(step == pl.num_programs(0) - 1)
    def _():
        sums_out[...] = jnp.sum(sums[...], axis=1)


def attention_backward(first_low, joined, probs, w_out, pieces, after=(), block=512):
    rows, width = first_low.shape
    steps = rows // block
    count, own_rows, columns = pieces.shape
    part = columns // steps
    return call_kernel(
        attention_backward_body,
        "attention_backward",
        (steps,),
        [first_low, joined, probs, w_out, pieces],
        [
            row_spec(block, width),
            row_spec(block, 3 * width),
            row_spec(block, 2 * width),
            held_spec(width, width),
            pl.BlockSpec((count, own_rows, part), lambda step, *_: (0, 0, step)),
        ],
        [
            shaped((rows, 3 * width), BF16),
            shaped((2, width), F32),
            shaped((own_rows, columns), F32),
        ],
        [
            row_spec(block, 3 * width),
            whole_spec((2, width)),
            pl.BlockSpec((own_rows, part), lambda step, *_: (0, step)),
        ],
        scratch=[pltpu.VMEM((block, width), BF16), pltpu.VMEM((2, 8, width), F32)],
        after=after,
        flops=16 * rows * width * width,
    )


def grad_tokens_body(joined_grad, grad_first, w_qkv, grad_out):
    grad_out[...] = (dot_nt(joined_grad[...], w_qkv[...]) + grad_first[...]).astype(BF16)


def grad_tokens(joined_grad, grad_first, w_qkv, after=(), block=512):
    rows, width = grad_first.shape
    return call_kernel(
        grad_tokens_body,
        "grad_tokens",
        (rows // block,),
        [joined_grad, grad_first, w_qkv],
        [row_spec(block, 3 * width), row_spec(block, width), held_spec(width, 3 * width)],
        shaped((rows, width), BF16),
        row_spec(block, width),
        after=after,
        flops=6 * rows * width * width,
    )


def pack_body(*refs):
    packed_out, column = refs[-1], 0
    for ref in refs[:-1]:
        packed_out[:, column : column + ref.shape[1]] = ref[...].astype(BF16)
        column += ref.shape[1]


def pack_rows(arrays):
    shape = (arrays[0].shape[0], sum(array.shape[1] for array in arrays))
    return call_kernel(
        pack_body,
        "pack_rows",
        (1,),
        arrays,
        [whole_spec(array.shape) for array in arrays],
        shaped(shape, BF16),
        whole_spec(shape),
    )


def split_rows(total, core, keep_out, send_out, columns=slice(None), order=None):
    groups, rows = keep_out.shape[0], keep_out.shape[1]
    for group in range(groups):
        for flip, target in enumerate((keep_out, send_out)):
            half = core[0] if flip == 0 else 1 - core[0]
            start = pl.multiple_of((2 * group + half) * rows, rows)
            if order is None:
                part = total[pl.ds(start, rows), :]
            else:
                size = rows // len(order)
                places = [pl.multiple_of(start + place * size, 8) for place in order]
                part = jnp.concatenate([total[pl.ds(place, size), :] for place in places], axis=0)
            target[group, :, columns] = part.astype(BF16)


def weight_grad_body(order, core, left, right, keep_out, send_out, total):
    total[...] = dot_tn(left[...], right[...])
    split_rows(total, core, keep_out, send_out, order=order)


def weight_grad(core, left, right, groups, order=None, after=(), block=256):
    tokens, height = left.shape
    width = right.shape[1]
    shape = (groups, height // (2 * groups), width)
    out_spec = pl.BlockSpec((*shape[:2], block), lambda step, *_: (0, 0, step))
    return call_kernel(
        functools.partial(weight_grad_body, order),
        "weight_grad",
        (width // block,),
        [left, right],
        [
            whole_spec((tokens, height)),
            pl.BlockSpec((tokens, block), lambda step, *_: (0, step)),
        ],
        [shaped(shape, BF16)] * 2,
        [out_spec, out_spec],
        scalars=[core],
        scratch=[pltpu.VMEM((height, block), F32)],
        after=after,
        flops=2 * tokens * height * width,
    )


def qkv_grad_body(order, core, left, right, extra, keep_out, send_out, keep_last, send_last, total):
    step, block = pl.program_id(0), right.shape[1]
    total[...] = dot_tn(left[...], right[...])

    @pl.when(step < 2)
    def _():
        columns = pl.ds(pl.multiple_of(step * block, block), block)
        split_rows(total, core, keep_out, send_out, columns)

    @pl.when(step == 2)
    def _():
        split_rows(total, core, keep_last, send_last, order=order)

    @pl.when(step == 0)
    def _():
        for group in range(keep_out.shape[0]):
            for flip, target in enumerate((keep_out, send_out)):
                half = core[0] if flip == 0 else 1 - core[0]
                target[group, :, target.shape[2] - LANES :] = extra[group, half].astype(BF16)


def qkv_grad(core, left, right, groups, extra, order):
    tokens, width = left.shape
    lead = (groups, width // (2 * groups))
    shapes = [(*lead, 2 * width + LANES)] * 2 + [(*lead, width)] * 2
    return call_kernel(
        functools.partial(qkv_grad_body, order),
        "qkv_grad",
        (3,),
        [left, right, extra],
        [
            whole_spec((tokens, width)),
            pl.BlockSpec((tokens, width), lambda step, *_: (0, step)),
            whole_spec(extra.shape),
        ],
        [shaped(shape, BF16) for shape in shapes],
        [whole_spec(shape) for shape in shapes],
        scalars=[core],
        scratch=[pltpu.VMEM((width, width), F32)],
        flops=6 * tokens * width * width,
    )


def plane_split_body(count, place, keep_front, other_front, *refs):
    arrays, front_out, outs = refs[: -count - 1], refs[-count - 1], refs[-count:]
    column = 0
    for keep, received in zip(arrays[::2], arrays[1::2]):
        width = keep.shape[-1]
        for step, out in enumerate(outs):
            chunk = place[0] ^ step
            both = keep[chunk].astype(F32) + received[chunk].astype(F32)
            out[:, column : column + width] = both.astype(out.dtype)
        column += width
    front_out[...] = (keep_front[...].astype(F32) + other_front[...].astype(F32)).astype(BF16)


def plane_split(front, pairs, place, count, after=()):
    arrays = [part.reshape(count, -1, part.shape[-1]) for pair in pairs for part in pair]
    shape = (arrays[0].shape[1], sum(array.shape[2] for array in arrays[::2]))
    outs = [shaped(front[0].shape, BF16), shaped(shape, F32)] + [shaped(shape, BF16)] * (count - 1)
    return call_kernel(
        functools.partial(plane_split_body, count),
        "plane_split",
        (1,),
        [*front, *arrays],
        [whole_spec(array.shape) for array in (*front, *arrays)],
        outs,
        [whole_spec(out.shape) for out in outs],
        scalars=[place],
        after=after,
    )


def line_split_body(pieces, count, place, *refs):
    outs, total = refs[-1 - count : -1], refs[-1]
    total[...] = sum(ref[...].astype(F32) for ref in refs[:pieces])
    rows = outs[0].shape[0]
    for step, out in enumerate(outs):
        start = pl.multiple_of((place[0] ^ step) * rows, rows)
        out[...] = total[pl.ds(start, rows), :].astype(out.dtype)


def line_split(pieces, place, count, after=()):
    rows, width = pieces[0].shape
    shape = (rows // count, width)
    outs = [shaped(shape, F32)] + [shaped(shape, BF16)] * (count - 1)
    return call_kernel(
        functools.partial(line_split_body, len(pieces), count),
        "line_split",
        (1,),
        pieces,
        [whole_spec(piece.shape) for piece in pieces],
        outs,
        [whole_spec(shape)] * count,
        scalars=[place],
        scratch=[pltpu.VMEM((rows, width), F32)],
        after=after,
    )


def trade(parts, axis):
    count = len(parts)
    return [parts[0]] + [
        lax.ppermute(parts[step], axis, [(place, place ^ step) for place in range(count)])
        for step in range(1, count)
    ]


def add_pairs(pairs):
    sums = [(keep.astype(F32) + received.astype(F32)).astype(BF16) for keep, received in pairs]
    return sums[0] if len(sums) == 1 else jnp.concatenate(sums, axis=-1)


def fold_body(pieces, total_out):
    total_out[...] = jnp.sum(pieces[...].astype(F32), axis=0)


def fold_pieces(pieces, after=()):
    count, rows, width = pieces.shape
    return call_kernel(
        fold_body,
        "fold_pieces",
        (1,),
        [pieces],
        [whole_spec(pieces.shape)],
        shaped((rows, width), F32),
        whole_spec((rows, width)),
        after=after,
        vmem=SMALL_VMEM,
    )


def squares_body(parts, pieces, *refs):
    total_out, *totals, spread_out = refs[-3 if parts else -2 :]
    others = refs[parts : len(refs) - (3 if parts else 2)]
    total = jnp.sum(pieces[...].astype(F32), axis=0)
    total_out[...] = total
    squares = jnp.sum(total * total)
    if parts:
        total = sum(ref[...].astype(F32) for ref in refs[:parts])
        totals[0][...] = total
        squares = squares + jnp.sum(total * total)
    for other in others:
        squares = squares + jnp.sum(other[...] * other[...])
    spread_out[...] = jnp.zeros(spread_out.shape, F32) + squares


def fold_with_squares(pieces, parts, others, copies, after=()):
    count, rows, width = pieces.shape
    inputs = [pieces, *parts, *others]
    outs = [shaped((rows, width), F32)]
    if parts:
        outs.append(shaped(parts[0].shape, F32))
    outs.append(shaped((copies, LANES), F32))
    return call_kernel(
        functools.partial(squares_body, len(parts)),
        "fold_with_squares",
        (1,),
        inputs,
        [whole_spec(array.shape) for array in inputs],
        outs,
        [whole_spec(array.shape) for array in outs],
        after=after,
        vmem=SMALL_VMEM,
    )


def update_body(places, squares, *refs):
    count = len(places)
    norm_out, results = refs[-1], refs[-1 - 4 * count : -1]
    states = refs[-1 - 7 * count : -1 - 4 * count]
    totals = refs[: -1 - 7 * count]
    grad_norm = jnp.sqrt(jnp.sum(squares[:, :1], axis=0, keepdims=True))
    factor = CLIP_LIMIT / jnp.maximum(grad_norm, CLIP_LIMIT)
    norm_out[...] = jnp.broadcast_to(grad_norm, norm_out.shape)
    for index, parts in enumerate(places):
        weight, first, second = (ref[...] for ref in states[3 * index : 3 * index + 3])
        grad = jnp.concatenate([totals[source][:, low:high] for source, low, high in parts], axis=1)
        fresh = adam_update(weight, first, second, grad * factor, RATE_MATRIX, DECAY)
        for target, value in zip(results[4 * index : 4 * index + 4], fresh):
            target[...] = value


def update_weights(squares, totals, places, states):
    inputs = [squares, *totals, *states]
    outs = []
    for index in range(len(places)):
        shape = states[3 * index].shape
        outs += [shaped(shape, F32)] * 3 + [shaped(shape, BF16)]
    outs.append(shaped((1, LANES), F32))
    return call_kernel(
        functools.partial(update_body, places),
        "update_weights",
        (1,),
        inputs,
        [whole_spec(array.shape) for array in inputs],
        outs,
        [whole_spec(array.shape) for array in outs],
        vmem=SMALL_VMEM,
    )


def gather_axis(value, axis, size):
    pieces = [value] + [
        lax.ppermute(value, axis, [(place, place ^ step) for place in range(size)])
        for step in range(1, size)
    ]
    stacked = jnp.stack(pieces)
    place, bit = lax.axis_index(axis), 1
    while bit < size:
        paired = stacked.reshape(size // (2 * bit), 2, bit, *value.shape)
        stacked = jnp.where((place & bit) != 0, paired[:, ::-1], paired).reshape(stacked.shape)
        bit *= 2
    return stacked


def adam_update(weight, first_moment, second_moment, grad_clip, rate, decay):
    fresh_one = BETA_ONE * first_moment + (1.0 - BETA_ONE) * grad_clip
    fresh_two = BETA_TWO * second_moment + (1.0 - BETA_TWO) * grad_clip * grad_clip
    correct_one = 1.0 - BETA_ONE**STEP
    correct_two = 1.0 - BETA_TWO**STEP
    stepped = fresh_one / correct_one / (jnp.sqrt(fresh_two / correct_two) + ADAM_EPS)
    updated = weight - rate * (stepped + decay * weight)
    return (updated, fresh_one, fresh_two, updated.astype(BF16))


def body(
    high_count,
    zed_count,
    low_count,
    tokens,
    cotangent,
    seg_counts,
    w_qkv,
    w_out,
    w_up,
    w_down,
    small_params,
    first_qkv,
    second_qkv,
    first_out,
    second_out,
    first_up,
    second_up,
    first_down,
    second_down,
    first_small,
    second_small,
):
    inner_count = zed_count * low_count
    device_count = 2 * high_count * inner_count
    own_rows, width = w_out.shape
    hidden = w_up.shape[1]
    own_small = small_params.shape[0]
    core = lax.axis_index("core").astype(jnp.int32).reshape(1)
    swap = [(0, 1), (1, 0)]

    back = pack_rows([w_up, w_down])
    packed = lax.all_gather(back, ALL, axis=0, tiled=True)
    low_qkv = w_qkv.astype(BF16)
    per_row = own_small // own_rows
    small_block = jnp.pad(
        small_params.astype(BF16).reshape(own_rows, per_row), ((0, 0), (0, LANES - per_row))
    )
    front = jnp.concatenate([low_qkv, small_block, w_out.astype(BF16)], axis=1)
    along = gather_axis(front, "zed", zed_count)
    split = 2 * width
    at_small = low_qkv.shape[1] - split
    quarters = []
    for piece, order in ((along[..., :split], (0, 1)), (along[..., split:], (1, 0))):
        for stage in order:
            if stage == 0:
                piece = jnp.moveaxis(gather_axis(piece, "low", low_count), 0, -3)
            else:
                piece = gather_axis(piece, "hi", high_count)
        quarters.append(piece.reshape(high_count, inner_count * own_rows, piece.shape[-1]))
    quarters = [
        half
        for quarter in quarters
        for half in (quarter, lax.ppermute(quarter, "core", swap))
    ]
    mine, theirs = (half[..., at_small : at_small + per_row] for half in quarters[2:])
    small = (
        jnp.where(core[0] == 0, jnp.stack([mine, theirs], 1), jnp.stack([theirs, mine], 1))
        .reshape(1, device_count * own_small)
        .astype(F32)
    )

    (
        joined,
        probs,
        mixed,
        normed_one,
        inverse_one,
        hidden_low,
        whole_qkv,
        whole_out,
    ) = attention_forward(core, seg_counts, tokens, quarters, small)
    result, slope, grad_second, sums_two, *down = mlp_forward(
        core, seg_counts, normed_one, cotangent, packed, small, high_count
    )

    def swap_cores(parts):
        keep, send = parts
        return keep, lax.ppermute(send, "core", swap)

    def peer_sum(both):
        columns = both.shape[-1]
        pieces = lax.all_to_all(both.reshape(-1, columns), PEERS, 0, 0, tiled=True)
        return pieces.reshape(high_count * inner_count, own_rows, columns)

    down = add_pairs([swap_cores(down)])
    grad_first, first_low, sums_one, sums_wide, *up = mlp_backward(
        core,
        grad_second,
        slope,
        normed_one,
        inverse_one,
        hidden_low,
        packed,
        small,
        high_count,
        after=[down],
    )
    down = peer_sum(down)
    by_low = [zed * low_count + low for low in range(low_count) for zed in range(zed_count)]
    order = by_low if own_rows % 8 == 0 else None
    out = weight_grad(core, first_low, mixed, high_count, order, after=[up[0]])
    keep, received = swap_cores(up)
    keep, out_done = lax.optimization_barrier((keep, out[0]))
    up = add_pairs([(keep, received)])
    out = swap_cores(out)
    joined_grad, sums_qv, sum_down = attention_backward(
        first_low, joined, probs, whole_out, down, after=[out_done, out[1], up]
    )
    up = peer_sum(up)
    grad_small = jnp.concatenate(
        [
            sums_qv.reshape(-1),
            sums_one[2],
            sums_wide[0],
            sums_two[2],
            sums_one[:2].reshape(-1),
            sums_two[:2].reshape(-1),
        ]
    )
    by_owner = jnp.pad(
        grad_small.reshape(high_count, 2, inner_count * own_rows, per_row),
        ((0, 0),) * 3 + ((0, LANES - per_row),),
    )
    *query, keep, send = qkv_grad(core, tokens, joined_grad, high_count, by_owner, order)
    value = swap_cores((keep, send))
    query = swap_cores(query)
    if order is not None:
        plane = high_count * low_count
        high, low = lax.axis_index("hi"), lax.axis_index("low")
        place = (high * low_count + low).astype(jnp.int32).reshape(1)
        front, *last = plane_split(query, [value, out], place, plane)
        last = trade(last, PLANE)
        grad_inputs = grad_tokens(joined_grad, grad_first, whole_qkv, after=[front, last[0]])
        place = lax.axis_index("zed").astype(jnp.int32).reshape(1)
        last = trade(line_split(last, place, zed_count, after=[grad_inputs]), "zed")
    else:
        front = add_pairs([query, value, out])
        grad_inputs = grad_tokens(joined_grad, grad_first, whole_qkv, after=[front])
        last = []
    sum_up = fold_pieces(up, after=[grad_inputs, *last[:1]])
    sum_front, *sum_last, spread = fold_with_squares(
        peer_sum(front), last, [sum_up, sum_down], device_count
    )
    if order is None:
        sum_last = [sum_front[:, 2 * width + LANES :]]
    squares = lax.all_to_all(spread, ALL, 0, 0, tiled=True)
    *updated, norm_row = update_weights(
        squares,
        [sum_front, sum_last[0], sum_up, sum_down],
        (
            ((0, 0, 2 * width), (1, 0, width)),
            ((1, width, 2 * width),),
            ((2, 0, hidden),),
            ((3, 0, hidden),),
        ),
        [
            *(w_qkv, first_qkv, second_qkv),
            *(w_out, first_out, second_out),
            *(w_up, first_up, second_up),
            *(w_down, first_down, second_down),
        ],
    )
    grad_norm = norm_row[0, 0]
    factor = CLIP_LIMIT / jnp.maximum(grad_norm, CLIP_LIMIT)
    sum_small = sum_front[:, 2 * width : 2 * width + per_row].reshape(own_small)
    updated += adam_update(
        small_params, first_small, second_small, sum_small * factor, RATE_SMALL, 0.0
    )
    return (result, grad_inputs, grad_norm, *updated)


def solution(mesh):
    outer, inner = mesh.devices.shape
    finer = Mesh(mesh.devices.reshape(outer // 2, 2, inner // 2, 2), ALL)
    rows, flat = P(ALL, None), P(ALL)
    return jax.shard_map(
        functools.partial(body, outer // 2, inner // 2, 2),
        mesh=finer,
        in_specs=(rows, rows, flat) + (rows,) * 4 + (flat,) + (rows,) * 8 + (flat,) * 2,
        out_specs=(rows, rows, P()) + (rows,) * 16 + (flat,) * 4,
        check_vma=False,
    )
```
